512 devices in a mesh: shard: 128 (over z, x, core), rep: 4 (over y).
Axes of the slice: x: 4, y: 4, z: 16, core: 2. Of those that a mesh axis runs over, the one named last changes fastest.
Arguments:
- embeddings: bfloat16 [32768, 4096], P('shard')
- cluster_of: int32 [32768], P('shard'), may hold values from 0 to 127, as said below
Outputs:
- max_similarity: float32 [32768], P('shard')
The draws below stay inside these ranges and needn't reach their ends.
Inputs may be any that keep to these rules, and one draw needn't show every extreme that they name: `cluster_of`: cluster c is owned by index c // 1 of shard. Of the 256 documents of one index of shard at most 4 lie in clusters of one owner, and one owner takes exactly 4 from every index of shard.
All inputs are finite; a program needn't handle non-finite values.
Results may differ from the reference program's by a relative error of at most 0.0003.
Values may be sent and summed in bfloat16 or wider, within the bound.
No kernel may reach another device: no remote copies, remote signals or barrier semaphores. Data moves between devices by JAX's collectives and lax.ppermute only.
A program may use at most 64 MiB of HBM per device.

```python
import math
import jax
import jax.numpy as jnp
from jax import lax

D = 4096
DOC_DEV = 256
CL_OWN = 1
CAP = 4
SLOTS = 512
DOCS = 32768
N_SHARD = 128


def route_docs(key):
    slot_count = N_SHARD * CAP
    key_busy, key_weight, key_noise, key_shuffle, key_first, key_second, key_offset = jax.random.split(key, 7)
    busy_owner = jax.random.randint(key_busy, (), 0, N_SHARD)
    owner_weight = jax.random.randint(key_weight, (N_SHARD,), 0, 2 ** 20)
    owner_weight = jnp.where(jnp.arange(N_SHARD) == busy_owner, 2 ** 22, owner_weight)
    slot_owner = jnp.arange(slot_count) // CAP
    scores = jax.random.randint(key_noise, (N_SHARD, slot_count), 0, 2 ** 20) + owner_weight[slot_owner][None, :]
    ranking = jnp.argsort(-scores, axis=1, stable=True)
    chosen = ranking[:, :DOC_DEV]
    chosen = jax.random.permutation(key_shuffle, chosen, axis=1, independent=True)
    owner_doc = chosen // CAP
    first_pick = jax.random.randint(key_first, (N_SHARD, DOC_DEV), 0, CL_OWN)
    second_pick = jax.random.randint(key_second, (N_SHARD, DOC_DEV), 0, CL_OWN)
    offsets = jax.random.randint(key_offset, (N_SHARD,), 0, CL_OWN)
    local_index = (jnp.minimum(first_pick, second_pick) + offsets[owner_doc]) % CL_OWN
    return (owner_doc * CL_OWN + local_index).reshape(-1).astype(jnp.int32)


def draw_cluster_of(key, part):
    return route_docs(key)


def draw_embeddings(key, part):
    clusters = route_docs(key)
    key = jax.random.fold_in(key, 7)
    key_center, key_noise, key_mix, key_scale = jax.random.split(key, 4)
    centers = jax.vmap(lambda cluster_id: jax.random.normal(jax.random.fold_in(key_center, cluster_id), (D,), jnp.float32))(clusters)
    noise_part = jax.random.normal(key_noise, (DOCS, D), jnp.float32)
    row_scale = jnp.exp(jax.random.uniform(key_scale, (DOCS, 1), jnp.float32, 0.0, math.log(10.0)))
    mixing = jnp.exp(jax.random.uniform(key_mix, (DOCS, 1), jnp.float32, math.log(0.3), math.log(3.0)))
    values = row_scale * (mixing * centers + noise_part) / jnp.sqrt(1.0 + mixing * mixing)
    return values.astype(jnp.bfloat16)


def setup_inputs(seed: int = 0) -> dict:
    key_list = jax.random.split(jax.random.key(seed), 3)
    embeddings = draw_embeddings(jax.random.fold_in(key_list[2], 71), 0)
    cluster_of = draw_cluster_of(jax.random.fold_in(key_list[2], 71), 0)
    return {"embeddings": embeddings, "cluster_of": cluster_of}


epsilon = 1e-06

def reference(embeddings, cluster_of):
    owner_of_doc = cluster_of // CL_OWN
    doc_total = owner_of_doc.shape[0]
    sorted_docs = jnp.argsort(owner_of_doc, stable=True).astype(jnp.int32)
    owner_ids = jnp.arange(N_SHARD, dtype=jnp.int32)
    counts = lax.optimization_barrier(jnp.sum((owner_of_doc[None, :] == owner_ids[:, None]).astype(jnp.int32), axis=1))
    starts = (jnp.cumsum(counts) - counts).astype(jnp.int32)
    positions = jnp.arange(doc_total, dtype=jnp.int32)
    rank_in_owner = jnp.zeros((doc_total,), jnp.int32).at[sorted_docs].set(positions - starts[owner_of_doc[sorted_docs]])
    padded = jnp.concatenate([sorted_docs, jnp.zeros((SLOTS,), jnp.int32)])
    slot_ids = jnp.arange(SLOTS, dtype=jnp.int32)

    def per_owner(owner_index):
        window = lax.dynamic_slice(padded, (starts[owner_index],), (SLOTS,))
        is_live = slot_ids < counts[owner_index]
        row_data = embeddings[window]
        labels = cluster_of[window]
        inverse = lax.rsqrt(lax.optimization_barrier(jnp.sum(jnp.square(row_data.astype(jnp.float32)), axis=1)) + epsilon)
        products = jnp.dot(row_data, row_data.T, preferred_element_type=jnp.float32)
        cosine = products * inverse[:, None] * inverse[None, :]
        mate_mask = (labels[:, None] == labels[None, :]) & is_live[:, None] & is_live[None, :] & (slot_ids[:, None] != slot_ids[None, :])
        return lax.optimization_barrier(jnp.max(jnp.where(mate_mask, cosine, jnp.float32(-1.0)), axis=1))
    maxima = lax.map(per_owner, owner_ids)
    return maxima[owner_of_doc, rank_in_owner]
```

```python
import jax
import jax.numpy as jnp
import numpy as np
from jax import lax
from jax.experimental import pallas as pl
from jax.experimental.pallas import tpu as pltpu
from jax.sharding import Mesh
from jax.sharding import PartitionSpec as P

SHARDS = 128
PLANES = 16
LANES = 8
REPS = 4
RANKS = 4
DOCS = 256
WIDTH = 1024
HALF = WIDTH // 2
ROWS = SHARDS * RANKS * 2
SLOTS = SHARDS * RANKS
PAIR_ROWS = 168

epsilon = 1e-06
f32 = jnp.float32
bf16 = jnp.bfloat16


def iota(shape, dim):
    return lax.broadcasted_iota(jnp.int32, shape, dim)


def as_column(row, neutral):
    n = row.shape[1]
    eye = iota((n, n), 0) == iota((n, n), 1)
    return jnp.max(jnp.where(eye, jnp.broadcast_to(row, (n, n)), neutral), axis=1, keepdims=True)


def as_row(column, neutral):
    n = column.shape[0]
    eye = iota((n, n), 0) == iota((n, n), 1)
    return jnp.max(jnp.where(eye, jnp.broadcast_to(column, (n, n)), neutral), axis=0, keepdims=True)


def dispatch_kernel(rep_ref, cluster_ref, docs_ref, out_ref, slot_ref):
    cluster = cluster_ref[...].astype(f32)
    column = as_column(cluster, f32(-1.0))
    earlier = (column == cluster) & (iota((DOCS, DOCS), 0) < iota((DOCS, DOCS), 1))
    rank = jnp.sum(jnp.where(earlier, f32(1.0), f32(0.0)), axis=0, keepdims=True)
    slot = cluster_ref[...] * RANKS + rank.astype(jnp.int32)
    slot_ref[...] = slot
    step = 256
    docs = [docs_ref[:, h * HALF : (h + 1) * HALF] for h in range(2)]
    ones = jnp.ones((DOCS, 128), bf16)
    for start in range(0, ROWS, step):
        row = iota((step, DOCS), 0) + start
        chosen = jnp.where((row >> 1) == slot, f32(1.0), f32(0.0)).astype(bf16)
        values = [jnp.dot(chosen, d, preferred_element_type=f32) for d in docs]
        live = jnp.dot(chosen, ones, preferred_element_type=f32) > 0.5
        odd = (iota((step, 128), 0) & 1) == 1
        for part in range(HALF // 128):
            lanes = slice(part * 128, (part + 1) * 128)
            merged = jnp.where(odd, values[1][:, lanes], values[0][:, lanes])
            out_ref[start : start + step, lanes] = jnp.where(live, merged, jnp.nan).astype(bf16)


def gram_kernel(pick_ref, rows_ref, out_ref, gram_ref):
    rows = rows_ref[...].astype(f32)
    empty = rows != rows
    clean = jnp.where(empty, f32(0.0), rows).astype(bf16)
    flags = jnp.where(empty[:, :128], f32(1.0), f32(0.0)).astype(bf16)
    slots = jnp.concatenate(
        [
            jnp.dot(pick_ref[h], clean, preferred_element_type=f32).astype(bf16)
            for h in range(2)
        ],
        axis=1,
    )
    vacant = jnp.dot(pick_ref[0], flags, preferred_element_type=f32)
    gram_ref[...] = lax.dot_general(
        slots, slots, (((1,), (1,)), ((), ())), preferred_element_type=f32
    )

    def block(a, b):
        return gram_ref[a * 128 : (a + 1) * 128, b * 128 : (b + 1) * 128]

    eye = iota((128, 128), 0) == iota((128, 128), 1)
    squares = []
    for k in range(RANKS):
        diagonal = jnp.where(vacant[k * 128 : (k + 1) * 128] > 0.5, jnp.nan, block(k, k))
        squares.append(jnp.sum(jnp.where(eye, diagonal, f32(0.0)), axis=0, keepdims=True))
    for r in range(REPS):
        following = (r + 1) % RANKS
        a, b, half = r % 2, r % 2 + 2, r // 2
        out_ref[r, 0:128, 0:128] = block(r, r)
        out_ref[r, 0:128, 128:256] = block(r, following)
        top = a * 128 + half * 64
        out_ref[r, 128:160, 0:128] = gram_ref[top : top + 32, b * 128 : (b + 1) * 128]
        out_ref[r, 128:160, 128:256] = gram_ref[top + 32 : top + 64, b * 128 : (b + 1) * 128]
        norms = [
            jnp.concatenate([squares[r], squares[following]], axis=1),
            jnp.concatenate([squares[a], squares[b]], axis=1),
            jnp.zeros((6, 256), f32),
        ]
        out_ref[r, 160:168, :] = jnp.concatenate(norms, axis=0)


def best_kernel(rep_ref, parts_ref, out_ref):
    rep = rep_ref[0]
    total = parts_ref[0] + parts_ref[1] + parts_ref[2] + parts_ref[3]
    eye = iota((128, 128), 0) == iota((128, 128), 1)

    def scales(squares):
        live = squares == squares
        return jnp.where(live, lax.rsqrt(squares + epsilon), f32(-1.0))

    def scored(products, column, row):
        cosine = products * column * row
        return jnp.where((column >= 0.0) & (row >= 0.0), cosine, f32(-1.0))

    main = scales(total[160:161, :])
    other = scales(total[161:162, :])
    own, nxt = main[:, 0:128], main[:, 128:256]
    own_column = as_column(own, f32(-2.0))
    same = jnp.where(eye, f32(-1.0), scored(total[0:128, 0:128], own_column, own))
    near = scored(total[0:128, 128:256], own_column, nxt)
    best_own = as_row(
        jnp.maximum(jnp.max(same, axis=1, keepdims=True), jnp.max(near, axis=1, keepdims=True)),
        f32(-1.0),
    )
    best_next = jnp.max(near, axis=0, keepdims=True)
    a_column = as_column(other[:, 0:128], f32(-2.0))
    upper = rep >= 2
    a_column = jnp.where(upper, a_column[64:128], a_column[0:64])
    extra = jnp.concatenate([total[128:160, 0:128], total[128:160, 128:256]], axis=0)
    far = scored(extra, a_column, other[:, 128:256])
    best_b = jnp.max(far, axis=0, keepdims=True)
    rows = jnp.max(far, axis=1, keepdims=True)
    rows = jnp.concatenate([rows, rows], axis=0)
    in_half = (iota((1, 128), 1) >= 64) == upper
    best_a = jnp.where(in_half, as_row(rows, f32(-1.0)), f32(-1.0))
    rank = iota((RANKS, 128), 0)
    low = jnp.full((RANKS, 128), -1.0, f32)
    best = jnp.where(rank == rep, best_own, low)
    best = jnp.maximum(best, jnp.where(rank == (rep + 1) % RANKS, best_next, low))
    best = jnp.maximum(best, jnp.where(rank == rep % 2, best_a, low))
    best = jnp.maximum(best, jnp.where(rank == rep % 2 + 2, best_b, low))
    for target in range(LANES * REPS):
        out_ref[target] = best


def turn_kernel(lane_ref, best_ref, out_ref, turned_ref):
    joined = []
    for lane in range(LANES):
        base = lane * REPS
        joined.append(
            jnp.maximum(
                jnp.maximum(best_ref[base], best_ref[base + 1]),
                jnp.maximum(best_ref[base + 2], best_ref[base + 3]),
            )
        )
    joined.append(jnp.zeros((128 - LANES * RANKS, 128), f32))
    turned_ref[...] = jnp.transpose(jnp.concatenate(joined, axis=0))
    start = pl.multiple_of(lane_ref[0] * PLANES, PLANES)
    out_ref[...] = turned_ref[pl.ds(start, PLANES), :].reshape(PLANES, 1, 128)


def collect_kernel(slot_ref, best_ref, out_ref):
    slot = slot_ref[...]
    best = best_ref[...].reshape(PLANES, 128)
    chosen = jnp.where(iota((128, DOCS), 0) == slot % (LANES * RANKS), f32(1.0), f32(0.0))
    values = jnp.dot(best, chosen, precision=lax.Precision.HIGHEST, preferred_element_type=f32)
    plane = iota((PLANES, DOCS), 0) == slot // (LANES * RANKS)
    out_ref[...] = jnp.sum(jnp.where(plane, values, f32(0.0)), axis=0, keepdims=True)


VMEM = pl.BlockSpec(memory_space=pltpu.VMEM)
SMEM = pl.BlockSpec(memory_space=pltpu.SMEM)
PARAMS = pltpu.CompilerParams(vmem_limit_bytes=40 * 1024 * 1024)


def picks():
    slot = np.arange(SLOTS)
    rank, place = slot // SHARDS, slot % SHARDS
    source = (place % PLANES) * LANES + place // PLANES
    row = source * (2 * RANKS) + rank * 2
    out = [jnp.arange(ROWS)[None, :] == jnp.asarray(row + h, jnp.int32)[:, None] for h in range(2)]
    return jnp.stack(out).astype(bf16)


def on_device(embeddings, cluster_of):
    rep = lax.axis_index("rep").reshape(1)
    lane = (lax.axis_index("x") * 2 + lax.axis_index("core")).reshape(1)
    outgoing, slot = pl.pallas_call(
        dispatch_kernel,
        grid_spec=pltpu.PrefetchScalarGridSpec(
            num_scalar_prefetch=1,
            grid=(1,),
            in_specs=[
                pl.BlockSpec((1, DOCS), lambda i, r: (0, 0)),
                pl.BlockSpec((DOCS, WIDTH), lambda i, r: (0, r[0])),
            ],
            out_specs=[
                pl.BlockSpec((ROWS, HALF), lambda i, r: (0, 0)),
                pl.BlockSpec((1, DOCS), lambda i, r: (0, 0)),
            ],
        ),
        out_shape=[
            jax.ShapeDtypeStruct((ROWS, HALF), bf16),
            jax.ShapeDtypeStruct((1, DOCS), jnp.int32),
        ],
        compiler_params=PARAMS,
        name="dispatch",
    )(rep, cluster_of.reshape(1, DOCS), embeddings)
    rows = lax.all_to_all(
        outgoing.reshape(SHARDS, 2 * RANKS, HALF), ("z", "x", "core"), 0, 0, tiled=True
    ).reshape(ROWS, HALF)
    grams = pl.pallas_call(
        gram_kernel,
        in_specs=[VMEM, VMEM],
        out_specs=VMEM,
        out_shape=jax.ShapeDtypeStruct((REPS, PAIR_ROWS, 256), f32),
        scratch_shapes=[pltpu.VMEM((SLOTS, SLOTS), f32)],
        compiler_params=PARAMS,
        name="gram",
    )(picks(), rows)
    parts = lax.all_to_all(grams, "rep", 0, 0, tiled=True)
    best = pl.pallas_call(
        best_kernel,
        in_specs=[SMEM, VMEM],
        out_specs=VMEM,
        out_shape=jax.ShapeDtypeStruct((LANES * REPS, RANKS, 128), f32),
        compiler_params=PARAMS,
        name="best",
    )(rep, parts)
    best = lax.all_to_all(best, ("x", "core", "rep"), 0, 0, tiled=True)
    turned = pl.pallas_call(
        turn_kernel,
        in_specs=[SMEM, VMEM],
        out_specs=VMEM,
        out_shape=jax.ShapeDtypeStruct((PLANES, 1, 128), f32),
        scratch_shapes=[pltpu.VMEM((128, 128), f32)],
        compiler_params=PARAMS,
        name="turn",
    )(lane, best)
    returned = lax.all_to_all(turned, "z", 0, 0, tiled=True)
    out = pl.pallas_call(
        collect_kernel,
        in_specs=[VMEM, VMEM],
        out_specs=VMEM,
        out_shape=jax.ShapeDtypeStruct((1, DOCS), f32),
        compiler_params=PARAMS,
        name="collect",
    )(slot, returned)
    return out.reshape(DOCS)


def solution(mesh):
    fine = Mesh(mesh.devices.reshape(PLANES, LANES // 2, 2, REPS), ("z", "x", "core", "rep"))
    shard = ("z", "x", "core")
    return jax.shard_map(
        on_device,
        mesh=fine,
        in_specs=(P(shard, None), P(shard)),
        out_specs=P(shard),
        check_vma=False,
    )
```

```python
import jax
import jax.numpy as jnp
from jax import lax
from jax.experimental import pallas as pl
from jax.experimental.pallas import tpu as pltpu
from jax.sharding import Mesh
from jax.sharding import PartitionSpec as P

SHARDS = 128
PLANES = 16
LANES = 8
PARTS = 4
PAIR = 2
REPS = 4
RANKS = 4
DOCS = 256
WIDTH = 4096
QUARTER = WIDTH // PARTS
HALF = QUARTER // 2
ROWS = SHARDS * RANKS * 2
SLOTS = SHARDS * RANKS
LOCAL = SLOTS // LANES
CHUNK = 256
BLOCK = LOCAL + 8

epsilon = 1e-06
f32 = jnp.float32
bf16 = jnp.bfloat16


def iota(shape, dim):
    return lax.broadcasted_iota(jnp.int32, shape, dim)


def dispatch_kernel(
    rep_ref, cluster_ref, docs_ref, out_ref, slot_ref, labels, docs, staged, label_sem, sems, out_sems
):
    fetch_labels = pltpu.make_async_copy(cluster_ref, labels, label_sem)
    fetch_labels.start()
    fetches = []
    for part in range(PARTS):
        columns = slice(part * QUARTER, (part + 1) * QUARTER)
        fetch = pltpu.make_async_copy(docs_ref.at[:, columns], docs.at[part], sems.at[part])
        fetch.start()
        fetches.append(fetch)
    fetch_labels.wait()
    cluster = labels[...]
    row = jnp.broadcast_to(cluster.astype(f32), (DOCS, DOCS))
    first, second = iota((DOCS, DOCS), 0), iota((DOCS, DOCS), 1)
    column = jnp.max(jnp.where(first == second, row, f32(-1.0)), axis=1, keepdims=True)
    earlier = (column == row) & (first < second)
    rank = jnp.sum(jnp.where(earlier, f32(1.0), f32(0.0)), axis=0, keepdims=True)
    slot = cluster * RANKS + rank.astype(jnp.int32)
    slot_ref[...] = slot
    local = slot - rep_ref[0] * SHARDS
    chosen = jnp.where((first >> 1) == local, f32(1.0), f32(0.0)).astype(bf16)
    live = jnp.dot(chosen, jnp.ones((DOCS, 128), bf16), preferred_element_type=f32) > 0.5
    odd = (iota((DOCS, 128), 0) & 1) == 1
    stores = []
    for part in range(PARTS):
        fetches[part].wait()
        even_rows = jnp.dot(chosen, docs[part, :, :HALF], preferred_element_type=f32)
        odd_rows = jnp.dot(chosen, docs[part, :, HALF:], preferred_element_type=f32)
        for start in range(0, HALF, 128):
            lanes = slice(start, start + 128)
            merged = jnp.where(odd, odd_rows[:, lanes], even_rows[:, lanes])
            if start == 0:
                merged = jnp.where(live, merged, jnp.nan)
            staged[part, :, :, lanes] = merged.astype(bf16).reshape(PLANES, 16, 128)
        store = pltpu.make_async_copy(staged.at[part], out_ref.at[:, part], out_sems.at[part])
        store.start()
        stores.append(store)
    for store in stores:
        store.wait()


def gram_kernel(rows_ref, out_ref, slots_ref, vacant_ref):
    row = iota((CHUNK, CHUNK), 0)
    half, lane, rank, plane = row >> 7, (row >> 4) & 7, (row >> 2) & 3, row & 3
    source = (plane * LANES + lane) * (2 * RANKS) + rank * 2 + half
    pick = jnp.where(iota((CHUNK, CHUNK), 1) == source, f32(1.0), f32(0.0)).astype(bf16)
    for chunk in range(ROWS // CHUNK):
        span = slice(chunk * CHUNK, (chunk + 1) * CHUNK)
        marked = rows_ref[span, :128].astype(f32)
        empty = marked != marked
        clean = jnp.where(empty, f32(0.0), marked).astype(bf16)
        flags = jnp.where(empty, f32(1.0), f32(0.0)).astype(bf16)
        rows = jnp.concatenate([clean, rows_ref[span, 128:]], axis=1)
        picked = jnp.dot(pick, rows, preferred_element_type=f32).astype(bf16)
        vacant = jnp.dot(pick[: CHUNK // 2], flags, preferred_element_type=f32)
        for lane in range(LANES):
            at = slice(lane * LOCAL + chunk * 16, lane * LOCAL + (chunk + 1) * 16)
            slots_ref[at, :HALF] = picked[lane * 16 : (lane + 1) * 16]
            slots_ref[at, HALF:] = picked[128 + lane * 16 : 128 + (lane + 1) * 16]
            vacant_ref[at, :] = vacant[lane * 16 : (lane + 1) * 16]
    slots = slots_ref[...]
    eye = iota((128, 128), 0) == iota((128, 128), 1)
    squares = []
    for b in range(SLOTS // 128):
        span = slice(b * 128, (b + 1) * 128)
        products = lax.dot_general(
            slots[span], slots, (((1,), (1,)), ((), ())), preferred_element_type=f32
        )
        diagonal = jnp.where(eye & (vacant_ref[span, :] > 0.5), jnp.nan, products[:, span])
        squares.append(jnp.sum(jnp.where(eye, diagonal, f32(0.0)), axis=0, keepdims=True))
        for half in range(2):
            rows = slice(half * LOCAL, (half + 1) * LOCAL)
            out_ref[2 * b + half, :LOCAL, :] = products[rows]
            out_ref[2 * b + half, :LOCAL, span] = diagonal[rows]
    norms = jnp.broadcast_to(jnp.concatenate(squares, axis=1), (8, SLOTS))
    for lane in range(LANES):
        out_ref[lane, LOCAL:, :] = norms


def best_kernel(lane_ref, parts_ref, out_ref):
    row, column = iota((LOCAL, SLOTS), 0), iota((LOCAL, SLOTS), 1)
    same = column == row + lane_ref[0] * LOCAL
    spot = iota((LOCAL, 128), 1)
    rank = (iota((LOCAL, 128), 0) >> 2) & 3
    spread = jnp.zeros((LOCAL, 128), f32)

    def scale(squares):
        return jnp.where(squares == squares, lax.rsqrt(squares + epsilon), f32(-1.0))

    for cluster in range(PAIR):
        total = parts_ref[cluster]
        for part in range(1, PARTS):
            total = total + parts_ref[part * PAIR + cluster]
        products = total[:LOCAL]
        own = scale(jnp.sum(jnp.where(same, products, f32(0.0)), axis=1, keepdims=True))
        mate = scale(total[LOCAL : LOCAL + 1])
        cosine = products * own * mate
        mates = (own >= 0.0) & (mate >= 0.0) & jnp.logical_not(same)
        best = jnp.max(jnp.where(mates, cosine, f32(-1.0)), axis=1, keepdims=True)
        spread = jnp.where(spot == cluster * RANKS + rank, best, spread)
    planes = []
    for chunk in range(4):
        both = spread[chunk * 16 : chunk * 16 + 8] + spread[chunk * 16 + 8 : chunk * 16 + 16]
        planes.append(both[0:4] + both[4:8])
    turned = jnp.concatenate(planes, axis=0).reshape(PLANES, 1, 128)
    for rep in range(REPS):
        out_ref[rep * PLANES : (rep + 1) * PLANES] = turned


def collect_kernel(slot_ref, best_ref, out_ref):
    slot = slot_ref[...]
    best = best_ref[...].reshape(REPS * PLANES, 128)
    chosen = jnp.where(iota((128, DOCS), 0) == slot % (PAIR * RANKS), f32(1.0), f32(0.0))
    values = jnp.dot(best, chosen, precision=lax.Precision.HIGHEST, preferred_element_type=f32)
    line = iota((REPS * PLANES, DOCS), 0) == slot // (PAIR * RANKS)
    out_ref[...] = jnp.sum(jnp.where(line, values, f32(0.0)), axis=0, keepdims=True)


VMEM = pl.BlockSpec(memory_space=pltpu.VMEM)
SMEM = pl.BlockSpec(memory_space=pltpu.SMEM)
HBM = pl.BlockSpec(memory_space=pltpu.HBM)
WIDE = pltpu.CompilerParams(vmem_limit_bytes=60 * 1024 * 1024)
PARAMS = pltpu.CompilerParams(vmem_limit_bytes=32 * 1024 * 1024)


def on_device(embeddings, cluster_of):
    rep = lax.axis_index("rep").reshape(1)
    lane = (lax.axis_index("x") * 2 + lax.axis_index("core")).reshape(1)
    outgoing, slot = pl.pallas_call(
        dispatch_kernel,
        in_specs=[SMEM, HBM, HBM],
        out_specs=[HBM, VMEM],
        out_shape=[
            jax.ShapeDtypeStruct((PLANES, PARTS, 16, HALF), bf16),
            jax.ShapeDtypeStruct((1, DOCS), jnp.int32),
        ],
        scratch_shapes=[
            pltpu.VMEM((1, DOCS), jnp.int32),
            pltpu.VMEM((PARTS, DOCS, QUARTER), bf16),
            pltpu.VMEM((PARTS, PLANES, 16, HALF), bf16),
            pltpu.SemaphoreType.DMA,
            pltpu.SemaphoreType.DMA((PARTS,)),
            pltpu.SemaphoreType.DMA((PARTS,)),
        ],
        compiler_params=WIDE,
        name="dispatch",
    )(rep, cluster_of.reshape(1, DOCS), embeddings)
    rows = lax.all_to_all(
        outgoing.reshape(SHARDS, 2 * RANKS, HALF), ("z", "x", "core"), 0, 0, tiled=True
    ).reshape(ROWS, HALF)
    products = pl.pallas_call(
        gram_kernel,
        in_specs=[VMEM],
        out_specs=VMEM,
        out_shape=jax.ShapeDtypeStruct((LANES, BLOCK, SLOTS), f32),
        scratch_shapes=[pltpu.VMEM((SLOTS, QUARTER), bf16), pltpu.VMEM((SLOTS, 128), f32)],
        compiler_params=PARAMS,
        name="gram",
    )(rows)
    products = lax.all_to_all(products, ("x", "core"), 0, 0, tiled=True)
    best = pl.pallas_call(
        best_kernel,
        in_specs=[SMEM, VMEM],
        out_specs=VMEM,
        out_shape=jax.ShapeDtypeStruct((REPS * PLANES, 1, 128), f32),
        compiler_params=PARAMS,
        name="best",
    )(lane, products)
    returned = lax.all_to_all(best, ("rep", "z"), 0, 0, tiled=True)
    out = pl.pallas_call(
        collect_kernel,
        in_specs=[VMEM, VMEM],
        out_specs=VMEM,
        out_shape=jax.ShapeDtypeStruct((1, DOCS), f32),
        compiler_params=PARAMS,
        name="collect",
    )(slot, returned)
    return out.reshape(DOCS)


def solution(mesh):
    fine = Mesh(mesh.devices.reshape(PLANES, PARTS, PAIR, REPS), ("z", "x", "core", "rep"))
    shard = ("z", "x", "core")
    return jax.shard_map(
        on_device,
        mesh=fine,
        in_specs=(P(shard, None), P(shard)),
        out_specs=P(shard),
        check_vma=False,
    )
```

```python
import jax
import jax.numpy as jnp
from jax import lax
from jax.experimental import pallas as pl
from jax.experimental.pallas import tpu as pltpu
from jax.sharding import Mesh
from jax.sharding import PartitionSpec as P

PLANES = 16
LANES = 4
PARTS = 2
PAIR = 2
REPS = 4
RANKS = 4
DOCS = 256
WIDTH = 4096
SHARE = WIDTH // PARTS
HALF = SHARE // 2
SOURCES = PLANES * LANES
SLOTS = SOURCES * RANKS
ROWS = SLOTS * 2
CHUNK = 256
LOCAL = SLOTS // LANES
BLOCK = LOCAL + 8

epsilon = 1e-06
f32 = jnp.float32
bf16 = jnp.bfloat16


def iota(shape, dim):
    return lax.broadcasted_iota(jnp.int32, shape, dim)


def dispatch_kernel(rep_ref, cluster_ref, docs_ref, out_ref, slot_ref, docs, sems):
    fetches = []
    for part in range(PARTS):
        columns = slice(part * SHARE, (part + 1) * SHARE)
        fetch = pltpu.make_async_copy(docs_ref.at[:, columns], docs.at[part], sems.at[part])
        fetch.start()
        fetches.append(fetch)
    cluster = cluster_ref[...]
    row = jnp.broadcast_to(cluster.astype(f32), (DOCS, DOCS))
    first, second = iota((DOCS, DOCS), 0), iota((DOCS, DOCS), 1)
    column = jnp.max(jnp.where(first == second, row, f32(-1.0)), axis=1, keepdims=True)
    earlier = (column == row) & (first < second)
    rank = jnp.sum(jnp.where(earlier, f32(1.0), f32(0.0)), axis=0, keepdims=True)
    slot = cluster * RANKS + rank.astype(jnp.int32)
    slot_ref[...] = slot
    local = slot - rep_ref[0] * (PLANES * PAIR * RANKS)
    chosen = jnp.where((first >> 1) == local, f32(1.0), f32(0.0)).astype(bf16)
    live = jnp.dot(chosen, jnp.ones((DOCS, 128), bf16), preferred_element_type=f32) > 0.5
    odd = (iota((DOCS, 128), 0) & 1) == 1
    for part in range(PARTS):
        fetches[part].wait()
        for start in range(0, HALF, 256):
            here = slice(start, start + 256)
            there = slice(HALF + start, HALF + start + 256)
            even_rows = jnp.dot(chosen, docs[part, :, here], preferred_element_type=f32)
            odd_rows = jnp.dot(chosen, docs[part, :, there], preferred_element_type=f32)
            for step in range(0, 256, 128):
                lanes = slice(step, step + 128)
                merged = jnp.where(odd, odd_rows[:, lanes], even_rows[:, lanes])
                if start + step == 0:
                    merged = jnp.where(live, merged, jnp.nan)
                target = slice(start + step, start + step + 128)
                out_ref[:, part, :, target] = merged.astype(bf16).reshape(PLANES, 16, 128)


def gram_kernel(own_ref, other_ref, out_ref, slots_ref, vacant_ref):
    row = iota((CHUNK, CHUNK), 0)
    half, lane, rank, plane = row >> 7, (row >> 5) & 3, (row >> 3) & 3, row & 7
    source = (plane * LANES + lane) * (2 * RANKS) + rank * 2 + half
    pick = jnp.where(iota((CHUNK, CHUNK), 1) == source, f32(1.0), f32(0.0)).astype(bf16)
    for side, rows_ref in enumerate((own_ref, other_ref)):
        for chunk in range(ROWS // CHUNK):
            span = slice(chunk * CHUNK, (chunk + 1) * CHUNK)
            marked = rows_ref[span, :128].astype(f32)
            empty = marked != marked
            clean = jnp.where(empty, f32(0.0), marked).astype(bf16)
            flags = jnp.where(empty, f32(1.0), f32(0.0)).astype(bf16)
            rows = jnp.concatenate([clean, rows_ref[span, 128:]], axis=1)
            picked = jnp.dot(pick, rows, preferred_element_type=f32).astype(bf16)
            vacant = jnp.dot(pick[: CHUNK // 2], flags, preferred_element_type=f32)
            for lane in range(LANES):
                top = side * SLOTS + lane * LOCAL + chunk * 32
                slots_ref[top : top + 32, :HALF] = picked[lane * 32 : (lane + 1) * 32]
                slots_ref[top : top + 32, HALF:] = picked[128 + lane * 32 : 128 + (lane + 1) * 32]
                vacant_ref[top : top + 32, :] = vacant[lane * 32 : (lane + 1) * 32]

    def multiply(left, right):
        return lax.dot_general(left, right, (((1,), (1,)), ((), ())), preferred_element_type=f32)

    def flagged(block, span):
        return jnp.where(eye & (vacant_ref[span, :] > 0.5), jnp.nan, block)

    def diagonal(block):
        return jnp.sum(jnp.where(eye, block, f32(0.0)), axis=0, keepdims=True)

    eye = iota((128, 128), 0) == iota((128, 128), 1)
    squares = []
    for b in range(SLOTS // 128):
        span = slice(b * 128, (b + 1) * 128)
        products = multiply(slots_ref[span, :], slots_ref[...])
        block = flagged(products[:, span], span)
        squares.append(diagonal(block))
        for half in range(2):
            rows = slice(half * LOCAL, (half + 1) * LOCAL)
            out_ref[2 * b + half, :LOCAL, :] = products[rows]
            out_ref[2 * b + half, :LOCAL, span] = block[rows]
    for b in range(SLOTS // 128, 2 * SLOTS // 128):
        span = slice(b * 128, (b + 1) * 128)
        others = slots_ref[span, :]
        squares.append(diagonal(flagged(multiply(others, others), span)))
    norms = jnp.broadcast_to(jnp.concatenate(squares, axis=1), (8, 2 * SLOTS))
    for lane in range(LANES):
        out_ref[lane, LOCAL:, :] = norms


def best_kernel(lane_ref, parts_ref, out_ref):
    row, column = iota((LOCAL, 2 * SLOTS), 0), iota((LOCAL, 2 * SLOTS), 1)
    same = column == row + lane_ref[0] * LOCAL
    spot = iota((LOCAL, 128), 1)
    rank = (iota((LOCAL, 128), 0) >> 3) & 3
    spread = jnp.zeros((LOCAL, 128), f32)

    def scale(squares):
        return jnp.where(squares == squares, lax.rsqrt(squares + epsilon), f32(-1.0))

    for cluster in range(PAIR):
        total = parts_ref[cluster] + parts_ref[PAIR + cluster]
        products = total[:LOCAL]
        own = scale(jnp.sum(jnp.where(same, products, f32(0.0)), axis=1, keepdims=True))
        mate = scale(total[LOCAL : LOCAL + 1])
        cosine = products * own * mate
        mates = (own >= 0.0) & (mate >= 0.0) & jnp.logical_not(same)
        best = jnp.max(jnp.where(mates, cosine, f32(-1.0)), axis=1, keepdims=True)
        spread = jnp.where(spot == cluster * RANKS + rank, best, spread)
    planes = []
    for top in range(0, LOCAL, 32):
        tiles = [spread[top + k * 8 : top + (k + 1) * 8] for k in range(RANKS)]
        planes.append((tiles[0] + tiles[1]) + (tiles[2] + tiles[3]))
    turned = jnp.concatenate(planes, axis=0).reshape(PLANES, 1, 128)
    for rep in range(REPS):
        out_ref[rep * PLANES : (rep + 1) * PLANES] = turned


def collect_kernel(slot_ref, best_ref, out_ref):
    slot = slot_ref[...]
    best = best_ref[...].reshape(REPS * PLANES, 128)
    chosen = jnp.where(iota((128, DOCS), 0) == slot % (PAIR * RANKS), f32(1.0), f32(0.0))
    values = jnp.dot(best, chosen, precision=lax.Precision.HIGHEST, preferred_element_type=f32)
    line = iota((REPS * PLANES, DOCS), 0) == slot // (PAIR * RANKS)
    out_ref[...] = jnp.sum(jnp.where(line, values, f32(0.0)), axis=0, keepdims=True)


VMEM = pl.BlockSpec(memory_space=pltpu.VMEM)
SMEM = pl.BlockSpec(memory_space=pltpu.SMEM)
HBM = pl.BlockSpec(memory_space=pltpu.HBM)
WIDE = pltpu.CompilerParams(vmem_limit_bytes=52 * 1024 * 1024)
PARAMS = pltpu.CompilerParams(vmem_limit_bytes=32 * 1024 * 1024)


def on_device(embeddings, cluster_of):
    rep = lax.axis_index("rep").reshape(1)
    lane = lax.axis_index("x").reshape(1)
    outgoing, slot = pl.pallas_call(
        dispatch_kernel,
        in_specs=[SMEM, VMEM, HBM],
        out_specs=[VMEM, VMEM],
        out_shape=[
            jax.ShapeDtypeStruct((PLANES, PARTS, 16, HALF), bf16),
            jax.ShapeDtypeStruct((1, DOCS), jnp.int32),
        ],
        scratch_shapes=[
            pltpu.VMEM((PARTS, DOCS, SHARE), bf16),
            pltpu.SemaphoreType.DMA((PARTS,)),
        ],
        compiler_params=WIDE,
        name="dispatch",
    )(rep, cluster_of.reshape(1, DOCS), embeddings)
    own = lax.all_to_all(
        outgoing.reshape(SOURCES, 2 * RANKS, HALF), ("z", "x"), 0, 0, tiled=True
    ).reshape(ROWS, HALF)
    other = lax.ppermute(own, "core", [(0, 1), (1, 0)])
    products = pl.pallas_call(
        gram_kernel,
        in_specs=[VMEM, VMEM],
        out_specs=VMEM,
        out_shape=jax.ShapeDtypeStruct((LANES, BLOCK, 2 * SLOTS), f32),
        scratch_shapes=[pltpu.VMEM((2 * SLOTS, SHARE), bf16), pltpu.VMEM((2 * SLOTS, 128), f32)],
        compiler_params=PARAMS,
        name="gram",
    )(own, other)
    products = lax.all_to_all(products, "x", 0, 0, tiled=True)
    best = pl.pallas_call(
        best_kernel,
        in_specs=[SMEM, VMEM],
        out_specs=VMEM,
        out_shape=jax.ShapeDtypeStruct((REPS * PLANES, 1, 128), f32),
        compiler_params=PARAMS,
        name="best",
    )(lane, products)
    returned = lax.all_to_all(best, ("rep", "z"), 0, 0, tiled=True)
    out = pl.pallas_call(
        collect_kernel,
        in_specs=[VMEM, VMEM],
        out_specs=VMEM,
        out_shape=jax.ShapeDtypeStruct((1, DOCS), f32),
        compiler_params=PARAMS,
        name="collect",
    )(slot, returned)
    return out.reshape(DOCS)


def solution(mesh):
    fine = Mesh(mesh.devices.reshape(PLANES, LANES, 2, REPS), ("z", "x", "core", "rep"))
    shard = ("z", "x", "core")
    return jax.shard_map(
        on_device,
        mesh=fine,
        in_specs=(P(shard, None), P(shard)),
        out_specs=P(shard),
        check_vma=False,
    )
```

```python
import jax
import jax.numpy as jnp
from jax import lax
from jax.experimental import pallas as pl
from jax.experimental.pallas import tpu as pltpu
from jax.sharding import Mesh
from jax.sharding import PartitionSpec as P

PLANES = 16
LANES = 4
PARTS = 2
PAIR = 2
REPS = 4
RANKS = 4
DOCS = 256
WIDTH = 4096
SHARE = WIDTH // PARTS
HALF = SHARE // 2
SOURCES = PLANES * LANES
SLOTS = SOURCES * RANKS
ROWS = SLOTS * 2
CHUNK = 256
LOCAL = SLOTS // LANES
BLOCK = 4 * LOCAL + 8
STRIP = HALF // 2
STEPS = PARTS * 2

epsilon = 1e-06
f32 = jnp.float32
bf16 = jnp.bfloat16


def iota(shape, dim):
    return lax.broadcasted_iota(jnp.int32, shape, dim)


def dispatch_kernel(
    rep_ref, cluster_ref, docs_ref, out_ref, slot_ref, labels, docs, label_sem, sems
):
    fetch_labels = pltpu.make_async_copy(cluster_ref, labels, label_sem)
    fetch_labels.start()
    fetches = []
    for step in range(STEPS):
        fetches.append([])
        for half in range(2):
            at = (step // 2) * SHARE + half * HALF + (step % 2) * STRIP
            fetch = pltpu.make_async_copy(
                docs_ref.at[:, at : at + STRIP],
                docs.at[step, half * DOCS : (half + 1) * DOCS, :],
                sems.at[step, half],
            )
            fetch.start()
            fetches[step].append(fetch)
    fetch_labels.wait()
    cluster = labels[...]
    row = jnp.broadcast_to(cluster.astype(f32), (DOCS, DOCS))
    first, second = iota((DOCS, DOCS), 0), iota((DOCS, DOCS), 1)
    column = jnp.max(jnp.where(first == second, row, f32(-1.0)), axis=1, keepdims=True)
    earlier = (column == row) & (first < second)
    rank = jnp.sum(jnp.where(earlier, f32(1.0), f32(0.0)), axis=0, keepdims=True)
    slot = cluster * RANKS + rank.astype(jnp.int32)
    slot_ref[...] = slot
    local = slot - rep_ref[0] * (PLANES * PAIR * RANKS)
    hit = (first >> 1) == local
    odd = (first & 1) == 1
    zero, one = f32(0.0), f32(1.0)
    chosen = jnp.concatenate(
        [
            jnp.where(hit & jnp.logical_not(odd), one, zero).astype(bf16),
            jnp.where(hit & odd, one, zero).astype(bf16),
        ],
        axis=1,
    )
    live = jnp.dot(chosen, jnp.ones((2 * DOCS, 128), bf16), preferred_element_type=f32) > 0.5
    for step in range(STEPS):
        for fetch in fetches[step]:
            fetch.wait()
        merged = jnp.dot(chosen, docs[step], preferred_element_type=f32)
        at = (step % 2) * STRIP
        if at == 0:
            marked = jnp.where(live, merged[:, :128], jnp.nan)
            merged = jnp.concatenate([marked, merged[:, 128:]], axis=1)
        out_ref[:, step // 2, :, at : at + STRIP] = merged.astype(bf16).reshape(PLANES, 16, STRIP)


def multiply(left, right):
    return lax.dot_general(left, right, (((1,), (1,)), ((), ())), preferred_element_type=f32)


def gather_slots(rows_ref, slots_ref, vacant_ref):
    row = iota((CHUNK, CHUNK), 0)
    half, lane, rank, plane = row >> 7, (row >> 5) & 3, (row >> 3) & 3, row & 7
    source = (plane * LANES + lane) * (2 * RANKS) + rank * 2 + half
    pick = jnp.where(iota((CHUNK, CHUNK), 1) == source, f32(1.0), f32(0.0)).astype(bf16)
    for chunk in range(ROWS // CHUNK):
        span = slice(chunk * CHUNK, (chunk + 1) * CHUNK)
        marked = rows_ref[span, :128].astype(f32)
        empty = marked != marked
        clean = jnp.where(empty, f32(0.0), marked).astype(bf16)
        flags = jnp.where(empty, f32(1.0), f32(0.0)).astype(bf16)
        rows = jnp.concatenate([clean, rows_ref[span, 128:], flags], axis=1)
        picked = jnp.dot(pick, rows, preferred_element_type=f32)
        slots = picked[:, :HALF].astype(bf16)
        for lane in range(LANES):
            top = lane * LOCAL + chunk * 32
            slots_ref[top : top + 32, :HALF] = slots[lane * 32 : (lane + 1) * 32]
            slots_ref[top : top + 32, HALF:] = slots[128 + lane * 32 : 128 + (lane + 1) * 32]
            vacant_ref[top : top + 32, :] = picked[lane * 32 : (lane + 1) * 32, HALF:]


def flagged_block(block, vacant):
    eye = iota((128, 128), 0) == iota((128, 128), 1)
    flagged = jnp.where(eye & (vacant > 0.5), jnp.nan, block)
    return flagged, jnp.sum(jnp.where(eye, flagged, f32(0.0)), axis=0, keepdims=True)


def own_kernel(rows_ref, out_ref, slots_ref, vacant_ref):
    gather_slots(rows_ref, slots_ref, vacant_ref)
    slots = slots_ref[...]
    products = multiply(slots, slots)
    for b in range(2):
        span = slice(b * 128, (b + 1) * 128)
        block, squares = flagged_block(products[span, span], vacant_ref[span, :])
        for lane in range(LANES):
            rows = slice(lane * LOCAL, (lane + 1) * LOCAL)
            inside = slice((lane % 2) * LOCAL, (lane % 2 + 1) * LOCAL)
            tile = block[inside] if lane // 2 == b else products[rows, span]
            out_ref[lane, b * LOCAL : (b + 1) * LOCAL, :] = tile
            out_ref[lane, 4 * LOCAL + b : 4 * LOCAL + b + 1, :] = squares


def cross_kernel(part_ref, slots_ref, rows_ref, out_ref, other_ref, vacant_ref):
    gather_slots(rows_ref, other_ref, vacant_ref)
    products = multiply(slots_ref[...], other_ref[...])
    for lane in range(LANES):
        rows = slice(lane * LOCAL, (lane + 1) * LOCAL)
        out_ref[lane, : 2 * LOCAL, :] = part_ref[lane, : 2 * LOCAL, :]
        out_ref[lane, 2 * LOCAL : 3 * LOCAL, :] = products[rows, :128]
        out_ref[lane, 3 * LOCAL : 4 * LOCAL, :] = products[rows, 128:]
    for b in range(2):
        span = slice(b * 128, (b + 1) * 128)
        others = other_ref[span, :]
        squares = flagged_block(multiply(others, others), vacant_ref[span, :])[1]
        for lane in range(LANES):
            out_ref[lane, 4 * LOCAL + 2 + b : 4 * LOCAL + 3 + b, :] = squares
    for lane in range(LANES):
        own_norms = slice(4 * LOCAL, 4 * LOCAL + 2)
        out_ref[lane, own_norms, :] = part_ref[lane, own_norms, :]
        out_ref[lane, 4 * LOCAL + 4 :, :] = jnp.zeros((4, 128), f32)


def best_kernel(lane_ref, parts_ref, out_ref):
    row, column = iota((LOCAL, 128), 0), iota((LOCAL, 128), 1)
    spot = column & 7
    rank = (row >> 3) & 3
    spread = jnp.zeros((LOCAL, 128), f32)

    def scale(squares):
        return jnp.where(squares == squares, lax.rsqrt(squares + epsilon), f32(-1.0))

    for cluster in range(PAIR):
        total = parts_ref[cluster] + parts_ref[PAIR + cluster]
        tiles = [total[t * LOCAL : (t + 1) * LOCAL] for t in range(4)]
        mates = [scale(total[4 * LOCAL + t : 4 * LOCAL + t + 1]) for t in range(4)]
        same = [column + t * 128 == row + lane_ref[0] * LOCAL for t in range(2)]
        squares = jnp.where(same[0], tiles[0], f32(0.0)) + jnp.where(same[1], tiles[1], f32(0.0))
        own = scale(jnp.sum(squares, axis=1, keepdims=True))
        best = jnp.full((LOCAL, 128), -1.0, f32)
        for t in range(4):
            cosine = tiles[t] * own * mates[t]
            allowed = (own >= 0.0) & (mates[t] >= 0.0)
            if t < 2:
                allowed = allowed & jnp.logical_not(same[t])
            best = jnp.maximum(best, jnp.where(allowed, cosine, f32(-1.0)))
        best = jnp.max(best, axis=1, keepdims=True)
        spread = jnp.where(spot == cluster * RANKS + rank, best, spread)
    planes = []
    for top in range(0, LOCAL, 32):
        tiles = [spread[top + k * 8 : top + (k + 1) * 8] for k in range(RANKS)]
        planes.append((tiles[0] + tiles[1]) + (tiles[2] + tiles[3]))
    turned = jnp.concatenate(planes, axis=0)
    for rep in range(REPS):
        out_ref[rep * PLANES : (rep + 1) * PLANES, :] = turned


def collect_kernel(slot_ref, best_ref, out_ref):
    slot = slot_ref[...]
    best = best_ref[...]
    high = best.astype(bf16).astype(f32)
    middle = (best - high).astype(bf16).astype(f32)
    low = best - high - middle
    group = iota((REPS * PLANES, 128), 1) >> 3
    pieces = jnp.where(group == 0, high, jnp.where(group == 1, middle, low))
    pieces = jnp.where(group < 3, pieces, f32(0.0)).astype(bf16)
    chosen = (iota((128, DOCS), 0) & 7) == (slot & 7)
    chosen = jnp.where(chosen, f32(1.0), f32(0.0)).astype(bf16)
    values = jnp.dot(pieces, chosen, preferred_element_type=f32)
    line = iota((REPS * PLANES, DOCS), 0) == (slot >> 3)
    out_ref[...] = jnp.sum(jnp.where(line, values, f32(0.0)), axis=0, keepdims=True)


VMEM = pl.BlockSpec(memory_space=pltpu.VMEM)
SMEM = pl.BlockSpec(memory_space=pltpu.SMEM)
HBM = pl.BlockSpec(memory_space=pltpu.HBM)
WIDE = pltpu.CompilerParams(vmem_limit_bytes=52 * 1024 * 1024)
PARAMS = pltpu.CompilerParams(vmem_limit_bytes=32 * 1024 * 1024)


def on_device(embeddings, cluster_of):
    rep = lax.axis_index("rep").reshape(1)
    lane = lax.axis_index("x").reshape(1)
    outgoing, slot = pl.pallas_call(
        dispatch_kernel,
        in_specs=[SMEM, HBM, HBM],
        out_specs=[VMEM, VMEM],
        out_shape=[
            jax.ShapeDtypeStruct((PLANES, PARTS, 16, HALF), bf16),
            jax.ShapeDtypeStruct((1, DOCS), jnp.int32),
        ],
        scratch_shapes=[
            pltpu.VMEM((1, DOCS), jnp.int32),
            pltpu.VMEM((STEPS, 2 * DOCS, STRIP), bf16),
            pltpu.SemaphoreType.DMA,
            pltpu.SemaphoreType.DMA((STEPS, 2)),
        ],
        compiler_params=WIDE,
        name="dispatch",
    )(rep, cluster_of.reshape(1, DOCS), embeddings)
    own_rows = lax.all_to_all(
        outgoing.reshape(SOURCES, 2 * RANKS, HALF), ("z", "x"), 0, 0, tiled=True
    ).reshape(ROWS, HALF)
    other_rows = lax.ppermute(own_rows, "core", [(0, 1), (1, 0)])
    part, slots = pl.pallas_call(
        own_kernel,
        in_specs=[VMEM],
        out_specs=[VMEM, VMEM],
        out_shape=[
            jax.ShapeDtypeStruct((LANES, BLOCK, 128), f32),
            jax.ShapeDtypeStruct((SLOTS, SHARE), bf16),
        ],
        scratch_shapes=[pltpu.VMEM((SLOTS, 128), f32)],
        compiler_params=PARAMS,
        cost_estimate=pl.CostEstimate(
            flops=2 * SLOTS * SLOTS * SHARE * 2, bytes_accessed=2**22, transcendentals=0
        ),
        name="own",
    )(own_rows)
    products = pl.pallas_call(
        cross_kernel,
        in_specs=[VMEM, VMEM, VMEM],
        out_specs=VMEM,
        out_shape=jax.ShapeDtypeStruct((LANES, BLOCK, 128), f32),
        scratch_shapes=[pltpu.VMEM((SLOTS, SHARE), bf16), pltpu.VMEM((SLOTS, 128), f32)],
        compiler_params=PARAMS,
        name="cross",
    )(part, slots, other_rows)
    products = lax.all_to_all(products, "x", 0, 0, tiled=True)
    best = pl.pallas_call(
        best_kernel,
        in_specs=[SMEM, VMEM],
        out_specs=VMEM,
        out_shape=jax.ShapeDtypeStruct((REPS * PLANES, 128), f32),
        compiler_params=PARAMS,
        name="best",
    )(lane, products)
    returned = lax.all_to_all(
        best.reshape(REPS * PLANES, 1, 128), ("rep", "z"), 0, 0, tiled=True
    ).reshape(REPS * PLANES, 128)
    out = pl.pallas_call(
        collect_kernel,
        in_specs=[VMEM, VMEM],
        out_specs=VMEM,
        out_shape=jax.ShapeDtypeStruct((1, DOCS), f32),
        compiler_params=PARAMS,
        name="collect",
    )(slot, returned)
    return out.reshape(DOCS)


def solution(mesh):
    fine = Mesh(mesh.devices.reshape(PLANES, LANES, 2, REPS), ("z", "x", "core", "rep"))
    shard = ("z", "x", "core")
    return jax.shard_map(
        on_device,
        mesh=fine,
        in_specs=(P(shard, None), P(shard)),
        out_specs=P(shard),
        check_vma=False,
    )
```

```python
import jax
import jax.numpy as jnp
from jax import lax
from jax.experimental import pallas as pl
from jax.experimental.pallas import tpu as pltpu
from jax.sharding import Mesh
from jax.sharding import PartitionSpec as P

PLANES = 16
LANES = 4
PARTS = 2
PAIR = 2
REPS = 4
RANKS = 4
DOCS = 256
WIDTH = 4096
SHARE = WIDTH // PARTS
HALF = SHARE // 2
SOURCES = PLANES * LANES
SLOTS = SOURCES * RANKS
ROWS = SLOTS * 2
CHUNK = 256
LOCAL = SLOTS // LANES
BLOCK = 4 * LOCAL + 8
STRIP = HALF // 2
STEPS = PARTS * 2

epsilon = 1e-06
f32 = jnp.float32
bf16 = jnp.bfloat16


def iota(shape, dim):
    return lax.broadcasted_iota(jnp.int32, shape, dim)


def dispatch_kernel(
    rep_ref, cluster_ref, docs_ref, out_ref, slot_ref, labels, docs, label_sem, sems
):
    fetch_labels = pltpu.make_async_copy(cluster_ref, labels, label_sem)
    fetch_labels.start()
    fetches = []
    for step in range(STEPS):
        fetches.append([])
        for half in range(2):
            at = (step // 2) * SHARE + half * HALF + (step % 2) * STRIP
            fetch = pltpu.make_async_copy(
                docs_ref.at[:, at : at + STRIP],
                docs.at[step, half * DOCS : (half + 1) * DOCS, :],
                sems.at[step, half],
            )
            fetch.start()
            fetches[step].append(fetch)
    fetch_labels.wait()
    cluster = labels[...]
    row = jnp.broadcast_to(cluster.astype(f32), (DOCS, DOCS))
    first, second = iota((DOCS, DOCS), 0), iota((DOCS, DOCS), 1)
    column = jnp.max(jnp.where(first == second, row, f32(-1.0)), axis=1, keepdims=True)
    earlier = (column == row) & (first < second)
    rank = jnp.sum(jnp.where(earlier, f32(1.0), f32(0.0)), axis=0, keepdims=True)
    slot = cluster * RANKS + rank.astype(jnp.int32)
    slot_ref[...] = slot
    local = slot - rep_ref[0] * (PLANES * PAIR * RANKS)
    hit = (first >> 1) == local
    odd = (first & 1) == 1
    zero, one = f32(0.0), f32(1.0)
    chosen = jnp.concatenate(
        [
            jnp.where(hit & jnp.logical_not(odd), one, zero).astype(bf16),
            jnp.where(hit & odd, one, zero).astype(bf16),
        ],
        axis=1,
    )
    live = jnp.dot(chosen, jnp.ones((2 * DOCS, 128), bf16), preferred_element_type=f32) > 0.5
    for step in range(STEPS):
        for fetch in fetches[step]:
            fetch.wait()
        merged = jnp.dot(chosen, docs[step], preferred_element_type=f32)
        at = (step % 2) * STRIP
        if at == 0:
            marked = jnp.where(live, merged[:, :128], jnp.nan)
            merged = jnp.concatenate([marked, merged[:, 128:]], axis=1)
        out_ref[:, step // 2, :, at : at + STRIP] = merged.astype(bf16).reshape(PLANES, 16, STRIP)


def multiply(left, right):
    return lax.dot_general(left, right, (((1,), (1,)), ((), ())), preferred_element_type=f32)


def gather_slots(rows_ref, slots_ref, vacant_ref):
    row = iota((CHUNK, CHUNK), 0)
    half, lane, rank, plane = row >> 7, (row >> 5) & 3, (row >> 3) & 3, row & 7
    source = (plane * LANES + lane) * (2 * RANKS) + rank * 2 + half
    pick = jnp.where(iota((CHUNK, CHUNK), 1) == source, f32(1.0), f32(0.0)).astype(bf16)
    for chunk in range(ROWS // CHUNK):
        span = slice(chunk * CHUNK, (chunk + 1) * CHUNK)
        marked = rows_ref[span, :128].astype(f32)
        empty = marked != marked
        clean = jnp.where(empty, f32(0.0), marked).astype(bf16)
        flags = jnp.where(empty, f32(1.0), f32(0.0)).astype(bf16)
        rows = jnp.concatenate([clean, rows_ref[span, 128:], flags], axis=1)
        picked = jnp.dot(pick, rows, preferred_element_type=f32)
        slots = picked[:, :HALF].astype(bf16)
        for lane in range(LANES):
            top = lane * LOCAL + chunk * 32
            slots_ref[top : top + 32, :HALF] = slots[lane * 32 : (lane + 1) * 32]
            slots_ref[top : top + 32, HALF:] = slots[128 + lane * 32 : 128 + (lane + 1) * 32]
            vacant_ref[top : top + 32, :] = picked[lane * 32 : (lane + 1) * 32, HALF:]


def flagged_block(block, vacant):
    eye = iota((128, 128), 0) == iota((128, 128), 1)
    flagged = jnp.where(eye & (vacant > 0.5), jnp.nan, block)
    return flagged, jnp.sum(jnp.where(eye, flagged, f32(0.0)), axis=0, keepdims=True)


def own_kernel(rows_ref, out_ref, slots_ref, vacant_ref):
    gather_slots(rows_ref, slots_ref, vacant_ref)
    slots = slots_ref[...]
    products = multiply(slots, slots)
    for b in range(2):
        span = slice(b * 128, (b + 1) * 128)
        block, squares = flagged_block(products[span, span], vacant_ref[span, :])
        for lane in range(LANES):
            rows = slice(lane * LOCAL, (lane + 1) * LOCAL)
            inside = slice((lane % 2) * LOCAL, (lane % 2 + 1) * LOCAL)
            tile = block[inside] if lane // 2 == b else products[rows, span]
            out_ref[lane, b * LOCAL : (b + 1) * LOCAL, :] = tile
            out_ref[lane, 4 * LOCAL + b : 4 * LOCAL + b + 1, :] = squares
    for lane in range(LANES):
        out_ref[lane, 4 * LOCAL + 4 :, :] = jnp.zeros((4, 128), f32)


def cross_kernel(part_ref, own_ref, rows_ref, out_ref, other_ref, vacant_ref):
    gather_slots(rows_ref, other_ref, vacant_ref)
    other = other_ref[...]
    products = multiply(jnp.concatenate([own_ref[...], other], axis=0), other)
    for lane in range(LANES):
        rows = slice(lane * LOCAL, (lane + 1) * LOCAL)
        own_rows = slice(0, 2 * LOCAL)
        out_ref[lane, own_rows, :] = part_ref[lane, own_rows, :]
        out_ref[lane, 2 * LOCAL : 3 * LOCAL, :] = products[rows, :128]
        out_ref[lane, 3 * LOCAL : 4 * LOCAL, :] = products[rows, 128:]
        out_ref[lane, 4 * LOCAL :, :] = part_ref[lane, 4 * LOCAL :, :]
    for b in range(2):
        span = slice(b * 128, (b + 1) * 128)
        below = products[SLOTS + b * 128 : SLOTS + (b + 1) * 128, span]
        squares = flagged_block(below, vacant_ref[span, :])[1]
        for lane in range(LANES):
            out_ref[lane, 4 * LOCAL + 2 + b : 4 * LOCAL + 3 + b, :] = squares


def best_kernel(lane_ref, parts_ref, out_ref):
    row, column = iota((LOCAL, 128), 0), iota((LOCAL, 128), 1)
    spot = column & 7
    rank = (row >> 3) & 3
    spread = jnp.zeros((LOCAL, 128), f32)

    def scale(squares):
        return jnp.where(squares == squares, lax.rsqrt(squares + epsilon), f32(-1.0))

    for cluster in range(PAIR):
        total = parts_ref[cluster] + parts_ref[PAIR + cluster]
        tiles = [total[t * LOCAL : (t + 1) * LOCAL] for t in range(4)]
        mates = [scale(total[4 * LOCAL + t : 4 * LOCAL + t + 1]) for t in range(4)]
        same = [column + t * 128 == row + lane_ref[0] * LOCAL for t in range(2)]
        squares = jnp.where(same[0], tiles[0], f32(0.0)) + jnp.where(same[1], tiles[1], f32(0.0))
        own = scale(jnp.sum(squares, axis=1, keepdims=True))
        best = jnp.full((LOCAL, 128), -1.0, f32)
        for t in range(4):
            cosine = tiles[t] * own * mates[t]
            allowed = (own >= 0.0) & (mates[t] >= 0.0)
            if t < 2:
                allowed = allowed & jnp.logical_not(same[t])
            best = jnp.maximum(best, jnp.where(allowed, cosine, f32(-1.0)))
        best = jnp.max(best, axis=1, keepdims=True)
        spread = jnp.where(spot == cluster * RANKS + rank, best, spread)
    planes = []
    for top in range(0, LOCAL, 32):
        tiles = [spread[top + k * 8 : top + (k + 1) * 8] for k in range(RANKS)]
        planes.append((tiles[0] + tiles[1]) + (tiles[2] + tiles[3]))
    turned = jnp.concatenate(planes, axis=0)
    for rep in range(REPS):
        out_ref[rep * PLANES : (rep + 1) * PLANES, :] = turned


def collect_kernel(slot_ref, best_ref, out_ref):
    slot = slot_ref[...]
    best = best_ref[...]
    high = best.astype(bf16).astype(f32)
    middle = (best - high).astype(bf16).astype(f32)
    low = best - high - middle
    group = iota((REPS * PLANES, 128), 1) >> 3
    pieces = jnp.where(group == 0, high, jnp.where(group == 1, middle, low))
    pieces = jnp.where(group < 3, pieces, f32(0.0)).astype(bf16)
    chosen = (iota((128, DOCS), 0) & 7) == (slot & 7)
    chosen = jnp.where(chosen, f32(1.0), f32(0.0)).astype(bf16)
    values = jnp.dot(pieces, chosen, preferred_element_type=f32)
    line = iota((REPS * PLANES, DOCS), 0) == (slot >> 3)
    out_ref[...] = jnp.sum(jnp.where(line, values, f32(0.0)), axis=0, keepdims=True)


VMEM = pl.BlockSpec(memory_space=pltpu.VMEM)
SMEM = pl.BlockSpec(memory_space=pltpu.SMEM)
HBM = pl.BlockSpec(memory_space=pltpu.HBM)
PARAMS = pltpu.CompilerParams(vmem_limit_bytes=32 * 1024 * 1024)


def on_device(embeddings, cluster_of):
    rep = lax.axis_index("rep").reshape(1)
    lane = lax.axis_index("x").reshape(1)
    labels = pltpu.with_memory_space_constraint(cluster_of.reshape(1, DOCS), pltpu.HBM)
    outgoing, slot = pl.pallas_call(
        dispatch_kernel,
        in_specs=[SMEM, HBM, HBM],
        out_specs=[VMEM, VMEM],
        out_shape=[
            jax.ShapeDtypeStruct((PLANES, PARTS, 16, HALF), bf16),
            jax.ShapeDtypeStruct((1, DOCS), jnp.int32),
        ],
        scratch_shapes=[
            pltpu.VMEM((1, DOCS), jnp.int32),
            pltpu.VMEM((STEPS, 2 * DOCS, STRIP), bf16),
            pltpu.SemaphoreType.DMA,
            pltpu.SemaphoreType.DMA((STEPS, 2)),
        ],
        compiler_params=PARAMS,
        name="dispatch",
    )(rep, labels, pltpu.with_memory_space_constraint(embeddings, pltpu.HBM))
    own_rows = lax.all_to_all(
        outgoing.reshape(SOURCES, 2 * RANKS, HALF), ("z", "x"), 0, 0, tiled=True
    ).reshape(ROWS, HALF)
    other_rows = lax.ppermute(own_rows, "core", [(0, 1), (1, 0)])
    part, slots = pl.pallas_call(
        own_kernel,
        in_specs=[VMEM],
        out_specs=[VMEM, VMEM],
        out_shape=[
            jax.ShapeDtypeStruct((LANES, BLOCK, 128), f32),
            jax.ShapeDtypeStruct((SLOTS, SHARE), bf16),
        ],
        scratch_shapes=[pltpu.VMEM((SLOTS, 128), f32)],
        compiler_params=PARAMS,
        cost_estimate=pl.CostEstimate(
            flops=2 * SLOTS * SLOTS * SHARE * 2, bytes_accessed=2**22, transcendentals=0
        ),
        name="own",
    )(own_rows)
    products = pl.pallas_call(
        cross_kernel,
        in_specs=[VMEM, VMEM, VMEM],
        out_specs=VMEM,
        out_shape=jax.ShapeDtypeStruct((LANES, BLOCK, 128), f32),
        scratch_shapes=[pltpu.VMEM((SLOTS, SHARE), bf16), pltpu.VMEM((SLOTS, 128), f32)],
        compiler_params=PARAMS,
        name="cross",
    )(part, slots, other_rows)
    products = lax.all_to_all(products, "x", 0, 0, tiled=True)
    best = pl.pallas_call(
        best_kernel,
        in_specs=[SMEM, VMEM],
        out_specs=VMEM,
        out_shape=jax.ShapeDtypeStruct((REPS * PLANES, 128), f32),
        compiler_params=PARAMS,
        name="best",
    )(lane, products)
    returned = lax.all_to_all(
        best.reshape(REPS * PLANES, 1, 128), ("rep", "z"), 0, 0, tiled=True
    ).reshape(REPS * PLANES, 128)
    out = pl.pallas_call(
        collect_kernel,
        in_specs=[VMEM, VMEM],
        out_specs=VMEM,
        out_shape=jax.ShapeDtypeStruct((1, DOCS), f32),
        compiler_params=PARAMS,
        name="collect",
    )(slot, returned)
    return out.reshape(DOCS)


def solution(mesh):
    fine = Mesh(mesh.devices.reshape(PLANES, LANES, 2, REPS), ("z", "x", "core", "rep"))
    shard = ("z", "x", "core")
    return jax.shard_map(
        on_device,
        mesh=fine,
        in_specs=(P(shard, None), P(shard)),
        out_specs=P(shard),
        check_vma=False,
    )
```

```python
import jax
import jax.numpy as jnp
from jax import lax
from jax.experimental import pallas as pl
from jax.experimental.pallas import tpu as pltpu
from jax.sharding import Mesh
from jax.sharding import PartitionSpec as P

PLANES = 16
LANES = 4
PARTS = 2
PAIR = 2
REPS = 4
RANKS = 4
DOCS = 256
WIDTH = 4096
SHARE = WIDTH // PARTS
HALF = SHARE // 2
SOURCES = PLANES * LANES
SLOTS = SOURCES * RANKS
ROWS = SLOTS * 2
CHUNK = 256
LOCAL = SLOTS // LANES
BLOCK = 4 * LOCAL + 8
STRIP = HALF // 2
STEPS = PARTS * 2

epsilon = 1e-06
f32 = jnp.float32
bf16 = jnp.bfloat16


def iota(shape, dim):
    return lax.broadcasted_iota(jnp.int32, shape, dim)


def dispatch_kernel(
    cluster_ref, docs_ref, out_ref, slot_ref, labels, docs, label_sem, sems
):
    fetch_labels = pltpu.make_async_copy(cluster_ref, labels, label_sem)
    fetch_labels.start()
    fetches = []
    for step in range(STEPS):
        fetches.append([])
        for half in range(2):
            at = (step // 2) * SHARE + half * HALF + (step % 2) * STRIP
            fetch = pltpu.make_async_copy(
                docs_ref.at[:, at : at + STRIP],
                docs.at[step, half * DOCS : (half + 1) * DOCS, :],
                sems.at[step, half],
            )
            fetch.start()
            fetches[step].append(fetch)
    fetch_labels.wait()
    cluster = labels[...]
    row = jnp.broadcast_to(cluster.astype(f32), (DOCS, DOCS))
    first, second = iota((DOCS, DOCS), 0), iota((DOCS, DOCS), 1)
    column = jnp.max(jnp.where(first == second, row, f32(-1.0)), axis=1, keepdims=True)
    earlier = (column == row) & (first < second)
    rank = jnp.sum(jnp.where(earlier, f32(1.0), f32(0.0)), axis=0, keepdims=True)
    slot = cluster * RANKS + rank.astype(jnp.int32)
    slot_ref[...] = slot
    local = slot - lax.axis_index("rep") * (PLANES * PAIR * RANKS)
    hit = (first >> 1) == local
    odd = (first & 1) == 1
    zero, one = f32(0.0), f32(1.0)
    chosen = jnp.concatenate(
        [
            jnp.where(hit & jnp.logical_not(odd), one, zero).astype(bf16),
            jnp.where(hit & odd, one, zero).astype(bf16),
        ],
        axis=1,
    )
    live = jnp.dot(chosen, jnp.ones((2 * DOCS, 128), bf16), preferred_element_type=f32) > 0.5
    for step in range(STEPS):
        for fetch in fetches[step]:
            fetch.wait()
        merged = jnp.dot(chosen, docs[step], preferred_element_type=f32)
        at = (step % 2) * STRIP
        if at == 0:
            marked = jnp.where(live, merged[:, :128], jnp.nan)
            merged = jnp.concatenate([marked, merged[:, 128:]], axis=1)
        out_ref[:, step // 2, :, at : at + STRIP] = merged.astype(bf16).reshape(PLANES, 16, STRIP)


def multiply(left, right):
    return lax.dot_general(left, right, (((1,), (1,)), ((), ())), preferred_element_type=f32)


def gather_slots(rows_ref, slots_ref, vacant_ref):
    row = iota((CHUNK, CHUNK), 0)
    half, lane, rank, plane = row >> 7, (row >> 5) & 3, (row >> 3) & 3, row & 7
    source = (plane * LANES + lane) * (2 * RANKS) + rank * 2 + half
    pick = jnp.where(iota((CHUNK, CHUNK), 1) == source, f32(1.0), f32(0.0)).astype(bf16)
    for chunk in range(ROWS // CHUNK):
        span = slice(chunk * CHUNK, (chunk + 1) * CHUNK)
        marked = rows_ref[span, :128].astype(f32)
        empty = marked != marked
        clean = jnp.where(empty, f32(0.0), marked).astype(bf16)
        flags = jnp.where(empty, f32(1.0), f32(0.0)).astype(bf16)
        rows = jnp.concatenate([clean, rows_ref[span, 128:], flags], axis=1)
        picked = jnp.dot(pick, rows, preferred_element_type=f32)
        slots = picked[:, :HALF].astype(bf16)
        for lane in range(LANES):
            top = lane * LOCAL + chunk * 32
            slots_ref[top : top + 32, :HALF] = slots[lane * 32 : (lane + 1) * 32]
            slots_ref[top : top + 32, HALF:] = slots[128 + lane * 32 : 128 + (lane + 1) * 32]
            vacant_ref[top : top + 32, :] = picked[lane * 32 : (lane + 1) * 32, HALF:]


def flagged_block(block, vacant):
    eye = iota((128, 128), 0) == iota((128, 128), 1)
    flagged = jnp.where(eye & (vacant > 0.5), jnp.nan, block)
    return flagged, jnp.sum(jnp.where(eye, flagged, f32(0.0)), axis=0, keepdims=True)


def own_kernel(rows_ref, out_ref, slots_ref, vacant_ref):
    gather_slots(rows_ref, slots_ref, vacant_ref)
    slots = slots_ref[...]
    products = multiply(slots, slots)
    for b in range(2):
        span = slice(b * 128, (b + 1) * 128)
        block, squares = flagged_block(products[span, span], vacant_ref[span, :])
        for lane in range(LANES):
            rows = slice(lane * LOCAL, (lane + 1) * LOCAL)
            inside = slice((lane % 2) * LOCAL, (lane % 2 + 1) * LOCAL)
            tile = block[inside] if lane // 2 == b else products[rows, span]
            out_ref[lane, b * LOCAL : (b + 1) * LOCAL, :] = tile
            out_ref[lane, 4 * LOCAL + b : 4 * LOCAL + b + 1, :] = squares
    for lane in range(LANES):
        out_ref[lane, 4 * LOCAL + 4 :, :] = jnp.zeros((4, 128), f32)


def cross_kernel(part_ref, own_ref, rows_ref, out_ref, other_ref, vacant_ref):
    gather_slots(rows_ref, other_ref, vacant_ref)
    other = other_ref[...]
    products = multiply(jnp.concatenate([own_ref[...], other], axis=0), other)
    for lane in range(LANES):
        rows = slice(lane * LOCAL, (lane + 1) * LOCAL)
        own_rows = slice(0, 2 * LOCAL)
        out_ref[lane, own_rows, :] = part_ref[lane, own_rows, :]
        out_ref[lane, 2 * LOCAL : 3 * LOCAL, :] = products[rows, :128]
        out_ref[lane, 3 * LOCAL : 4 * LOCAL, :] = products[rows, 128:]
        out_ref[lane, 4 * LOCAL :, :] = part_ref[lane, 4 * LOCAL :, :]
    for b in range(2):
        span = slice(b * 128, (b + 1) * 128)
        below = products[SLOTS + b * 128 : SLOTS + (b + 1) * 128, span]
        squares = flagged_block(below, vacant_ref[span, :])[1]
        for lane in range(LANES):
            out_ref[lane, 4 * LOCAL + 2 + b : 4 * LOCAL + 3 + b, :] = squares


def best_kernel(parts_ref, out_ref):
    row, column = iota((LOCAL, 128), 0), iota((LOCAL, 128), 1)
    spot = column & 7
    rank = (row >> 3) & 3
    spread = jnp.zeros((LOCAL, 128), f32)

    def scale(squares):
        return jnp.where(squares == squares, lax.rsqrt(squares + epsilon), f32(-1.0))

    for cluster in range(PAIR):
        total = parts_ref[cluster] + parts_ref[PAIR + cluster]
        tiles = [total[t * LOCAL : (t + 1) * LOCAL] for t in range(4)]
        mates = [scale(total[4 * LOCAL + t : 4 * LOCAL + t + 1]) for t in range(4)]
        same = [column + t * 128 == row + lax.axis_index("x") * LOCAL for t in range(2)]
        squares = jnp.where(same[0], tiles[0], f32(0.0)) + jnp.where(same[1], tiles[1], f32(0.0))
        own = scale(jnp.sum(squares, axis=1, keepdims=True))
        best = jnp.full((LOCAL, 128), -1.0, f32)
        for t in range(4):
            cosine = tiles[t] * own * mates[t]
            allowed = (own >= 0.0) & (mates[t] >= 0.0)
            if t < 2:
                allowed = allowed & jnp.logical_not(same[t])
            best = jnp.maximum(best, jnp.where(allowed, cosine, f32(-1.0)))
        best = jnp.max(best, axis=1, keepdims=True)
        spread = jnp.where(spot == cluster * RANKS + rank, best, spread)
    planes = []
    for top in range(0, LOCAL, 32):
        tiles = [spread[top + k * 8 : top + (k + 1) * 8] for k in range(RANKS)]
        planes.append((tiles[0] + tiles[1]) + (tiles[2] + tiles[3]))
    turned = jnp.concatenate(planes, axis=0)
    for rep in range(REPS):
        out_ref[rep * PLANES : (rep + 1) * PLANES, :] = turned


def collect_kernel(slot_ref, best_ref, out_ref):
    slot = slot_ref[...]
    best = best_ref[...]
    high = best.astype(bf16).astype(f32)
    middle = (best - high).astype(bf16).astype(f32)
    low = best - high - middle
    group = iota((REPS * PLANES, 128), 1) >> 3
    pieces = jnp.where(group == 0, high, jnp.where(group == 1, middle, low))
    pieces = jnp.where(group < 3, pieces, f32(0.0)).astype(bf16)
    chosen = (iota((128, DOCS), 0) & 7) == (slot & 7)
    chosen = jnp.where(chosen, f32(1.0), f32(0.0)).astype(bf16)
    values = jnp.dot(pieces, chosen, preferred_element_type=f32)
    line = iota((REPS * PLANES, DOCS), 0) == (slot >> 3)
    out_ref[...] = jnp.sum(jnp.where(line, values, f32(0.0)), axis=0, keepdims=True)


VMEM = pl.BlockSpec(memory_space=pltpu.VMEM)
HBM = pl.BlockSpec(memory_space=pltpu.HBM)
PARAMS = pltpu.CompilerParams(vmem_limit_bytes=32 * 1024 * 1024)


def on_device(embeddings, cluster_of):
    labels = pltpu.with_memory_space_constraint(cluster_of.reshape(1, DOCS), pltpu.HBM)
    outgoing, slot = pl.pallas_call(
        dispatch_kernel,
        in_specs=[HBM, HBM],
        out_specs=[VMEM, VMEM],
        out_shape=[
            jax.ShapeDtypeStruct((PLANES, PARTS, 16, HALF), bf16),
            jax.ShapeDtypeStruct((1, DOCS), jnp.int32),
        ],
        scratch_shapes=[
            pltpu.VMEM((1, DOCS), jnp.int32),
            pltpu.VMEM((STEPS, 2 * DOCS, STRIP), bf16),
            pltpu.SemaphoreType.DMA,
            pltpu.SemaphoreType.DMA((STEPS, 2)),
        ],
        compiler_params=PARAMS,
        name="dispatch",
    )(labels, pltpu.with_memory_space_constraint(embeddings, pltpu.HBM))
    own_rows = lax.all_to_all(
        outgoing.reshape(SOURCES, 2 * RANKS, HALF), ("z", "x"), 0, 0, tiled=True
    ).reshape(ROWS, HALF)
    other_rows = lax.ppermute(own_rows, "core", [(0, 1), (1, 0)])
    part, slots = pl.pallas_call(
        own_kernel,
        in_specs=[VMEM],
        out_specs=[VMEM, VMEM],
        out_shape=[
            jax.ShapeDtypeStruct((LANES, BLOCK, 128), f32),
            jax.ShapeDtypeStruct((SLOTS, SHARE), bf16),
        ],
        scratch_shapes=[pltpu.VMEM((SLOTS, 128), f32)],
        compiler_params=PARAMS,
        cost_estimate=pl.CostEstimate(
            flops=2 * SLOTS * SLOTS * SHARE * 2, bytes_accessed=2**22, transcendentals=0
        ),
        name="own",
    )(own_rows)
    products = pl.pallas_call(
        cross_kernel,
        in_specs=[VMEM, VMEM, VMEM],
        out_specs=VMEM,
        out_shape=jax.ShapeDtypeStruct((LANES, BLOCK, 128), f32),
        scratch_shapes=[pltpu.VMEM((SLOTS, SHARE), bf16), pltpu.VMEM((SLOTS, 128), f32)],
        compiler_params=PARAMS,
        name="cross",
    )(part, slots, other_rows)
    products = lax.all_to_all(products, "x", 0, 0, tiled=True)
    best = pl.pallas_call(
        best_kernel,
        in_specs=[VMEM],
        out_specs=VMEM,
        out_shape=jax.ShapeDtypeStruct((REPS * PLANES, 128), f32),
        compiler_params=PARAMS,
        name="best",
    )(products)
    returned = lax.all_to_all(
        best.reshape(REPS * PLANES, 1, 128), ("rep", "z"), 0, 0, tiled=True
    ).reshape(REPS * PLANES, 128)
    out = pl.pallas_call(
        collect_kernel,
        in_specs=[VMEM, VMEM],
        out_specs=VMEM,
        out_shape=jax.ShapeDtypeStruct((1, DOCS), f32),
        compiler_params=PARAMS,
        name="collect",
    )(slot, returned)
    return out.reshape(DOCS)


def solution(mesh):
    fine = Mesh(mesh.devices.reshape(PLANES, LANES, 2, REPS), ("z", "x", "core", "rep"))
    shard = ("z", "x", "core")
    return jax.shard_map(
        on_device,
        mesh=fine,
        in_specs=(P(shard, None), P(shard)),
        out_specs=P(shard),
        check_vma=False,
    )
```

```python
import jax
import jax.numpy as jnp
from jax import lax
from jax.experimental import pallas as pl
from jax.experimental.pallas import tpu as pltpu
from jax.sharding import Mesh
from jax.sharding import PartitionSpec as P

PLANES = 16
LANES = 4
PARTS = 2
PAIR = 2
REPS = 4
RANKS = 4
DOCS = 256
WIDTH = 4096
SHARE = WIDTH // PARTS
HALF = SHARE // 2
SOURCES = PLANES * LANES
SLOTS = SOURCES * RANKS
ROWS = SLOTS * 2
CHUNK = 256
LOCAL = SLOTS // LANES
BLOCK = 4 * LOCAL + 8
STRIP = HALF // 2
STEPS = PARTS * 2

epsilon = 1e-06
f32 = jnp.float32
bf16 = jnp.bfloat16


def iota(shape, dim):
    return lax.broadcasted_iota(jnp.int32, shape, dim)


def dispatch_kernel(
    cluster_ref, docs_ref, out_ref, slot_ref, labels, docs, label_sem, sems
):
    fetch_labels = pltpu.make_async_copy(cluster_ref, labels, label_sem)
    fetch_labels.start()

    def fetch(step):
        copies = []
        for half in range(2):
            at = (step // 2) * SHARE + half * HALF + (step % 2) * STRIP
            copy = pltpu.make_async_copy(
                docs_ref.at[:, at : at + STRIP],
                docs.at[step, half * DOCS : (half + 1) * DOCS, :],
                sems.at[step, half],
            )
            copy.start()
            copies.append(copy)
        return copies

    fetches = [fetch(step) for step in range(STEPS // 2)]
    fetch_labels.wait()
    fetches += [fetch(step) for step in range(STEPS // 2, STEPS)]
    cluster = labels[...]
    row = jnp.broadcast_to(cluster.astype(f32), (DOCS, DOCS))
    first, second = iota((DOCS, DOCS), 0), iota((DOCS, DOCS), 1)
    column = jnp.max(jnp.where(first == second, row, f32(-1.0)), axis=1, keepdims=True)
    earlier = (column == row) & (first < second)
    rank = jnp.sum(jnp.where(earlier, f32(1.0), f32(0.0)), axis=0, keepdims=True)
    slot = cluster * RANKS + rank.astype(jnp.int32)
    slot_ref[...] = slot
    local = slot - lax.axis_index("rep") * (PLANES * PAIR * RANKS)
    hit = (first >> 1) == local
    odd = (first & 1) == 1
    zero, one = f32(0.0), f32(1.0)
    chosen = jnp.concatenate(
        [
            jnp.where(hit & jnp.logical_not(odd), one, zero).astype(bf16),
            jnp.where(hit & odd, one, zero).astype(bf16),
        ],
        axis=1,
    )
    live = jnp.dot(chosen, jnp.ones((2 * DOCS, 128), bf16), preferred_element_type=f32) > 0.5
    for step in range(STEPS):
        for copy in fetches[step]:
            copy.wait()
        merged = jnp.dot(chosen, docs[step], preferred_element_type=f32)
        at = (step % 2) * STRIP
        if at == 0:
            marked = jnp.where(live, merged[:, :128], jnp.nan)
            merged = jnp.concatenate([marked, merged[:, 128:]], axis=1)
        out_ref[:, step // 2, :, at : at + STRIP] = merged.astype(bf16).reshape(PLANES, 16, STRIP)


def multiply(left, right):
    return lax.dot_general(left, right, (((1,), (1,)), ((), ())), preferred_element_type=f32)


def gather_slots(rows_ref, slots_ref, vacant_ref):
    row = iota((CHUNK, CHUNK), 0)
    half, lane, rank, plane = row >> 7, (row >> 5) & 3, (row >> 3) & 3, row & 7
    source = (plane * LANES + lane) * (2 * RANKS) + rank * 2 + half
    pick = jnp.where(iota((CHUNK, CHUNK), 1) == source, f32(1.0), f32(0.0)).astype(bf16)
    for chunk in range(ROWS // CHUNK):
        span = slice(chunk * CHUNK, (chunk + 1) * CHUNK)
        marked = rows_ref[span, :128].astype(f32)
        empty = marked != marked
        clean = jnp.where(empty, f32(0.0), marked).astype(bf16)
        flags = jnp.where(empty, f32(1.0), f32(0.0)).astype(bf16)
        rows = jnp.concatenate([clean, rows_ref[span, 128:], flags], axis=1)
        picked = jnp.dot(pick, rows, preferred_element_type=f32)
        slots = picked[:, :HALF].astype(bf16)
        for lane in range(LANES):
            top = lane * LOCAL + chunk * 32
            slots_ref[top : top + 32, :HALF] = slots[lane * 32 : (lane + 1) * 32]
            slots_ref[top : top + 32, HALF:] = slots[128 + lane * 32 : 128 + (lane + 1) * 32]
            vacant_ref[top : top + 32, :] = picked[lane * 32 : (lane + 1) * 32, HALF:]


def flagged_block(block, vacant):
    eye = iota((128, 128), 0) == iota((128, 128), 1)
    flagged = jnp.where(eye & (vacant > 0.5), jnp.nan, block)
    return flagged, jnp.sum(jnp.where(eye, flagged, f32(0.0)), axis=0, keepdims=True)


def own_kernel(rows_ref, out_ref, slots_ref, vacant_ref):
    gather_slots(rows_ref, slots_ref, vacant_ref)
    slots = slots_ref[...]
    products = multiply(slots, slots)
    for b in range(2):
        span = slice(b * 128, (b + 1) * 128)
        block, squares = flagged_block(products[span, span], vacant_ref[span, :])
        for lane in range(LANES):
            rows = slice(lane * LOCAL, (lane + 1) * LOCAL)
            inside = slice((lane % 2) * LOCAL, (lane % 2 + 1) * LOCAL)
            tile = block[inside] if lane // 2 == b else products[rows, span]
            out_ref[lane, b * LOCAL : (b + 1) * LOCAL, :] = tile
            out_ref[lane, 4 * LOCAL + b : 4 * LOCAL + b + 1, :] = squares
    for lane in range(LANES):
        out_ref[lane, 4 * LOCAL + 4 :, :] = jnp.zeros((4, 128), f32)


def cross_kernel(part_ref, own_ref, rows_ref, out_ref, other_ref, vacant_ref):
    gather_slots(rows_ref, other_ref, vacant_ref)
    other = other_ref[...]
    products = multiply(jnp.concatenate([own_ref[...], other], axis=0), other)
    for lane in range(LANES):
        rows = slice(lane * LOCAL, (lane + 1) * LOCAL)
        own_rows = slice(0, 2 * LOCAL)
        out_ref[lane, own_rows, :] = part_ref[lane, own_rows, :]
        out_ref[lane, 2 * LOCAL : 3 * LOCAL, :] = products[rows, :128]
        out_ref[lane, 3 * LOCAL : 4 * LOCAL, :] = products[rows, 128:]
        out_ref[lane, 4 * LOCAL :, :] = part_ref[lane, 4 * LOCAL :, :]
    for b in range(2):
        span = slice(b * 128, (b + 1) * 128)
        below = products[SLOTS + b * 128 : SLOTS + (b + 1) * 128, span]
        squares = flagged_block(below, vacant_ref[span, :])[1]
        for lane in range(LANES):
            out_ref[lane, 4 * LOCAL + 2 + b : 4 * LOCAL + 3 + b, :] = squares


def best_kernel(parts_ref, out_ref):
    row, column = iota((LOCAL, 128), 0), iota((LOCAL, 128), 1)
    spot = column & 7
    rank = (row >> 3) & 3
    spread = jnp.zeros((LOCAL, 128), f32)

    def scale(squares):
        return jnp.where(squares == squares, lax.rsqrt(squares + epsilon), f32(-1.0))

    for cluster in range(PAIR):
        total = parts_ref[cluster] + parts_ref[PAIR + cluster]
        tiles = [total[t * LOCAL : (t + 1) * LOCAL] for t in range(4)]
        mates = [scale(total[4 * LOCAL + t : 4 * LOCAL + t + 1]) for t in range(4)]
        same = [column + t * 128 == row + lax.axis_index("x") * LOCAL for t in range(2)]
        squares = jnp.where(same[0], tiles[0], f32(0.0)) + jnp.where(same[1], tiles[1], f32(0.0))
        own = scale(jnp.sum(squares, axis=1, keepdims=True))
        best = jnp.full((LOCAL, 128), -1.0, f32)
        for t in range(4):
            cosine = tiles[t] * own * mates[t]
            allowed = (own >= 0.0) & (mates[t] >= 0.0)
            if t < 2:
                allowed = allowed & jnp.logical_not(same[t])
            best = jnp.maximum(best, jnp.where(allowed, cosine, f32(-1.0)))
        best = jnp.max(best, axis=1, keepdims=True)
        spread = jnp.where(spot == cluster * RANKS + rank, best, spread)
    planes = []
    for top in range(0, LOCAL, 32):
        tiles = [spread[top + k * 8 : top + (k + 1) * 8] for k in range(RANKS)]
        planes.append((tiles[0] + tiles[1]) + (tiles[2] + tiles[3]))
    turned = jnp.concatenate(planes, axis=0)
    for rep in range(REPS):
        out_ref[rep * PLANES : (rep + 1) * PLANES, :] = turned


def collect_kernel(slot_ref, best_ref, out_ref):
    slot = slot_ref[...]
    best = best_ref[...]
    high = best.astype(bf16).astype(f32)
    middle = (best - high).astype(bf16).astype(f32)
    low = best - high - middle
    group = iota((REPS * PLANES, 128), 1) >> 3
    pieces = jnp.where(group == 0, high, jnp.where(group == 1, middle, low))
    pieces = jnp.where(group < 3, pieces, f32(0.0)).astype(bf16)
    chosen = (iota((128, DOCS), 0) & 7) == (slot & 7)
    chosen = jnp.where(chosen, f32(1.0), f32(0.0)).astype(bf16)
    values = jnp.dot(pieces, chosen, preferred_element_type=f32)
    line = iota((REPS * PLANES, DOCS), 0) == (slot >> 3)
    out_ref[...] = jnp.sum(jnp.where(line, values, f32(0.0)), axis=0, keepdims=True)


VMEM = pl.BlockSpec(memory_space=pltpu.VMEM)
HBM = pl.BlockSpec(memory_space=pltpu.HBM)
PARAMS = pltpu.CompilerParams(vmem_limit_bytes=32 * 1024 * 1024)


def on_device(embeddings, cluster_of):
    labels = pltpu.with_memory_space_constraint(cluster_of.reshape(1, DOCS), pltpu.HBM)
    outgoing, slot = pl.pallas_call(
        dispatch_kernel,
        in_specs=[HBM, HBM],
        out_specs=[VMEM, VMEM],
        out_shape=[
            jax.ShapeDtypeStruct((PLANES, PARTS, 16, HALF), bf16),
            jax.ShapeDtypeStruct((1, DOCS), jnp.int32),
        ],
        scratch_shapes=[
            pltpu.VMEM((1, DOCS), jnp.int32),
            pltpu.VMEM((STEPS, 2 * DOCS, STRIP), bf16),
            pltpu.SemaphoreType.DMA,
            pltpu.SemaphoreType.DMA((STEPS, 2)),
        ],
        compiler_params=PARAMS,
        name="dispatch",
    )(labels, pltpu.with_memory_space_constraint(embeddings, pltpu.HBM))
    own_rows = lax.all_to_all(
        outgoing.reshape(SOURCES, 2 * RANKS, HALF), ("z", "x"), 0, 0, tiled=True
    ).reshape(ROWS, HALF)
    other_rows = lax.ppermute(own_rows, "core", [(0, 1), (1, 0)])
    part, slots = pl.pallas_call(
        own_kernel,
        in_specs=[VMEM],
        out_specs=[VMEM, VMEM],
        out_shape=[
            jax.ShapeDtypeStruct((LANES, BLOCK, 128), f32),
            jax.ShapeDtypeStruct((SLOTS, SHARE), bf16),
        ],
        scratch_shapes=[pltpu.VMEM((SLOTS, 128), f32)],
        compiler_params=PARAMS,
        cost_estimate=pl.CostEstimate(
            flops=2 * SLOTS * SLOTS * SHARE * 2, bytes_accessed=2**22, transcendentals=0
        ),
        name="own",
    )(own_rows)
    products = pl.pallas_call(
        cross_kernel,
        in_specs=[VMEM, VMEM, VMEM],
        out_specs=VMEM,
        out_shape=jax.ShapeDtypeStruct((LANES, BLOCK, 128), f32),
        scratch_shapes=[pltpu.VMEM((SLOTS, SHARE), bf16), pltpu.VMEM((SLOTS, 128), f32)],
        compiler_params=PARAMS,
        name="cross",
    )(part, slots, other_rows)
    products = lax.all_to_all(products, "x", 0, 0, tiled=True)
    best = pl.pallas_call(
        best_kernel,
        in_specs=[VMEM],
        out_specs=VMEM,
        out_shape=jax.ShapeDtypeStruct((REPS * PLANES, 128), f32),
        compiler_params=PARAMS,
        name="best",
    )(products)
    returned = lax.all_to_all(
        best.reshape(REPS * PLANES, 1, 128), ("rep", "z"), 0, 0, tiled=True
    ).reshape(REPS * PLANES, 128)
    out = pl.pallas_call(
        collect_kernel,
        in_specs=[VMEM, VMEM],
        out_specs=VMEM,
        out_shape=jax.ShapeDtypeStruct((1, DOCS), f32),
        compiler_params=PARAMS,
        name="collect",
    )(slot, returned)
    return out.reshape(DOCS)


def solution(mesh):
    fine = Mesh(mesh.devices.reshape(PLANES, LANES, 2, REPS), ("z", "x", "core", "rep"))
    shard = ("z", "x", "core")
    return jax.shard_map(
        on_device,
        mesh=fine,
        in_specs=(P(shard, None), P(shard)),
        out_specs=P(shard),
        check_vma=False,
    )
```

```python
import jax
import jax.numpy as jnp
from jax import lax
from jax.experimental import pallas as pl
from jax.experimental.pallas import tpu as pltpu
from jax.sharding import Mesh
from jax.sharding import PartitionSpec as P

PLANES = 16
LANES = 4
PARTS = 2
PAIR = 2
REPS = 4
RANKS = 4
DOCS = 256
WIDTH = 4096
SHARE = WIDTH // PARTS
HALF = SHARE // 2
SOURCES = PLANES * LANES
SLOTS = SOURCES * RANKS
ROWS = SLOTS * 2
CHUNK = 256
LOCAL = SLOTS // LANES
BLOCK = 4 * LOCAL + 8

epsilon = 1e-06
f32 = jnp.float32
bf16 = jnp.bfloat16


def iota(shape, dim):
    return lax.broadcasted_iota(jnp.int32, shape, dim)


def dispatch_kernel(
    cluster_ref, docs_ref, out_ref, slot_ref, labels, docs, label_sem, sems
):
    fetch_labels = pltpu.make_async_copy(cluster_ref, labels, label_sem)
    fetch_labels.start()

    fetches = []
    for part in range(PARTS):
        columns = slice(part * SHARE, (part + 1) * SHARE)
        fetch = pltpu.make_async_copy(docs_ref.at[:, columns], docs.at[part], sems.at[part])
        fetch.start()
        fetches.append(fetch)
    fetch_labels.wait()
    cluster = labels[...]
    row = jnp.broadcast_to(cluster.astype(f32), (DOCS, DOCS))
    first, second = iota((DOCS, DOCS), 0), iota((DOCS, DOCS), 1)
    column = jnp.max(jnp.where(first == second, row, f32(-1.0)), axis=1, keepdims=True)
    earlier = (column == row) & (first < second)
    rank = jnp.sum(jnp.where(earlier, f32(1.0), f32(0.0)), axis=0, keepdims=True)
    slot = cluster * RANKS + rank.astype(jnp.int32)
    slot_ref[...] = slot
    local = slot - lax.axis_index("rep") * (PLANES * PAIR * RANKS)
    hit = (first >> 1) == local
    odd = (first & 1) == 1
    zero, one = f32(0.0), f32(1.0)
    even = jnp.where(hit & jnp.logical_not(odd), one, zero).astype(bf16)
    uneven = jnp.where(hit & odd, one, zero).astype(bf16)
    ones = jnp.ones((DOCS, 128), bf16)
    live = jnp.dot(even + uneven, ones, preferred_element_type=f32) > 0.5
    for part in range(PARTS):
        fetches[part].wait()
        merged = jnp.dot(even, docs[part, :, :HALF], preferred_element_type=f32)
        merged = merged + jnp.dot(uneven, docs[part, :, HALF:], preferred_element_type=f32)
        marked = jnp.where(live, merged[:, :128], jnp.nan)
        merged = jnp.concatenate([marked, merged[:, 128:]], axis=1)
        out_ref[:, part, :, :] = merged.astype(bf16).reshape(PLANES, 16, HALF)


def multiply(left, right):
    return lax.dot_general(left, right, (((1,), (1,)), ((), ())), preferred_element_type=f32)


def gather_slots(rows_ref, slots_ref, vacant_ref):
    row = iota((CHUNK, CHUNK), 0)
    half, lane, rank, plane = row >> 7, (row >> 5) & 3, (row >> 3) & 3, row & 7
    source = (plane * LANES + lane) * (2 * RANKS) + rank * 2 + half
    pick = jnp.where(iota((CHUNK, CHUNK), 1) == source, f32(1.0), f32(0.0)).astype(bf16)
    for chunk in range(ROWS // CHUNK):
        span = slice(chunk * CHUNK, (chunk + 1) * CHUNK)
        marked = rows_ref[span, :128].astype(f32)
        empty = marked != marked
        clean = jnp.where(empty, f32(0.0), marked).astype(bf16)
        flags = jnp.where(empty, f32(1.0), f32(0.0)).astype(bf16)
        rows = jnp.concatenate([clean, rows_ref[span, 128:], flags], axis=1)
        picked = jnp.dot(pick, rows, preferred_element_type=f32)
        slots = picked[:, :HALF].astype(bf16)
        for lane in range(LANES):
            top = lane * LOCAL + chunk * 32
            slots_ref[top : top + 32, :HALF] = slots[lane * 32 : (lane + 1) * 32]
            slots_ref[top : top + 32, HALF:] = slots[128 + lane * 32 : 128 + (lane + 1) * 32]
            vacant_ref[top : top + 32, :] = picked[lane * 32 : (lane + 1) * 32, HALF:]


def flagged_block(block, vacant):
    eye = iota((128, 128), 0) == iota((128, 128), 1)
    flagged = jnp.where(eye & (vacant > 0.5), jnp.nan, block)
    return flagged, jnp.sum(jnp.where(eye, flagged, f32(0.0)), axis=0, keepdims=True)


def own_kernel(rows_ref, out_ref, slots_ref, vacant_ref):
    gather_slots(rows_ref, slots_ref, vacant_ref)
    slots = slots_ref[...]
    products = multiply(slots, slots)
    for b in range(2):
        span = slice(b * 128, (b + 1) * 128)
        block, squares = flagged_block(products[span, span], vacant_ref[span, :])
        for lane in range(LANES):
            rows = slice(lane * LOCAL, (lane + 1) * LOCAL)
            inside = slice((lane % 2) * LOCAL, (lane % 2 + 1) * LOCAL)
            tile = block[inside] if lane // 2 == b else products[rows, span]
            out_ref[lane, b * LOCAL : (b + 1) * LOCAL, :] = tile
            out_ref[lane, 4 * LOCAL + b : 4 * LOCAL + b + 1, :] = squares
    for lane in range(LANES):
        out_ref[lane, 4 * LOCAL + 4 :, :] = jnp.zeros((4, 128), f32)


def cross_kernel(part_ref, own_ref, rows_ref, out_ref, other_ref, vacant_ref):
    gather_slots(rows_ref, other_ref, vacant_ref)
    other = other_ref[...]
    products = multiply(jnp.concatenate([own_ref[...], other], axis=0), other)
    for lane in range(LANES):
        rows = slice(lane * LOCAL, (lane + 1) * LOCAL)
        own_rows = slice(0, 2 * LOCAL)
        out_ref[lane, own_rows, :] = part_ref[lane, own_rows, :]
        out_ref[lane, 2 * LOCAL : 3 * LOCAL, :] = products[rows, :128]
        out_ref[lane, 3 * LOCAL : 4 * LOCAL, :] = products[rows, 128:]
        out_ref[lane, 4 * LOCAL :, :] = part_ref[lane, 4 * LOCAL :, :]
    for b in range(2):
        span = slice(b * 128, (b + 1) * 128)
        below = products[SLOTS + b * 128 : SLOTS + (b + 1) * 128, span]
        squares = flagged_block(below, vacant_ref[span, :])[1]
        for lane in range(LANES):
            out_ref[lane, 4 * LOCAL + 2 + b : 4 * LOCAL + 3 + b, :] = squares


def best_kernel(parts_ref, out_ref):
    row, column = iota((LOCAL, 128), 0), iota((LOCAL, 128), 1)
    spot = column & 7
    rank = (row >> 3) & 3
    spread = jnp.zeros((LOCAL, 128), f32)

    def scale(squares):
        return jnp.where(squares == squares, lax.rsqrt(squares + epsilon), f32(-1.0))

    for cluster in range(PAIR):
        total = parts_ref[cluster] + parts_ref[PAIR + cluster]
        tiles = [total[t * LOCAL : (t + 1) * LOCAL] for t in range(4)]
        mates = [scale(total[4 * LOCAL + t : 4 * LOCAL + t + 1]) for t in range(4)]
        same = [column + t * 128 == row + lax.axis_index("x") * LOCAL for t in range(2)]
        squares = jnp.where(same[0], tiles[0], f32(0.0)) + jnp.where(same[1], tiles[1], f32(0.0))
        own = scale(jnp.sum(squares, axis=1, keepdims=True))
        best = jnp.full((LOCAL, 128), -1.0, f32)
        for t in range(4):
            cosine = tiles[t] * own * mates[t]
            allowed = (own >= 0.0) & (mates[t] >= 0.0)
            if t < 2:
                allowed = allowed & jnp.logical_not(same[t])
            best = jnp.maximum(best, jnp.where(allowed, cosine, f32(-1.0)))
        best = jnp.max(best, axis=1, keepdims=True)
        spread = jnp.where(spot == cluster * RANKS + rank, best, spread)
    planes = []
    for top in range(0, LOCAL, 32):
        tiles = [spread[top + k * 8 : top + (k + 1) * 8] for k in range(RANKS)]
        planes.append((tiles[0] + tiles[1]) + (tiles[2] + tiles[3]))
    turned = jnp.concatenate(planes, axis=0)
    for rep in range(REPS):
        out_ref[rep * PLANES : (rep + 1) * PLANES, :] = turned


def collect_kernel(slot_ref, best_ref, out_ref):
    slot = slot_ref[...]
    best = best_ref[...]
    high = best.astype(bf16).astype(f32)
    middle = (best - high).astype(bf16).astype(f32)
    low = best - high - middle
    group = iota((REPS * PLANES, 128), 1) >> 3
    pieces = jnp.where(group == 0, high, jnp.where(group == 1, middle, low))
    pieces = jnp.where(group < 3, pieces, f32(0.0)).astype(bf16)
    chosen = (iota((128, DOCS), 0) & 7) == (slot & 7)
    chosen = jnp.where(chosen, f32(1.0), f32(0.0)).astype(bf16)
    values = jnp.dot(pieces, chosen, preferred_element_type=f32)
    line = iota((REPS * PLANES, DOCS), 0) == (slot >> 3)
    out_ref[...] = jnp.sum(jnp.where(line, values, f32(0.0)), axis=0, keepdims=True)


VMEM = pl.BlockSpec(memory_space=pltpu.VMEM)
HBM = pl.BlockSpec(memory_space=pltpu.HBM)
PARAMS = pltpu.CompilerParams(vmem_limit_bytes=32 * 1024 * 1024)


def on_device(embeddings, cluster_of):
    labels = pltpu.with_memory_space_constraint(cluster_of.reshape(1, DOCS), pltpu.HBM)
    outgoing, slot = pl.pallas_call(
        dispatch_kernel,
        in_specs=[HBM, HBM],
        out_specs=[VMEM, VMEM],
        out_shape=[
            jax.ShapeDtypeStruct((PLANES, PARTS, 16, HALF), bf16),
            jax.ShapeDtypeStruct((1, DOCS), jnp.int32),
        ],
        scratch_shapes=[
            pltpu.VMEM((1, DOCS), jnp.int32),
            pltpu.VMEM((PARTS, DOCS, SHARE), bf16),
            pltpu.SemaphoreType.DMA,
            pltpu.SemaphoreType.DMA((PARTS,)),
        ],
        compiler_params=PARAMS,
        name="dispatch",
    )(labels, pltpu.with_memory_space_constraint(embeddings, pltpu.HBM))
    own_rows = lax.all_to_all(
        outgoing.reshape(SOURCES, 2 * RANKS, HALF), ("z", "x"), 0, 0, tiled=True
    ).reshape(ROWS, HALF)
    other_rows = lax.ppermute(own_rows, "core", [(0, 1), (1, 0)])
    part, slots = pl.pallas_call(
        own_kernel,
        in_specs=[VMEM],
        out_specs=[VMEM, VMEM],
        out_shape=[
            jax.ShapeDtypeStruct((LANES, BLOCK, 128), f32),
            jax.ShapeDtypeStruct((SLOTS, SHARE), bf16),
        ],
        scratch_shapes=[pltpu.VMEM((SLOTS, 128), f32)],
        compiler_params=PARAMS,
        cost_estimate=pl.CostEstimate(
            flops=2 * SLOTS * SLOTS * SHARE * 2, bytes_accessed=2**22, transcendentals=0
        ),
        name="own",
    )(own_rows)
    products = pl.pallas_call(
        cross_kernel,
        in_specs=[VMEM, VMEM, VMEM],
        out_specs=VMEM,
        out_shape=jax.ShapeDtypeStruct((LANES, BLOCK, 128), f32),
        scratch_shapes=[pltpu.VMEM((SLOTS, SHARE), bf16), pltpu.VMEM((SLOTS, 128), f32)],
        compiler_params=PARAMS,
        name="cross",
    )(part, slots, other_rows)
    products = lax.all_to_all(products, "x", 0, 0, tiled=True)
    best = pl.pallas_call(
        best_kernel,
        in_specs=[VMEM],
        out_specs=VMEM,
        out_shape=jax.ShapeDtypeStruct((REPS * PLANES, 128), f32),
        compiler_params=PARAMS,
        name="best",
    )(products)
    returned = lax.all_to_all(
        best.reshape(REPS * PLANES, 1, 128), ("rep", "z"), 0, 0, tiled=True
    ).reshape(REPS * PLANES, 128)
    out = pl.pallas_call(
        collect_kernel,
        in_specs=[VMEM, VMEM],
        out_specs=VMEM,
        out_shape=jax.ShapeDtypeStruct((1, DOCS), f32),
        compiler_params=PARAMS,
        name="collect",
    )(slot, returned)
    return out.reshape(DOCS)


def solution(mesh):
    fine = Mesh(mesh.devices.reshape(PLANES, LANES, 2, REPS), ("z", "x", "core", "rep"))
    shard = ("z", "x", "core")
    return jax.shard_map(
        on_device,
        mesh=fine,
        in_specs=(P(shard, None), P(shard)),
        out_specs=P(shard),
        check_vma=False,
    )
```

```python
import jax
import jax.numpy as jnp
from jax import lax
from jax.experimental import pallas as pl
from jax.experimental.pallas import tpu as pltpu
from jax.sharding import Mesh
from jax.sharding import PartitionSpec as P

PLANES = 16
LANES = 4
PARTS = 2
PAIR = 2
REPS = 4
RANKS = 4
DOCS = 256
WIDTH = 4096
SHARE = WIDTH // PARTS
HALF = SHARE // 2
SOURCES = PLANES * LANES
SLOTS = SOURCES * RANKS
KEPT = SLOTS // 2
ROWS = SLOTS * 2
CHUNK = 256
LOCAL = SLOTS // LANES
BLOCK = 2 * KEPT + 8

RETURNS = REPS * PAIR * PLANES

epsilon = 1e-06
f32 = jnp.float32
bf16 = jnp.bfloat16


def iota(shape, dim):
    return lax.broadcasted_iota(jnp.int32, shape, dim)


def dispatch_kernel(
    cluster_ref, docs_ref, out_ref, slot_ref, labels, docs, label_sem, sems
):
    fetch_labels = pltpu.make_async_copy(cluster_ref, labels, label_sem)
    fetch_labels.start()

    fetches = []
    for part in range(PARTS):
        columns = slice(part * SHARE, (part + 1) * SHARE)
        fetch = pltpu.make_async_copy(docs_ref.at[:, columns], docs.at[part], sems.at[part])
        fetch.start()
        fetches.append(fetch)
    fetch_labels.wait()
    cluster = labels[...]
    row = jnp.broadcast_to(cluster.astype(f32), (DOCS, DOCS))
    first, second = iota((DOCS, DOCS), 0), iota((DOCS, DOCS), 1)
    column = jnp.max(jnp.where(first == second, row, f32(-1.0)), axis=1, keepdims=True)
    earlier = (column == row) & (first < second)
    rank = jnp.sum(jnp.where(earlier, f32(1.0), f32(0.0)), axis=0, keepdims=True)
    slot = cluster * RANKS + rank.astype(jnp.int32)
    slot_ref[...] = slot
    local = slot - lax.axis_index("rep") * (PLANES * PAIR * RANKS)
    hit = (first >> 1) == local
    odd = (first & 1) == 1
    zero, one = f32(0.0), f32(1.0)
    even = jnp.where(hit & jnp.logical_not(odd), one, zero).astype(bf16)
    uneven = jnp.where(hit & odd, one, zero).astype(bf16)
    ones = jnp.ones((DOCS, 128), bf16)
    live = jnp.dot(even + uneven, ones, preferred_element_type=f32) > 0.5
    for part in range(PARTS):
        fetches[part].wait()
        merged = jnp.dot(even, docs[part, :, :HALF], preferred_element_type=f32)
        merged = merged + jnp.dot(uneven, docs[part, :, HALF:], preferred_element_type=f32)
        marked = jnp.where(live, merged[:, :128], jnp.nan)
        merged = jnp.concatenate([marked, merged[:, 128:]], axis=1)
        out_ref[:, part, :, :] = merged.astype(bf16).reshape(PLANES, 16, HALF)


def multiply(left, right):
    return lax.dot_general(left, right, (((1,), (1,)), ((), ())), preferred_element_type=f32)


def gather_slots(rows_ref, slots_ref, vacant_ref):
    row = iota((CHUNK, CHUNK), 0)
    half, lane, rank, plane = row >> 7, (row >> 5) & 3, (row >> 3) & 3, row & 7
    source = (plane * LANES + lane) * (2 * RANKS) + rank * 2 + half
    pick = jnp.where(iota((CHUNK, CHUNK), 1) == source, f32(1.0), f32(0.0)).astype(bf16)
    for chunk in range(ROWS // CHUNK):
        span = slice(chunk * CHUNK, (chunk + 1) * CHUNK)
        marked = rows_ref[span, :128].astype(f32)
        empty = marked != marked
        clean = jnp.where(empty, f32(0.0), marked).astype(bf16)
        flags = jnp.where(empty, f32(1.0), f32(0.0)).astype(bf16)
        rows = jnp.concatenate([clean, rows_ref[span, 128:], flags], axis=1)
        picked = jnp.dot(pick, rows, preferred_element_type=f32)
        slots = picked[:, :HALF].astype(bf16)
        for lane in range(LANES):
            top = lane * LOCAL + chunk * 32
            slots_ref[top : top + 32, :HALF] = slots[lane * 32 : (lane + 1) * 32]
            slots_ref[top : top + 32, HALF:] = slots[128 + lane * 32 : 128 + (lane + 1) * 32]
            vacant_ref[top : top + 32, :] = picked[lane * 32 : (lane + 1) * 32, HALF:]


def flagged_block(block, vacant):
    eye = iota((128, 128), 0) == iota((128, 128), 1)
    flagged = jnp.where(eye & (vacant > 0.5), jnp.nan, block)
    return flagged, jnp.sum(jnp.where(eye, flagged, f32(0.0)), axis=0, keepdims=True)


def split_rows(products_ref, squares, keep_ref, send_ref):
    mine = lax.axis_index("xl")
    for target, ref in ((mine, keep_ref), (1 - mine, send_ref)):
        start = pl.multiple_of(target * KEPT, KEPT)
        for t in range(2):
            tile = products_ref[pl.ds(start, KEPT), t * 128 : (t + 1) * 128]
            ref[t * KEPT : (t + 1) * KEPT, :] = tile
        ref[2 * KEPT :, :] = jnp.concatenate(squares + [jnp.zeros((6, 128), f32)], axis=0)


def own_kernel(rows_ref, keep_ref, send_ref, slots_ref, vacant_ref, products_ref):
    gather_slots(rows_ref, slots_ref, vacant_ref)
    slots = slots_ref[...]
    products_ref[...] = multiply(slots, slots)
    squares = []
    for b in range(2):
        span = slice(b * 128, (b + 1) * 128)
        block, diagonal = flagged_block(products_ref[span, span], vacant_ref[span, :])
        products_ref[span, span] = block
        squares.append(diagonal)
    split_rows(products_ref, squares, keep_ref, send_ref)


def cross_kernel(own_ref, rows_ref, keep_ref, send_ref, other_ref, vacant_ref, products_ref):
    gather_slots(rows_ref, other_ref, vacant_ref)
    other = other_ref[...]
    products_ref[...] = multiply(jnp.concatenate([own_ref[...], other], axis=0), other)
    squares = []
    for b in range(2):
        span = slice(b * 128, (b + 1) * 128)
        below = products_ref[SLOTS + b * 128 : SLOTS + (b + 1) * 128, span]
        squares.append(flagged_block(below, vacant_ref[span, :])[1])
    split_rows(products_ref, squares, keep_ref, send_ref)


def best_kernel(own_keep, own_sent, cross_keep, cross_sent, out_ref):
    row, column = iota((KEPT, 128), 0), iota((KEPT, 128), 1)
    mine = lax.axis_index("xl")

    def scale(squares):
        return jnp.where(squares == squares, lax.rsqrt(squares + epsilon), f32(-1.0))

    tiles, mates = [], []
    for keep, sent in ((own_keep, own_sent), (cross_keep, cross_sent)):
        total = keep[...] + sent[...]
        tiles += [total[t * KEPT : (t + 1) * KEPT] for t in range(2)]
        mates += [scale(total[2 * KEPT + t : 2 * KEPT + t + 1]) for t in range(2)]
    same = [(column == row) & (mine == t) for t in range(2)]
    squares = jnp.where(same[0], tiles[0], f32(0.0)) + jnp.where(same[1], tiles[1], f32(0.0))
    own = scale(jnp.sum(squares, axis=1, keepdims=True))
    best = jnp.full((KEPT, 128), -1.0, f32)
    for t in range(4):
        cosine = tiles[t] * own * mates[t]
        allowed = (own >= 0.0) & (mates[t] >= 0.0)
        if t < 2:
            allowed = allowed & jnp.logical_not(same[t])
        best = jnp.maximum(best, jnp.where(allowed, cosine, f32(-1.0)))
    best = jnp.max(best, axis=1, keepdims=True)
    spread = jnp.where((column & 3) == ((row >> 3) & 3), best, f32(0.0))
    lines = []
    for top in range(0, KEPT, 32):
        parts = [spread[top + k * 8 : top + (k + 1) * 8] for k in range(RANKS)]
        lines.append((parts[0] + parts[1]) + (parts[2] + parts[3]))
    turned = jnp.concatenate(lines, axis=0)
    for rep in range(REPS):
        out_ref[rep * PAIR * PLANES : (rep + 1) * PAIR * PLANES, :] = turned


def collect_kernel(slot_ref, best_ref, out_ref):
    slot = slot_ref[...]
    best = best_ref[...]
    high = best.astype(bf16).astype(f32)
    middle = (best - high).astype(bf16).astype(f32)
    low = best - high - middle
    group = iota((RETURNS, 128), 1) >> 2
    pieces = jnp.where(group == 0, high, jnp.where(group == 1, middle, low))
    pieces = jnp.where(group < 3, pieces, f32(0.0)).astype(bf16)
    chosen = (iota((128, DOCS), 0) & 3) == (slot & 3)
    chosen = jnp.where(chosen, f32(1.0), f32(0.0)).astype(bf16)
    values = jnp.dot(pieces, chosen, preferred_element_type=f32)
    cluster = slot >> 2
    line = (cluster >> 5) * (PAIR * PLANES) + (cluster & 1) * PLANES + ((cluster & 31) >> 1)
    hit = iota((RETURNS, DOCS), 0) == line
    out_ref[...] = jnp.sum(jnp.where(hit, values, f32(0.0)), axis=0, keepdims=True)


VMEM = pl.BlockSpec(memory_space=pltpu.VMEM)
HBM = pl.BlockSpec(memory_space=pltpu.HBM)
PARAMS = pltpu.CompilerParams(vmem_limit_bytes=32 * 1024 * 1024)


def on_device(embeddings, cluster_of):
    labels = pltpu.with_memory_space_constraint(cluster_of.reshape(1, DOCS), pltpu.HBM)
    outgoing, slot = pl.pallas_call(
        dispatch_kernel,
        in_specs=[HBM, HBM],
        out_specs=[VMEM, VMEM],
        out_shape=[
            jax.ShapeDtypeStruct((PLANES, PARTS, 16, HALF), bf16),
            jax.ShapeDtypeStruct((1, DOCS), jnp.int32),
        ],
        scratch_shapes=[
            pltpu.VMEM((1, DOCS), jnp.int32),
            pltpu.VMEM((PARTS, DOCS, SHARE), bf16),
            pltpu.SemaphoreType.DMA,
            pltpu.SemaphoreType.DMA((PARTS,)),
        ],
        compiler_params=PARAMS,
        name="dispatch",
    )(labels, pltpu.with_memory_space_constraint(embeddings, pltpu.HBM))
    own_rows = lax.all_to_all(
        outgoing.reshape(SOURCES, 2 * RANKS, HALF), ("z", "xl", "xh"), 0, 0, tiled=True
    ).reshape(ROWS, HALF)
    swap = [(0, 1), (1, 0)]
    other_rows = lax.ppermute(own_rows, "core", swap)
    half_rows = jax.ShapeDtypeStruct((BLOCK, 128), f32)
    own_keep, own_send, slots = pl.pallas_call(
        own_kernel,
        in_specs=[VMEM],
        out_specs=[VMEM, VMEM, VMEM],
        out_shape=[half_rows, half_rows, jax.ShapeDtypeStruct((SLOTS, SHARE), bf16)],
        scratch_shapes=[pltpu.VMEM((SLOTS, 128), f32), pltpu.VMEM((SLOTS, SLOTS), f32)],
        compiler_params=PARAMS,
        cost_estimate=pl.CostEstimate(
            flops=2 * SLOTS * SLOTS * SHARE * 2, bytes_accessed=2**22, transcendentals=0
        ),
        name="own",
    )(own_rows)
    own_sent = lax.ppermute(own_send, "xl", swap)
    cross_keep, cross_send = pl.pallas_call(
        cross_kernel,
        in_specs=[VMEM, VMEM],
        out_specs=[VMEM, VMEM],
        out_shape=[half_rows, half_rows],
        scratch_shapes=[
            pltpu.VMEM((SLOTS, SHARE), bf16),
            pltpu.VMEM((SLOTS, 128), f32),
            pltpu.VMEM((2 * SLOTS, SLOTS), f32),
        ],
        compiler_params=PARAMS,
        cost_estimate=pl.CostEstimate(
            flops=2 * SLOTS * SLOTS * SHARE * 2, bytes_accessed=2**22, transcendentals=0
        ),
        name="cross",
    )(slots, other_rows)
    cross_sent = lax.ppermute(cross_send, "xl", swap)
    best = pl.pallas_call(
        best_kernel,
        in_specs=[VMEM, VMEM, VMEM, VMEM],
        out_specs=VMEM,
        out_shape=jax.ShapeDtypeStruct((RETURNS, 128), f32),
        compiler_params=PARAMS,
        name="best",
    )(own_keep, own_sent, cross_keep, cross_sent)
    returned = lax.all_to_all(
        best.reshape(RETURNS, 1, 128), ("rep", "xh", "z"), 0, 0, tiled=True
    ).reshape(RETURNS, 128)
    out = pl.pallas_call(
        collect_kernel,
        in_specs=[VMEM, VMEM],
        out_specs=VMEM,
        out_shape=jax.ShapeDtypeStruct((1, DOCS), f32),
        compiler_params=PARAMS,
        name="collect",
    )(slot, returned)
    return out.reshape(DOCS)


def solution(mesh):
    axes = ("z", "xh", "xl", "core", "rep")
    fine = Mesh(mesh.devices.reshape(PLANES, 2, 2, 2, REPS), axes)
    shard = axes[:4]
    return jax.shard_map(
        on_device,
        mesh=fine,
        in_specs=(P(shard, None), P(shard)),
        out_specs=P(shard),
        check_vma=False,
    )
```

```python
import jax
import jax.numpy as jnp
from jax import lax
from jax.experimental import pallas as pl
from jax.experimental.pallas import tpu as pltpu
from jax.sharding import Mesh
from jax.sharding import PartitionSpec as P

PLANES = 16
LANES = 4
PARTS = 2
PAIR = 2
REPS = 4
RANKS = 4
DOCS = 256
WIDTH = 4096
SHARE = WIDTH // PARTS
HALF = SHARE // 2
SOURCES = PLANES * LANES
SLOTS = SOURCES * RANKS
ROWS = SLOTS * 2
CHUNK = 256
LOCAL = SLOTS // LANES
BLOCK = 4 * LOCAL + 8

epsilon = 1e-06
f32 = jnp.float32
bf16 = jnp.bfloat16


def iota(shape, dim):
    return lax.broadcasted_iota(jnp.int32, shape, dim)


def dispatch_kernel(
    cluster_ref, docs_ref, out_ref, slot_ref, labels, docs, label_sem, sems
):
    fetch_labels = pltpu.make_async_copy(cluster_ref, labels, label_sem)
    fetch_labels.start()

    fetches = []
    for part in range(PARTS):
        columns = slice(part * SHARE, (part + 1) * SHARE)
        fetch = pltpu.make_async_copy(docs_ref.at[:, columns], docs.at[part], sems.at[part])
        fetch.start(priority=1)
        fetches.append(fetch)
    fetch_labels.wait()
    cluster = labels[...]
    row = jnp.broadcast_to(cluster.astype(f32), (DOCS, DOCS))
    first, second = iota((DOCS, DOCS), 0), iota((DOCS, DOCS), 1)
    column = jnp.max(jnp.where(first == second, row, f32(-1.0)), axis=1, keepdims=True)
    earlier = (column == row) & (first < second)
    rank = jnp.sum(jnp.where(earlier, f32(1.0), f32(0.0)), axis=0, keepdims=True)
    slot = cluster * RANKS + rank.astype(jnp.int32)
    slot_ref[...] = slot
    local = slot - lax.axis_index("rep") * (PLANES * PAIR * RANKS)
    hit = (first >> 1) == local
    odd = (first & 1) == 1
    zero, one = f32(0.0), f32(1.0)
    even = jnp.where(hit & jnp.logical_not(odd), one, zero).astype(bf16)
    uneven = jnp.where(hit & odd, one, zero).astype(bf16)
    ones = jnp.ones((DOCS, 128), bf16)
    live = jnp.dot(even + uneven, ones, preferred_element_type=f32) > 0.5
    for part in range(PARTS):
        fetches[part].wait()
        merged = jnp.dot(even, docs[part, :, :HALF], preferred_element_type=f32)
        merged = merged + jnp.dot(uneven, docs[part, :, HALF:], preferred_element_type=f32)
        marked = jnp.where(live, merged[:, :128], jnp.nan)
        merged = jnp.concatenate([marked, merged[:, 128:]], axis=1)
        out_ref[:, part, :, :] = merged.astype(bf16).reshape(PLANES, 16, HALF)


def multiply(left, right):
    return lax.dot_general(left, right, (((1,), (1,)), ((), ())), preferred_element_type=f32)


def gather_slots(rows_ref, slots_ref, vacant_ref):
    row = iota((CHUNK, CHUNK), 0)
    half, lane, rank, plane = row >> 7, (row >> 5) & 3, (row >> 3) & 3, row & 7
    source = (plane * LANES + lane) * (2 * RANKS) + rank * 2 + half
    pick = jnp.where(iota((CHUNK, CHUNK), 1) == source, f32(1.0), f32(0.0)).astype(bf16)
    for chunk in range(ROWS // CHUNK):
        span = slice(chunk * CHUNK, (chunk + 1) * CHUNK)
        marked = rows_ref[span, :128].astype(f32)
        empty = marked != marked
        clean = jnp.where(empty, f32(0.0), marked).astype(bf16)
        flags = jnp.where(empty, f32(1.0), f32(0.0)).astype(bf16)
        rows = jnp.concatenate([clean, rows_ref[span, 128:], flags], axis=1)
        picked = jnp.dot(pick, rows, preferred_element_type=f32)
        slots = picked[:, :HALF].astype(bf16)
        for lane in range(LANES):
            top = lane * LOCAL + chunk * 32
            slots_ref[top : top + 32, :HALF] = slots[lane * 32 : (lane + 1) * 32]
            slots_ref[top : top + 32, HALF:] = slots[128 + lane * 32 : 128 + (lane + 1) * 32]
            vacant_ref[top : top + 32, :] = picked[lane * 32 : (lane + 1) * 32, HALF:]


def flagged_block(block, vacant):
    eye = iota((128, 128), 0) == iota((128, 128), 1)
    flagged = jnp.where(eye & (vacant > 0.5), jnp.nan, block)
    return flagged, jnp.sum(jnp.where(eye, flagged, f32(0.0)), axis=0, keepdims=True)


def own_kernel(rows_ref, out_ref, slots_ref, vacant_ref):
    gather_slots(rows_ref, slots_ref, vacant_ref)
    slots = slots_ref[...]
    products = multiply(slots, slots)
    for b in range(2):
        span = slice(b * 128, (b + 1) * 128)
        block, squares = flagged_block(products[span, span], vacant_ref[span, :])
        for lane in range(LANES):
            rows = slice(lane * LOCAL, (lane + 1) * LOCAL)
            inside = slice((lane % 2) * LOCAL, (lane % 2 + 1) * LOCAL)
            tile = block[inside] if lane // 2 == b else products[rows, span]
            out_ref[lane, b * LOCAL : (b + 1) * LOCAL, :] = tile
            out_ref[lane, 4 * LOCAL + b : 4 * LOCAL + b + 1, :] = squares
    for lane in range(LANES):
        out_ref[lane, 4 * LOCAL + 4 :, :] = jnp.zeros((4, 128), f32)


def cross_kernel(part_ref, own_ref, rows_ref, out_ref, other_ref, vacant_ref):
    gather_slots(rows_ref, other_ref, vacant_ref)
    other = other_ref[...]
    products = multiply(jnp.concatenate([own_ref[...], other], axis=0), other)
    for lane in range(LANES):
        rows = slice(lane * LOCAL, (lane + 1) * LOCAL)
        own_rows = slice(0, 2 * LOCAL)
        out_ref[lane, own_rows, :] = part_ref[lane, own_rows, :]
        out_ref[lane, 2 * LOCAL : 3 * LOCAL, :] = products[rows, :128]
        out_ref[lane, 3 * LOCAL : 4 * LOCAL, :] = products[rows, 128:]
        out_ref[lane, 4 * LOCAL :, :] = part_ref[lane, 4 * LOCAL :, :]
    for b in range(2):
        span = slice(b * 128, (b + 1) * 128)
        below = products[SLOTS + b * 128 : SLOTS + (b + 1) * 128, span]
        squares = flagged_block(below, vacant_ref[span, :])[1]
        for lane in range(LANES):
            out_ref[lane, 4 * LOCAL + 2 + b : 4 * LOCAL + 3 + b, :] = squares


def best_kernel(parts_ref, out_ref):
    row, column = iota((LOCAL, 128), 0), iota((LOCAL, 128), 1)
    spot = column & 7
    rank = (row >> 3) & 3
    spread = jnp.zeros((LOCAL, 128), f32)

    def scale(squares):
        return jnp.where(squares == squares, lax.rsqrt(squares + epsilon), f32(-1.0))

    for cluster in range(PAIR):
        total = parts_ref[cluster] + parts_ref[PAIR + cluster]
        tiles = [total[t * LOCAL : (t + 1) * LOCAL] for t in range(4)]
        mates = [scale(total[4 * LOCAL + t : 4 * LOCAL + t + 1]) for t in range(4)]
        same = [column + t * 128 == row + lax.axis_index("x") * LOCAL for t in range(2)]
        squares = jnp.where(same[0], tiles[0], f32(0.0)) + jnp.where(same[1], tiles[1], f32(0.0))
        own = scale(jnp.sum(squares, axis=1, keepdims=True))
        best = jnp.full((LOCAL, 128), -1.0, f32)
        for t in range(4):
            cosine = tiles[t] * own * mates[t]
            allowed = (own >= 0.0) & (mates[t] >= 0.0)
            if t < 2:
                allowed = allowed & jnp.logical_not(same[t])
            best = jnp.maximum(best, jnp.where(allowed, cosine, f32(-1.0)))
        best = jnp.max(best, axis=1, keepdims=True)
        spread = jnp.where(spot == cluster * RANKS + rank, best, spread)
    planes = []
    for top in range(0, LOCAL, 32):
        tiles = [spread[top + k * 8 : top + (k + 1) * 8] for k in range(RANKS)]
        planes.append((tiles[0] + tiles[1]) + (tiles[2] + tiles[3]))
    turned = jnp.concatenate(planes, axis=0)
    for rep in range(REPS):
        out_ref[rep * PLANES : (rep + 1) * PLANES, :] = turned


def collect_kernel(slot_ref, best_ref, out_ref):
    slot = slot_ref[...]
    best = best_ref[...]
    high = best.astype(bf16).astype(f32)
    middle = (best - high).astype(bf16).astype(f32)
    low = best - high - middle
    group = iota((REPS * PLANES, 128), 1) >> 3
    pieces = jnp.where(group == 0, high, jnp.where(group == 1, middle, low))
    pieces = jnp.where(group < 3, pieces, f32(0.0)).astype(bf16)
    chosen = (iota((128, DOCS), 0) & 7) == (slot & 7)
    chosen = jnp.where(chosen, f32(1.0), f32(0.0)).astype(bf16)
    values = jnp.dot(pieces, chosen, preferred_element_type=f32)
    line = iota((REPS * PLANES, DOCS), 0) == (slot >> 3)
    out_ref[...] = jnp.sum(jnp.where(line, values, f32(0.0)), axis=0, keepdims=True)


VMEM = pl.BlockSpec(memory_space=pltpu.VMEM)
HBM = pl.BlockSpec(memory_space=pltpu.HBM)
PARAMS = pltpu.CompilerParams(vmem_limit_bytes=32 * 1024 * 1024)


def on_device(embeddings, cluster_of):
    labels = pltpu.with_memory_space_constraint(cluster_of.reshape(1, DOCS), pltpu.HBM)
    outgoing, slot = pl.pallas_call(
        dispatch_kernel,
        in_specs=[HBM, HBM],
        out_specs=[VMEM, VMEM],
        out_shape=[
            jax.ShapeDtypeStruct((PLANES, PARTS, 16, HALF), bf16),
            jax.ShapeDtypeStruct((1, DOCS), jnp.int32),
        ],
        scratch_shapes=[
            pltpu.VMEM((1, DOCS), jnp.int32),
            pltpu.VMEM((PARTS, DOCS, SHARE), bf16),
            pltpu.SemaphoreType.DMA,
            pltpu.SemaphoreType.DMA((PARTS,)),
        ],
        compiler_params=PARAMS,
        name="dispatch",
    )(labels, pltpu.with_memory_space_constraint(embeddings, pltpu.HBM))
    own_rows = lax.all_to_all(
        outgoing.reshape(SOURCES, 2 * RANKS, HALF), ("z", "x"), 0, 0, tiled=True
    ).reshape(ROWS, HALF)
    other_rows = lax.ppermute(own_rows, "core", [(0, 1), (1, 0)])
    part, slots = pl.pallas_call(
        own_kernel,
        in_specs=[VMEM],
        out_specs=[VMEM, VMEM],
        out_shape=[
            jax.ShapeDtypeStruct((LANES, BLOCK, 128), f32),
            jax.ShapeDtypeStruct((SLOTS, SHARE), bf16),
        ],
        scratch_shapes=[pltpu.VMEM((SLOTS, 128), f32)],
        compiler_params=PARAMS,
        cost_estimate=pl.CostEstimate(
            flops=2 * SLOTS * SLOTS * SHARE * 2, bytes_accessed=2**22, transcendentals=0
        ),
        name="own",
    )(own_rows)
    products = pl.pallas_call(
        cross_kernel,
        in_specs=[VMEM, VMEM, VMEM],
        out_specs=VMEM,
        out_shape=jax.ShapeDtypeStruct((LANES, BLOCK, 128), f32),
        scratch_shapes=[pltpu.VMEM((SLOTS, SHARE), bf16), pltpu.VMEM((SLOTS, 128), f32)],
        compiler_params=PARAMS,
        name="cross",
    )(part, slots, other_rows)
    products = lax.all_to_all(products, "x", 0, 0, tiled=True)
    best = pl.pallas_call(
        best_kernel,
        in_specs=[VMEM],
        out_specs=VMEM,
        out_shape=jax.ShapeDtypeStruct((REPS * PLANES, 128), f32),
        compiler_params=PARAMS,
        name="best",
    )(products)
    returned = lax.all_to_all(
        best.reshape(REPS * PLANES, 1, 128), ("rep", "z"), 0, 0, tiled=True
    ).reshape(REPS * PLANES, 128)
    out = pl.pallas_call(
        collect_kernel,
        in_specs=[VMEM, VMEM],
        out_specs=VMEM,
        out_shape=jax.ShapeDtypeStruct((1, DOCS), f32),
        compiler_params=PARAMS,
        name="collect",
    )(slot, returned)
    return out.reshape(DOCS)


def solution(mesh):
    fine = Mesh(mesh.devices.reshape(PLANES, LANES, 2, REPS), ("z", "x", "core", "rep"))
    shard = ("z", "x", "core")
    return jax.shard_map(
        on_device,
        mesh=fine,
        in_specs=(P(shard, None), P(shard)),
        out_specs=P(shard),
        check_vma=False,
    )
```

```python
import jax
import jax.numpy as jnp
from jax import lax
from jax.experimental import pallas as pl
from jax.experimental.pallas import tpu as pltpu
from jax.sharding import Mesh
from jax.sharding import PartitionSpec as P

PLANES = 16
LANES = 4
PARTS = 2
PAIR = 2
REPS = 4
RANKS = 4
DOCS = 256
WIDTH = 4096
SHARE = WIDTH // PARTS
HALF = SHARE // 2
SOURCES = PLANES * LANES
SLOTS = SOURCES * RANKS
ROWS = SLOTS * 2
CHUNK = 256
LOCAL = SLOTS // LANES
BLOCK = 4 * LOCAL + 8

epsilon = 1e-06
f32 = jnp.float32
bf16 = jnp.bfloat16


def iota(shape, dim):
    return lax.broadcasted_iota(jnp.int32, shape, dim)


def dispatch_kernel(
    cluster_ref, docs_ref, out_ref, slot_ref, labels, docs, label_sem, sems
):
    fetch_labels = pltpu.make_async_copy(cluster_ref, labels, label_sem)
    fetch_labels.start()

    fetches = []
    for part in range(PARTS):
        columns = slice(part * SHARE, (part + 1) * SHARE)
        fetch = pltpu.make_async_copy(docs_ref.at[:, columns], docs.at[part], sems.at[part])
        fetch.start(priority=1)
        fetches.append(fetch)
    fetch_labels.wait()
    cluster = labels[...]
    row = jnp.broadcast_to(cluster.astype(f32), (DOCS, DOCS))
    first, second = iota((DOCS, DOCS), 0), iota((DOCS, DOCS), 1)
    column = jnp.max(jnp.where(first == second, row, f32(-1.0)), axis=1, keepdims=True)
    earlier = (column == row) & (first < second)
    rank = jnp.sum(jnp.where(earlier, f32(1.0), f32(0.0)), axis=0, keepdims=True)
    slot = cluster * RANKS + rank.astype(jnp.int32)
    slot_ref[...] = slot
    local = slot - lax.axis_index("rep") * (PLANES * PAIR * RANKS)
    place = ((local >> 2) & 1) * (PLANES * RANKS) + (local >> 3) * RANKS + (local & 3)
    here = (local >= 0) & (local < PLANES * PAIR * RANKS)
    hit = (first >> 1) == jnp.where(here, place, -1)
    odd = (first & 1) == 1
    zero, one = f32(0.0), f32(1.0)
    even = jnp.where(hit & jnp.logical_not(odd), one, zero).astype(bf16)
    uneven = jnp.where(hit & odd, one, zero).astype(bf16)
    ones = jnp.ones((DOCS, 128), bf16)
    live = jnp.dot(even + uneven, ones, preferred_element_type=f32) > 0.5
    for part in range(PARTS):
        fetches[part].wait()
        merged = jnp.dot(even, docs[part, :, :HALF], preferred_element_type=f32)
        merged = merged + jnp.dot(uneven, docs[part, :, HALF:], preferred_element_type=f32)
        marked = jnp.where(live, merged[:, :128], jnp.nan)
        merged = jnp.concatenate([marked, merged[:, 128:]], axis=1)
        out_ref[part] = merged.astype(bf16)


def multiply(left, right):
    return lax.dot_general(left, right, (((1,), (1,)), ((), ())), preferred_element_type=f32)


def gather_slots(rows_ref, slots_ref, vacant_ref):
    row = iota((CHUNK, CHUNK), 0)
    half, lane, rank, plane = row >> 7, (row >> 6) & 1, (row >> 4) & 3, row & 15
    source = (lane * PLANES + plane) * (2 * RANKS) + rank * 2 + half
    pick = jnp.where(iota((CHUNK, CHUNK), 1) == source, f32(1.0), f32(0.0)).astype(bf16)
    for chunk in range(ROWS // CHUNK):
        span = slice(chunk * CHUNK, (chunk + 1) * CHUNK)
        marked = rows_ref[span, :128].astype(f32)
        empty = marked != marked
        clean = jnp.where(empty, f32(0.0), marked).astype(bf16)
        flags = jnp.where(empty, f32(1.0), f32(0.0)).astype(bf16)
        rows = jnp.concatenate([clean, rows_ref[span, 128:], flags], axis=1)
        picked = jnp.dot(pick, rows, preferred_element_type=f32)
        slots = picked[:, :HALF].astype(bf16)
        at = slice(chunk * 128, (chunk + 1) * 128)
        slots_ref[at, :HALF] = slots[:128]
        slots_ref[at, HALF:] = slots[128:]
        vacant_ref[at, :] = picked[:128, HALF:]


def flagged_block(block, vacant):
    eye = iota((128, 128), 0) == iota((128, 128), 1)
    flagged = jnp.where(eye & (vacant > 0.5), jnp.nan, block)
    return flagged, jnp.sum(jnp.where(eye, flagged, f32(0.0)), axis=0, keepdims=True)


def own_kernel(rows_ref, out_ref, slots_ref, vacant_ref):
    gather_slots(rows_ref, slots_ref, vacant_ref)
    slots = slots_ref[...]
    products = multiply(slots, slots)
    for b in range(2):
        span = slice(b * 128, (b + 1) * 128)
        block, squares = flagged_block(products[span, span], vacant_ref[span, :])
        for lane in range(LANES):
            rows = slice(lane * LOCAL, (lane + 1) * LOCAL)
            inside = slice((lane % 2) * LOCAL, (lane % 2 + 1) * LOCAL)
            tile = block[inside] if lane // 2 == b else products[rows, span]
            out_ref[lane, b * LOCAL : (b + 1) * LOCAL, :] = tile
            out_ref[lane, 4 * LOCAL + b : 4 * LOCAL + b + 1, :] = squares
    for lane in range(LANES):
        out_ref[lane, 4 * LOCAL + 4 :, :] = jnp.zeros((4, 128), f32)


def cross_kernel(part_ref, own_ref, rows_ref, out_ref, other_ref, vacant_ref):
    gather_slots(rows_ref, other_ref, vacant_ref)
    other = other_ref[...]
    products = multiply(jnp.concatenate([own_ref[...], other], axis=0), other)
    for lane in range(LANES):
        rows = slice(lane * LOCAL, (lane + 1) * LOCAL)
        own_rows = slice(0, 2 * LOCAL)
        out_ref[lane, own_rows, :] = part_ref[lane, own_rows, :]
        out_ref[lane, 2 * LOCAL : 3 * LOCAL, :] = products[rows, :128]
        out_ref[lane, 3 * LOCAL : 4 * LOCAL, :] = products[rows, 128:]
        out_ref[lane, 4 * LOCAL :, :] = part_ref[lane, 4 * LOCAL :, :]
    for b in range(2):
        span = slice(b * 128, (b + 1) * 128)
        below = products[SLOTS + b * 128 : SLOTS + (b + 1) * 128, span]
        squares = flagged_block(below, vacant_ref[span, :])[1]
        for lane in range(LANES):
            out_ref[lane, 4 * LOCAL + 2 + b : 4 * LOCAL + 3 + b, :] = squares


def best_kernel(parts_ref, out_ref):
    row, column = iota((LOCAL, 128), 0), iota((LOCAL, 128), 1)
    spot = column & 7
    rank = (row >> 4) & 3
    spread = jnp.zeros((LOCAL, 128), f32)

    def scale(squares):
        return jnp.where(squares == squares, lax.rsqrt(squares + epsilon), f32(-1.0))

    for cluster in range(PAIR):
        total = parts_ref[cluster] + parts_ref[PAIR + cluster]
        tiles = [total[t * LOCAL : (t + 1) * LOCAL] for t in range(4)]
        mates = [scale(total[4 * LOCAL + t : 4 * LOCAL + t + 1]) for t in range(4)]
        same = [column + t * 128 == row + lax.axis_index("x") * LOCAL for t in range(2)]
        squares = jnp.where(same[0], tiles[0], f32(0.0)) + jnp.where(same[1], tiles[1], f32(0.0))
        own = scale(jnp.sum(squares, axis=1, keepdims=True))
        best = jnp.full((LOCAL, 128), -1.0, f32)
        for t in range(4):
            cosine = tiles[t] * own * mates[t]
            allowed = (own >= 0.0) & (mates[t] >= 0.0)
            if t < 2:
                allowed = allowed & jnp.logical_not(same[t])
            best = jnp.maximum(best, jnp.where(allowed, cosine, f32(-1.0)))
        best = jnp.max(best, axis=1, keepdims=True)
        spread = jnp.where(spot == cluster * RANKS + rank, best, spread)
    ranks = [spread[k * PLANES : (k + 1) * PLANES] for k in range(RANKS)]
    turned = (ranks[0] + ranks[1]) + (ranks[2] + ranks[3])
    for rep in range(REPS):
        out_ref[rep * PLANES : (rep + 1) * PLANES, :] = turned


def collect_kernel(slot_ref, best_ref, out_ref):
    slot = slot_ref[...]
    best = best_ref[...]
    high = best.astype(bf16).astype(f32)
    middle = (best - high).astype(bf16).astype(f32)
    low = best - high - middle
    group = iota((REPS * PLANES, 128), 1) >> 3
    pieces = jnp.where(group == 0, high, jnp.where(group == 1, middle, low))
    pieces = jnp.where(group < 3, pieces, f32(0.0)).astype(bf16)
    chosen = (iota((128, DOCS), 0) & 7) == (slot & 7)
    chosen = jnp.where(chosen, f32(1.0), f32(0.0)).astype(bf16)
    values = jnp.dot(pieces, chosen, preferred_element_type=f32)
    line = iota((REPS * PLANES, DOCS), 0) == (slot >> 3)
    out_ref[...] = jnp.sum(jnp.where(line, values, f32(0.0)), axis=0, keepdims=True)


VMEM = pl.BlockSpec(memory_space=pltpu.VMEM)
HBM = pl.BlockSpec(memory_space=pltpu.HBM)
PARAMS = pltpu.CompilerParams(vmem_limit_bytes=32 * 1024 * 1024)


def on_device(embeddings, cluster_of):
    labels = pltpu.with_memory_space_constraint(cluster_of.reshape(1, DOCS), pltpu.HBM)
    outgoing, slot = pl.pallas_call(
        dispatch_kernel,
        in_specs=[HBM, HBM],
        out_specs=[VMEM, VMEM],
        out_shape=[
            jax.ShapeDtypeStruct((PARTS, PAIR * PLANES * RANKS * 2, HALF), bf16),
            jax.ShapeDtypeStruct((1, DOCS), jnp.int32),
        ],
        scratch_shapes=[
            pltpu.VMEM((1, DOCS), jnp.int32),
            pltpu.VMEM((PARTS, DOCS, SHARE), bf16),
            pltpu.SemaphoreType.DMA,
            pltpu.SemaphoreType.DMA((PARTS,)),
        ],
        compiler_params=PARAMS,
        name="dispatch",
    )(labels, pltpu.with_memory_space_constraint(embeddings, pltpu.HBM))
    own_rows = lax.all_to_all(
        outgoing.reshape(SOURCES, 2 * RANKS, HALF), ("x", "z"), 0, 0, tiled=True
    ).reshape(ROWS, HALF)
    other_rows = lax.ppermute(own_rows, "core", [(0, 1), (1, 0)])
    part, slots = pl.pallas_call(
        own_kernel,
        in_specs=[VMEM],
        out_specs=[VMEM, VMEM],
        out_shape=[
            jax.ShapeDtypeStruct((LANES, BLOCK, 128), f32),
            jax.ShapeDtypeStruct((SLOTS, SHARE), bf16),
        ],
        scratch_shapes=[pltpu.VMEM((SLOTS, 128), f32)],
        compiler_params=PARAMS,
        cost_estimate=pl.CostEstimate(
            flops=2 * SLOTS * SLOTS * SHARE * 2, bytes_accessed=2**22, transcendentals=0
        ),
        name="own",
    )(own_rows)
    products = pl.pallas_call(
        cross_kernel,
        in_specs=[VMEM, VMEM, VMEM],
        out_specs=VMEM,
        out_shape=jax.ShapeDtypeStruct((LANES, BLOCK, 128), f32),
        scratch_shapes=[pltpu.VMEM((SLOTS, SHARE), bf16), pltpu.VMEM((SLOTS, 128), f32)],
        compiler_params=PARAMS,
        name="cross",
    )(part, slots, other_rows)
    products = lax.all_to_all(products, "x", 0, 0, tiled=True)
    best = pl.pallas_call(
        best_kernel,
        in_specs=[VMEM],
        out_specs=VMEM,
        out_shape=jax.ShapeDtypeStruct((REPS * PLANES, 128), f32),
        compiler_params=PARAMS,
        name="best",
    )(products)
    returned = lax.all_to_all(
        best.reshape(REPS * PLANES, 1, 128), ("rep", "z"), 0, 0, tiled=True
    ).reshape(REPS * PLANES, 128)
    out = pl.pallas_call(
        collect_kernel,
        in_specs=[VMEM, VMEM],
        out_specs=VMEM,
        out_shape=jax.ShapeDtypeStruct((1, DOCS), f32),
        compiler_params=PARAMS,
        name="collect",
    )(slot, returned)
    return out.reshape(DOCS)


def solution(mesh):
    fine = Mesh(mesh.devices.reshape(PLANES, LANES, 2, REPS), ("z", "x", "core", "rep"))
    shard = ("z", "x", "core")
    return jax.shard_map(
        on_device,
        mesh=fine,
        in_specs=(P(shard, None), P(shard)),
        out_specs=P(shard),
        check_vma=False,
    )
```

```python
import jax
import jax.numpy as jnp
from jax import lax
from jax.experimental import pallas as pl
from jax.experimental.pallas import tpu as pltpu
from jax.sharding import Mesh
from jax.sharding import PartitionSpec as P

PLANES = 16
LANES = 4
PARTS = 2
PAIR = 2
REPS = 4
RANKS = 4
DOCS = 256
WIDTH = 4096
SHARE = WIDTH // PARTS
HALF = SHARE // 2
SOURCES = PLANES * LANES
SLOTS = SOURCES * RANKS
ROWS = SLOTS * 2
CHUNK = 256
LOCAL = SLOTS // LANES
BLOCK = 4 * LOCAL + 8

epsilon = 1e-06
f32 = jnp.float32
bf16 = jnp.bfloat16


def iota(shape, dim):
    return lax.broadcasted_iota(jnp.int32, shape, dim)


def turn_plane(z):
    return ((z & 7) << 1) + (z >> 3)


def dispatch_kernel(
    cluster_ref, docs_ref, out_ref, slot_ref, labels, docs, label_sem, sems
):
    fetch_labels = pltpu.make_async_copy(cluster_ref, labels, label_sem)
    fetch_labels.start()

    fetches = []
    for part in range(PARTS):
        columns = slice(part * SHARE, (part + 1) * SHARE)
        fetch = pltpu.make_async_copy(docs_ref.at[:, columns], docs.at[part], sems.at[part])
        fetch.start(priority=1)
        fetches.append(fetch)
    fetch_labels.wait()
    cluster = labels[...]
    row = jnp.broadcast_to(cluster.astype(f32), (DOCS, DOCS))
    first, second = iota((DOCS, DOCS), 0), iota((DOCS, DOCS), 1)
    column = jnp.max(jnp.where(first == second, row, f32(-1.0)), axis=1, keepdims=True)
    earlier = (column == row) & (first < second)
    rank = jnp.sum(jnp.where(earlier, f32(1.0), f32(0.0)), axis=0, keepdims=True)
    slot = cluster * RANKS + rank.astype(jnp.int32)
    slot_ref[...] = slot
    local = slot - lax.axis_index("rep") * (PLANES * PAIR * RANKS)
    here = (local >= 0) & (local < PLANES * PAIR * RANKS)
    place = turn_plane(local >> 3) * (PAIR * RANKS) + (local & 7)
    hit = (first >> 1) == jnp.where(here, place, -1)
    odd = (first & 1) == 1
    zero, one = f32(0.0), f32(1.0)
    even = jnp.where(hit & jnp.logical_not(odd), one, zero).astype(bf16)
    uneven = jnp.where(hit & odd, one, zero).astype(bf16)
    ones = jnp.ones((DOCS, 128), bf16)
    live = jnp.dot(even + uneven, ones, preferred_element_type=f32) > 0.5
    for part in range(PARTS):
        fetches[part].wait()
        merged = jnp.dot(even, docs[part, :, :HALF], preferred_element_type=f32)
        merged = merged + jnp.dot(uneven, docs[part, :, HALF:], preferred_element_type=f32)
        marked = jnp.where(live, merged[:, :128], jnp.nan)
        merged = jnp.concatenate([marked, merged[:, 128:]], axis=1)
        out_ref[:, part, :, :] = merged.astype(bf16).reshape(PLANES, 16, HALF)


def multiply(left, right):
    return lax.dot_general(left, right, (((1,), (1,)), ((), ())), preferred_element_type=f32)


def gather_slots(rows_ref, slots_ref, vacant_ref):
    row = iota((CHUNK, CHUNK), 0)
    half, lane, rank, plane = row >> 7, (row >> 5) & 3, (row >> 3) & 3, row & 7
    source = (plane * LANES + lane) * (2 * RANKS) + rank * 2 + half
    pick = jnp.where(iota((CHUNK, CHUNK), 1) == source, f32(1.0), f32(0.0)).astype(bf16)
    for chunk in range(ROWS // CHUNK):
        span = slice(chunk * CHUNK, (chunk + 1) * CHUNK)
        marked = rows_ref[span, :128].astype(f32)
        empty = marked != marked
        clean = jnp.where(empty, f32(0.0), marked).astype(bf16)
        flags = jnp.where(empty, f32(1.0), f32(0.0)).astype(bf16)
        rows = jnp.concatenate([clean, rows_ref[span, 128:], flags], axis=1)
        picked = jnp.dot(pick, rows, preferred_element_type=f32)
        slots = picked[:, :HALF].astype(bf16)
        for lane in range(LANES):
            top = lane * LOCAL + chunk * 32
            slots_ref[top : top + 32, :HALF] = slots[lane * 32 : (lane + 1) * 32]
            slots_ref[top : top + 32, HALF:] = slots[128 + lane * 32 : 128 + (lane + 1) * 32]
            vacant_ref[top : top + 32, :] = picked[lane * 32 : (lane + 1) * 32, HALF:]


def flagged_block(block, vacant):
    eye = iota((128, 128), 0) == iota((128, 128), 1)
    flagged = jnp.where(eye & (vacant > 0.5), jnp.nan, block)
    return flagged, jnp.sum(jnp.where(eye, flagged, f32(0.0)), axis=0, keepdims=True)


def own_kernel(rows_ref, out_ref, slots_ref, vacant_ref):
    gather_slots(rows_ref, slots_ref, vacant_ref)
    slots = slots_ref[...]
    products = multiply(slots, slots)
    for b in range(2):
        span = slice(b * 128, (b + 1) * 128)
        block, squares = flagged_block(products[span, span], vacant_ref[span, :])
        for lane in range(LANES):
            rows = slice(lane * LOCAL, (lane + 1) * LOCAL)
            inside = slice((lane % 2) * LOCAL, (lane % 2 + 1) * LOCAL)
            tile = block[inside] if lane // 2 == b else products[rows, span]
            out_ref[lane, b * LOCAL : (b + 1) * LOCAL, :] = tile
            out_ref[lane, 4 * LOCAL + b : 4 * LOCAL + b + 1, :] = squares
    for lane in range(LANES):
        out_ref[lane, 4 * LOCAL + 4 :, :] = jnp.zeros((4, 128), f32)


def cross_kernel(part_ref, own_ref, rows_ref, out_ref, other_ref, vacant_ref):
    gather_slots(rows_ref, other_ref, vacant_ref)
    other = other_ref[...]
    products = multiply(jnp.concatenate([own_ref[...], other], axis=0), other)
    for lane in range(LANES):
        rows = slice(lane * LOCAL, (lane + 1) * LOCAL)
        own_rows = slice(0, 2 * LOCAL)
        out_ref[lane, own_rows, :] = part_ref[lane, own_rows, :]
        out_ref[lane, 2 * LOCAL : 3 * LOCAL, :] = products[rows, :128]
        out_ref[lane, 3 * LOCAL : 4 * LOCAL, :] = products[rows, 128:]
        out_ref[lane, 4 * LOCAL :, :] = part_ref[lane, 4 * LOCAL :, :]
    for b in range(2):
        span = slice(b * 128, (b + 1) * 128)
        below = products[SLOTS + b * 128 : SLOTS + (b + 1) * 128, span]
        squares = flagged_block(below, vacant_ref[span, :])[1]
        for lane in range(LANES):
            out_ref[lane, 4 * LOCAL + 2 + b : 4 * LOCAL + 3 + b, :] = squares


def best_kernel(parts_ref, out_ref):
    row, column = iota((LOCAL, 128), 0), iota((LOCAL, 128), 1)
    spot = column & 7
    rank = (row >> 3) & 3
    spread = jnp.zeros((LOCAL, 128), f32)

    def scale(squares):
        return jnp.where(squares == squares, lax.rsqrt(squares + epsilon), f32(-1.0))

    for cluster in range(PAIR):
        total = parts_ref[cluster] + parts_ref[PAIR + cluster]
        tiles = [total[t * LOCAL : (t + 1) * LOCAL] for t in range(4)]
        mates = [scale(total[4 * LOCAL + t : 4 * LOCAL + t + 1]) for t in range(4)]
        same = [column + t * 128 == row + lax.axis_index("x") * LOCAL for t in range(2)]
        squares = jnp.where(same[0], tiles[0], f32(0.0)) + jnp.where(same[1], tiles[1], f32(0.0))
        own = scale(jnp.sum(squares, axis=1, keepdims=True))
        best = jnp.full((LOCAL, 128), -1.0, f32)
        for t in range(4):
            cosine = tiles[t] * own * mates[t]
            allowed = (own >= 0.0) & (mates[t] >= 0.0)
            if t < 2:
                allowed = allowed & jnp.logical_not(same[t])
            best = jnp.maximum(best, jnp.where(allowed, cosine, f32(-1.0)))
        best = jnp.max(best, axis=1, keepdims=True)
        spread = jnp.where(spot == cluster * RANKS + rank, best, spread)
    planes = []
    for top in range(0, LOCAL, 32):
        tiles = [spread[top + k * 8 : top + (k + 1) * 8] for k in range(RANKS)]
        planes.append((tiles[0] + tiles[1]) + (tiles[2] + tiles[3]))
    turned = jnp.concatenate(planes, axis=0)
    for rep in range(REPS):
        out_ref[rep * PLANES : (rep + 1) * PLANES, :] = turned


def collect_kernel(slot_ref, best_ref, out_ref):
    slot = slot_ref[...]
    best = best_ref[...]
    high = best.astype(bf16).astype(f32)
    middle = (best - high).astype(bf16).astype(f32)
    low = best - high - middle
    group = iota((REPS * PLANES, 128), 1) >> 3
    pieces = jnp.where(group == 0, high, jnp.where(group == 1, middle, low))
    pieces = jnp.where(group < 3, pieces, f32(0.0)).astype(bf16)
    chosen = (iota((128, DOCS), 0) & 7) == (slot & 7)
    chosen = jnp.where(chosen, f32(1.0), f32(0.0)).astype(bf16)
    values = jnp.dot(pieces, chosen, preferred_element_type=f32)
    home = slot >> 3
    home = (home & -PLANES) + turn_plane(home & (PLANES - 1))
    line = iota((REPS * PLANES, DOCS), 0) == home
    out_ref[...] = jnp.sum(jnp.where(line, values, f32(0.0)), axis=0, keepdims=True)


VMEM = pl.BlockSpec(memory_space=pltpu.VMEM)
HBM = pl.BlockSpec(memory_space=pltpu.HBM)
PARAMS = pltpu.CompilerParams(vmem_limit_bytes=32 * 1024 * 1024)


def on_device(embeddings, cluster_of):
    labels = pltpu.with_memory_space_constraint(cluster_of.reshape(1, DOCS), pltpu.HBM)
    outgoing, slot = pl.pallas_call(
        dispatch_kernel,
        in_specs=[HBM, HBM],
        out_specs=[VMEM, VMEM],
        out_shape=[
            jax.ShapeDtypeStruct((PLANES, PARTS, 16, HALF), bf16),
            jax.ShapeDtypeStruct((1, DOCS), jnp.int32),
        ],
        scratch_shapes=[
            pltpu.VMEM((1, DOCS), jnp.int32),
            pltpu.VMEM((PARTS, DOCS, SHARE), bf16),
            pltpu.SemaphoreType.DMA,
            pltpu.SemaphoreType.DMA((PARTS,)),
        ],
        compiler_params=PARAMS,
        name="dispatch",
    )(labels, pltpu.with_memory_space_constraint(embeddings, pltpu.HBM))
    own_rows = lax.all_to_all(
        outgoing.reshape(SOURCES, 2 * RANKS, HALF), ("zl", "zh", "x"), 0, 0, tiled=True
    ).reshape(ROWS, HALF)
    other_rows = lax.ppermute(own_rows, "core", [(0, 1), (1, 0)])
    part, slots = pl.pallas_call(
        own_kernel,
        in_specs=[VMEM],
        out_specs=[VMEM, VMEM],
        out_shape=[
            jax.ShapeDtypeStruct((LANES, BLOCK, 128), f32),
            jax.ShapeDtypeStruct((SLOTS, SHARE), bf16),
        ],
        scratch_shapes=[pltpu.VMEM((SLOTS, 128), f32)],
        compiler_params=PARAMS,
        cost_estimate=pl.CostEstimate(
            flops=2 * SLOTS * SLOTS * SHARE * 2, bytes_accessed=2**22, transcendentals=0
        ),
        name="own",
    )(own_rows)
    products = pl.pallas_call(
        cross_kernel,
        in_specs=[VMEM, VMEM, VMEM],
        out_specs=VMEM,
        out_shape=jax.ShapeDtypeStruct((LANES, BLOCK, 128), f32),
        scratch_shapes=[pltpu.VMEM((SLOTS, SHARE), bf16), pltpu.VMEM((SLOTS, 128), f32)],
        compiler_params=PARAMS,
        name="cross",
    )(part, slots, other_rows)
    products = lax.all_to_all(products, "x", 0, 0, tiled=True)
    best = pl.pallas_call(
        best_kernel,
        in_specs=[VMEM],
        out_specs=VMEM,
        out_shape=jax.ShapeDtypeStruct((REPS * PLANES, 128), f32),
        compiler_params=PARAMS,
        name="best",
    )(products)
    returned = lax.all_to_all(
        best.reshape(REPS * PLANES, 1, 128), ("rep", "zl", "zh"), 0, 0, tiled=True
    ).reshape(REPS * PLANES, 128)
    out = pl.pallas_call(
        collect_kernel,
        in_specs=[VMEM, VMEM],
        out_specs=VMEM,
        out_shape=jax.ShapeDtypeStruct((1, DOCS), f32),
        compiler_params=PARAMS,
        name="collect",
    )(slot, returned)
    return out.reshape(DOCS)


def solution(mesh):
    axes = ("zh", "zl", "x", "core", "rep")
    fine = Mesh(mesh.devices.reshape(2, PLANES // 2, LANES, 2, REPS), axes)
    shard = axes[:4]
    return jax.shard_map(
        on_device,
        mesh=fine,
        in_specs=(P(shard, None), P(shard)),
        out_specs=P(shard),
        check_vma=False,
    )
```

```python
import jax
import jax.numpy as jnp
from jax import lax
from jax.experimental import pallas as pl
from jax.experimental.pallas import tpu as pltpu
from jax.sharding import Mesh
from jax.sharding import PartitionSpec as P

PLANES = 16
LANES = 4
PARTS = 2
PAIR = 2
REPS = 4
RANKS = 4
DOCS = 256
WIDTH = 4096
SHARE = WIDTH // PARTS
HALF = SHARE // 2
SOURCES = PLANES * LANES
SLOTS = SOURCES * RANKS
ROWS = SLOTS * 2
CHUNK = 256
LOCAL = SLOTS // LANES
BLOCK = 4 * LOCAL + 8

epsilon = 1e-06
f32 = jnp.float32
bf16 = jnp.bfloat16


def iota(shape, dim):
    return lax.broadcasted_iota(jnp.int32, shape, dim)


def dispatch_kernel(
    cluster_ref, docs_ref, out_ref, slot_ref, labels, docs, label_sem, sems
):
    fetch_labels = pltpu.make_async_copy(cluster_ref, labels, label_sem)
    fetch_labels.start()

    fetches = []
    for part in range(PARTS):
        columns = slice(part * SHARE, (part + 1) * SHARE)
        fetch = pltpu.make_async_copy(docs_ref.at[:, columns], docs.at[part], sems.at[part])
        fetch.start(priority=1)
        fetches.append(fetch)
    fetch_labels.wait()
    cluster = labels[...]
    row = jnp.broadcast_to(cluster.astype(f32), (DOCS, DOCS))
    first, second = iota((DOCS, DOCS), 0), iota((DOCS, DOCS), 1)
    column = jnp.max(jnp.where(first == second, row, f32(-1.0)), axis=1, keepdims=True)
    earlier = (column == row) & (first < second)
    rank = jnp.sum(jnp.where(earlier, f32(1.0), f32(0.0)), axis=0, keepdims=True)
    slot = cluster * RANKS + rank.astype(jnp.int32)
    slot_ref[...] = slot
    local = slot - lax.axis_index("rep") * (PLANES * PAIR * RANKS)
    hit = (first >> 1) == local
    odd = (first & 1) == 1
    zero, one = f32(0.0), f32(1.0)
    even = jnp.where(hit & jnp.logical_not(odd), one, zero).astype(bf16)
    uneven = jnp.where(hit & odd, one, zero).astype(bf16)
    ones = jnp.ones((DOCS, 128), bf16)
    live = jnp.dot(even + uneven, ones, preferred_element_type=f32) > 0.5
    for part in range(PARTS):
        fetches[part].wait()
        merged = jnp.dot(even, docs[part, :, :HALF], preferred_element_type=f32)
        merged = merged + jnp.dot(uneven, docs[part, :, HALF:], preferred_element_type=f32)
        marked = jnp.where(live, merged[:, :128], jnp.nan)
        merged = jnp.concatenate([marked, merged[:, 128:]], axis=1)
        out_ref[:, part, :, :] = merged.astype(bf16).reshape(PLANES, 16, HALF)


def multiply(left, right):
    return lax.dot_general(left, right, (((1,), (1,)), ((), ())), preferred_element_type=f32)


def gather_slots(rows_ref, slots_ref, vacant_ref):
    row = iota((CHUNK, CHUNK), 0)
    half, lane, rank, plane = row >> 7, (row >> 5) & 3, (row >> 3) & 3, row & 7
    source = (plane * LANES + lane) * (2 * RANKS) + rank * 2 + half
    pick = jnp.where(iota((CHUNK, CHUNK), 1) == source, f32(1.0), f32(0.0)).astype(bf16)
    for chunk in range(ROWS // CHUNK):
        span = slice(chunk * CHUNK, (chunk + 1) * CHUNK)
        marked = rows_ref[span, :128].astype(f32)
        empty = marked != marked
        clean = jnp.where(empty, f32(0.0), marked).astype(bf16)
        flags = jnp.where(empty, f32(1.0), f32(0.0)).astype(bf16)
        rows = jnp.concatenate([clean, rows_ref[span, 128:], flags], axis=1)
        picked = jnp.dot(pick, rows, preferred_element_type=f32)
        slots = picked[:, :HALF].astype(bf16)
        for lane in range(LANES):
            top = lane * LOCAL + chunk * 32
            slots_ref[top : top + 32, :HALF] = slots[lane * 32 : (lane + 1) * 32]
            slots_ref[top : top + 32, HALF:] = slots[128 + lane * 32 : 128 + (lane + 1) * 32]
            vacant_ref[top : top + 32, :] = picked[lane * 32 : (lane + 1) * 32, HALF:]


def flagged_block(block, vacant):
    eye = iota((128, 128), 0) == iota((128, 128), 1)
    flagged = jnp.where(eye & (vacant > 0.5), jnp.nan, block)
    return flagged, jnp.sum(jnp.where(eye, flagged, f32(0.0)), axis=0, keepdims=True)


def own_kernel(rows_ref, out_ref, slots_ref, vacant_ref):
    gather_slots(rows_ref, slots_ref, vacant_ref)
    slots = slots_ref[...]
    products = multiply(slots, slots)
    for b in range(2):
        span = slice(b * 128, (b + 1) * 128)
        block, squares = flagged_block(products[span, span], vacant_ref[span, :])
        for lane in range(LANES):
            rows = slice(lane * LOCAL, (lane + 1) * LOCAL)
            inside = slice((lane % 2) * LOCAL, (lane % 2 + 1) * LOCAL)
            tile = block[inside] if lane // 2 == b else products[rows, span]
            out_ref[lane, b * LOCAL : (b + 1) * LOCAL, :] = tile
            out_ref[lane, 4 * LOCAL + b : 4 * LOCAL + b + 1, :] = squares
    for lane in range(LANES):
        out_ref[lane, 4 * LOCAL + 4 :, :] = jnp.zeros((4, 128), f32)


def cross_kernel(part_ref, own_ref, rows_ref, out_ref, other_ref, vacant_ref):
    gather_slots(rows_ref, other_ref, vacant_ref)
    other = other_ref[...]
    products = multiply(jnp.concatenate([own_ref[...], other], axis=0), other)
    for lane in range(LANES):
        rows = slice(lane * LOCAL, (lane + 1) * LOCAL)
        own_rows = slice(0, 2 * LOCAL)
        out_ref[lane, own_rows, :] = part_ref[lane, own_rows, :]
        out_ref[lane, 2 * LOCAL : 3 * LOCAL, :] = products[rows, :128]
        out_ref[lane, 3 * LOCAL : 4 * LOCAL, :] = products[rows, 128:]
        out_ref[lane, 4 * LOCAL :, :] = part_ref[lane, 4 * LOCAL :, :]
    for b in range(2):
        span = slice(b * 128, (b + 1) * 128)
        below = products[SLOTS + b * 128 : SLOTS + (b + 1) * 128, span]
        squares = flagged_block(below, vacant_ref[span, :])[1]
        for lane in range(LANES):
            out_ref[lane, 4 * LOCAL + 2 + b : 4 * LOCAL + 3 + b, :] = squares


def best_kernel(parts_ref, out_ref):
    row, column = iota((LOCAL, 128), 0), iota((LOCAL, 128), 1)
    spot = column & 7
    rank = (row >> 3) & 3
    spread = jnp.zeros((LOCAL, 128), f32)

    def scale(squares):
        return jnp.where(squares == squares, lax.rsqrt(squares + epsilon), f32(-1.0))

    for cluster in range(PAIR):
        total = parts_ref[cluster] + parts_ref[PAIR + cluster]
        tiles = [total[t * LOCAL : (t + 1) * LOCAL] for t in range(4)]
        mates = [scale(total[4 * LOCAL + t : 4 * LOCAL + t + 1]) for t in range(4)]
        same = [column + t * 128 == row + lax.axis_index("x") * LOCAL for t in range(2)]
        squares = jnp.where(same[0], tiles[0], f32(0.0)) + jnp.where(same[1], tiles[1], f32(0.0))
        own = scale(jnp.sum(squares, axis=1, keepdims=True))
        best = jnp.full((LOCAL, 128), -1.0, f32)
        for t in range(4):
            cosine = tiles[t] * own * mates[t]
            allowed = (own >= 0.0) & (mates[t] >= 0.0)
            if t < 2:
                allowed = allowed & jnp.logical_not(same[t])
            best = jnp.maximum(best, jnp.where(allowed, cosine, f32(-1.0)))
        best = jnp.max(best, axis=1, keepdims=True)
        spread = jnp.where(spot == cluster * RANKS + rank, best, spread)
    planes = []
    for top in range(0, LOCAL, 32):
        tiles = [spread[top + k * 8 : top + (k + 1) * 8] for k in range(RANKS)]
        planes.append((tiles[0] + tiles[1]) + (tiles[2] + tiles[3]))
    turned = jnp.concatenate(planes, axis=0)
    for rep in range(REPS):
        out_ref[:, rep, :] = turned


def collect_kernel(slot_ref, best_ref, out_ref):
    slot = slot_ref[...]
    best = best_ref[...]
    high = best.astype(bf16).astype(f32)
    middle = (best - high).astype(bf16).astype(f32)
    low = best - high - middle
    group = iota((REPS * PLANES, 128), 1) >> 3
    pieces = jnp.where(group == 0, high, jnp.where(group == 1, middle, low))
    pieces = jnp.where(group < 3, pieces, f32(0.0)).astype(bf16)
    chosen = (iota((128, DOCS), 0) & 7) == (slot & 7)
    chosen = jnp.where(chosen, f32(1.0), f32(0.0)).astype(bf16)
    values = jnp.dot(pieces, chosen, preferred_element_type=f32)
    home = slot >> 3
    home = (home & (PLANES - 1)) * REPS + home // PLANES
    line = iota((REPS * PLANES, DOCS), 0) == home
    out_ref[...] = jnp.sum(jnp.where(line, values, f32(0.0)), axis=0, keepdims=True)


VMEM = pl.BlockSpec(memory_space=pltpu.VMEM)
HBM = pl.BlockSpec(memory_space=pltpu.HBM)
PARAMS = pltpu.CompilerParams(vmem_limit_bytes=32 * 1024 * 1024)


def on_device(embeddings, cluster_of):
    labels = pltpu.with_memory_space_constraint(cluster_of.reshape(1, DOCS), pltpu.HBM)
    outgoing, slot = pl.pallas_call(
        dispatch_kernel,
        in_specs=[HBM, HBM],
        out_specs=[VMEM, VMEM],
        out_shape=[
            jax.ShapeDtypeStruct((PLANES, PARTS, 16, HALF), bf16),
            jax.ShapeDtypeStruct((1, DOCS), jnp.int32),
        ],
        scratch_shapes=[
            pltpu.VMEM((1, DOCS), jnp.int32),
            pltpu.VMEM((PARTS, DOCS, SHARE), bf16),
            pltpu.SemaphoreType.DMA,
            pltpu.SemaphoreType.DMA((PARTS,)),
        ],
        compiler_params=PARAMS,
        name="dispatch",
    )(labels, pltpu.with_memory_space_constraint(embeddings, pltpu.HBM))
    own_rows = lax.all_to_all(
        outgoing.reshape(SOURCES, 2 * RANKS, HALF), ("z", "x"), 0, 0, tiled=True
    ).reshape(ROWS, HALF)
    other_rows = lax.ppermute(own_rows, "core", [(0, 1), (1, 0)])
    part, slots = pl.pallas_call(
        own_kernel,
        in_specs=[VMEM],
        out_specs=[VMEM, VMEM],
        out_shape=[
            jax.ShapeDtypeStruct((LANES, BLOCK, 128), f32),
            jax.ShapeDtypeStruct((SLOTS, SHARE), bf16),
        ],
        scratch_shapes=[pltpu.VMEM((SLOTS, 128), f32)],
        compiler_params=PARAMS,
        cost_estimate=pl.CostEstimate(
            flops=2 * SLOTS * SLOTS * SHARE * 2, bytes_accessed=2**22, transcendentals=0
        ),
        name="own",
    )(own_rows)
    products = pl.pallas_call(
        cross_kernel,
        in_specs=[VMEM, VMEM, VMEM],
        out_specs=VMEM,
        out_shape=jax.ShapeDtypeStruct((LANES, BLOCK, 128), f32),
        scratch_shapes=[pltpu.VMEM((SLOTS, SHARE), bf16), pltpu.VMEM((SLOTS, 128), f32)],
        compiler_params=PARAMS,
        name="cross",
    )(part, slots, other_rows)
    products = lax.all_to_all(products, "x", 0, 0, tiled=True)
    best = pl.pallas_call(
        best_kernel,
        in_specs=[VMEM],
        out_specs=VMEM,
        out_shape=jax.ShapeDtypeStruct((PLANES, REPS, 128), f32),
        compiler_params=PARAMS,
        name="best",
    )(products)
    returned = lax.all_to_all(
        best.reshape(REPS * PLANES, 1, 128), ("z", "rep"), 0, 0, tiled=True
    ).reshape(REPS * PLANES, 128)
    out = pl.pallas_call(
        collect_kernel,
        in_specs=[VMEM, VMEM],
        out_specs=VMEM,
        out_shape=jax.ShapeDtypeStruct((1, DOCS), f32),
        compiler_params=PARAMS,
        name="collect",
    )(slot, returned)
    return out.reshape(DOCS)


def solution(mesh):
    fine = Mesh(mesh.devices.reshape(PLANES, LANES, 2, REPS), ("z", "x", "core", "rep"))
    shard = ("z", "x", "core")
    return jax.shard_map(
        on_device,
        mesh=fine,
        in_specs=(P(shard, None), P(shard)),
        out_specs=P(shard),
        check_vma=False,
    )
```

```python
import jax
import jax.numpy as jnp
from jax import lax
from jax.experimental import pallas as pl
from jax.experimental.pallas import tpu as pltpu
from jax.sharding import Mesh
from jax.sharding import PartitionSpec as P

PLANES = 16
LANES = 4
PARTS = 2
PAIR = 2
REPS = 4
RANKS = 4
DOCS = 256
WIDTH = 4096
SHARE = WIDTH // PARTS
HALF = SHARE // 2
SOURCES = PLANES * LANES
SLOTS = SOURCES * RANKS
ROWS = SLOTS * 2
CHUNK = 256
LOCAL = SLOTS // LANES
BLOCK = 4 * LOCAL + 8

epsilon = 1e-06
f32 = jnp.float32
bf16 = jnp.bfloat16


def iota(shape, dim):
    return lax.broadcasted_iota(jnp.int32, shape, dim)


def dispatch_kernel(
    cluster_ref, docs_ref, out_ref, slot_ref, labels, docs, label_sem, sems
):
    fetch_labels = pltpu.make_async_copy(cluster_ref, labels, label_sem)
    fetch_labels.start()

    fetches = []
    for part in range(PARTS):
        columns = slice(part * SHARE, (part + 1) * SHARE)
        fetch = pltpu.make_async_copy(docs_ref.at[:, columns], docs.at[part], sems.at[part])
        fetch.start(priority=1)
        fetches.append(fetch)
    fetch_labels.wait()
    cluster = labels[...]
    row = jnp.broadcast_to(cluster.astype(f32), (DOCS, DOCS))
    first, second = iota((DOCS, DOCS), 0), iota((DOCS, DOCS), 1)
    column = jnp.max(jnp.where(first == second, row, f32(-1.0)), axis=1, keepdims=True)
    earlier = (column == row) & (first < second)
    rank = jnp.sum(jnp.where(earlier, f32(1.0), f32(0.0)), axis=0, keepdims=True)
    slot = cluster * RANKS + rank.astype(jnp.int32)
    slot_ref[...] = slot
    local = slot - lax.axis_index("rep") * (PLANES * PAIR * RANKS)
    place = ((local >> 2) & 1) * (PLANES * RANKS) + (local >> 3) * RANKS + (local & 3)
    here = (local >= 0) & (local < PLANES * PAIR * RANKS)
    hit = (first >> 1) == jnp.where(here, place, -1)
    odd = (first & 1) == 1
    zero, one = f32(0.0), f32(1.0)
    even = jnp.where(hit & jnp.logical_not(odd), one, zero).astype(bf16)
    uneven = jnp.where(hit & odd, one, zero).astype(bf16)
    ones = jnp.ones((DOCS, 128), bf16)
    live = jnp.dot(even + uneven, ones, preferred_element_type=f32) > 0.5
    for part in range(PARTS):
        fetches[part].wait()
        merged = jnp.dot(even, docs[part, :, :HALF], preferred_element_type=f32)
        merged = merged + jnp.dot(uneven, docs[part, :, HALF:], preferred_element_type=f32)
        marked = jnp.where(live, merged[:, :128], jnp.nan)
        merged = jnp.concatenate([marked, merged[:, 128:]], axis=1)
        out_ref[part] = merged.astype(bf16)


def multiply(left, right):
    return lax.dot_general(left, right, (((1,), (1,)), ((), ())), preferred_element_type=f32)


def gather_slots(rows_ref, slots_ref, vacant_ref):
    row = iota((CHUNK, CHUNK), 0)
    half, lane, rank, plane = row >> 7, (row >> 6) & 1, (row >> 4) & 3, row & 15
    source = (lane * PLANES + plane) * (2 * RANKS) + rank * 2 + half
    pick = jnp.where(iota((CHUNK, CHUNK), 1) == source, f32(1.0), f32(0.0)).astype(bf16)
    for chunk in range(ROWS // CHUNK):
        span = slice(chunk * CHUNK, (chunk + 1) * CHUNK)
        marked = rows_ref[span, :128].astype(f32)
        empty = marked != marked
        clean = jnp.where(empty, f32(0.0), marked).astype(bf16)
        flags = jnp.where(empty, f32(1.0), f32(0.0)).astype(bf16)
        rows = jnp.concatenate([clean, rows_ref[span, 128:], flags], axis=1)
        picked = jnp.dot(pick, rows, preferred_element_type=f32)
        slots = picked[:, :HALF].astype(bf16)
        at = slice(chunk * 128, (chunk + 1) * 128)
        slots_ref[at, :HALF] = slots[:128]
        slots_ref[at, HALF:] = slots[128:]
        vacant_ref[at, :] = picked[:128, HALF:]


def flagged_block(block, vacant):
    eye = iota((128, 128), 0) == iota((128, 128), 1)
    flagged = jnp.where(eye & (vacant > 0.5), jnp.nan, block)
    return flagged, jnp.sum(jnp.where(eye, flagged, f32(0.0)), axis=0, keepdims=True)


def own_kernel(rows_ref, out_ref, slots_ref, vacant_ref):
    gather_slots(rows_ref, slots_ref, vacant_ref)
    slots = slots_ref[...]
    products = multiply(slots, slots)
    for b in range(2):
        span = slice(b * 128, (b + 1) * 128)
        block, squares = flagged_block(products[span, span], vacant_ref[span, :])
        for lane in range(LANES):
            rows = slice(lane * LOCAL, (lane + 1) * LOCAL)
            inside = slice((lane % 2) * LOCAL, (lane % 2 + 1) * LOCAL)
            tile = block[inside] if lane // 2 == b else products[rows, span]
            out_ref[lane, b * LOCAL : (b + 1) * LOCAL, :] = tile
            out_ref[lane, 4 * LOCAL + b : 4 * LOCAL + b + 1, :] = squares
    for lane in range(LANES):
        out_ref[lane, 4 * LOCAL + 4 :, :] = jnp.zeros((4, 128), f32)


def cross_kernel(part_ref, own_ref, rows_ref, out_ref, other_ref, vacant_ref):
    gather_slots(rows_ref, other_ref, vacant_ref)
    other = other_ref[...]
    products = multiply(jnp.concatenate([own_ref[...], other], axis=0), other)
    for lane in range(LANES):
        rows = slice(lane * LOCAL, (lane + 1) * LOCAL)
        own_rows = slice(0, 2 * LOCAL)
        out_ref[lane, own_rows, :] = part_ref[lane, own_rows, :]
        out_ref[lane, 2 * LOCAL : 3 * LOCAL, :] = products[rows, :128]
        out_ref[lane, 3 * LOCAL : 4 * LOCAL, :] = products[rows, 128:]
        out_ref[lane, 4 * LOCAL :, :] = part_ref[lane, 4 * LOCAL :, :]
    for b in range(2):
        span = slice(b * 128, (b + 1) * 128)
        below = products[SLOTS + b * 128 : SLOTS + (b + 1) * 128, span]
        squares = flagged_block(below, vacant_ref[span, :])[1]
        for lane in range(LANES):
            out_ref[lane, 4 * LOCAL + 2 + b : 4 * LOCAL + 3 + b, :] = squares


def best_kernel(parts_ref, out_ref):
    row, column = iota((LOCAL, 128), 0), iota((LOCAL, 128), 1)
    spot = column & 7
    rank = (row >> 4) & 3
    spread = jnp.zeros((LOCAL, 128), f32)

    def scale(squares):
        return jnp.where(squares == squares, lax.rsqrt(squares + epsilon), f32(-1.0))

    for cluster in range(PAIR):
        total = parts_ref[cluster] + parts_ref[PAIR + cluster]
        tiles = [total[t * LOCAL : (t + 1) * LOCAL] for t in range(4)]
        mates = [scale(total[4 * LOCAL + t : 4 * LOCAL + t + 1]) for t in range(4)]
        same = [column + t * 128 == row + lax.axis_index("x") * LOCAL for t in range(2)]
        squares = jnp.where(same[0], tiles[0], f32(0.0)) + jnp.where(same[1], tiles[1], f32(0.0))
        own = scale(jnp.sum(squares, axis=1, keepdims=True))
        best = jnp.full((LOCAL, 128), -1.0, f32)
        for t in range(4):
            cosine = tiles[t] * own * mates[t]
            allowed = (own >= 0.0) & (mates[t] >= 0.0)
            if t < 2:
                allowed = allowed & jnp.logical_not(same[t])
            best = jnp.maximum(best, jnp.where(allowed, cosine, f32(-1.0)))
        best = jnp.max(best, axis=1, keepdims=True)
        spread = jnp.where(spot == cluster * RANKS + rank, best, spread)
    ranks = [spread[k * PLANES : (k + 1) * PLANES] for k in range(RANKS)]
    turned = (ranks[0] + ranks[1]) + (ranks[2] + ranks[3])
    for rep in range(REPS):
        out_ref[:, rep, :] = turned


def collect_kernel(slot_ref, best_ref, out_ref):
    slot = slot_ref[...]
    best = best_ref[...]
    high = best.astype(bf16).astype(f32)
    middle = (best - high).astype(bf16).astype(f32)
    low = best - high - middle
    group = iota((REPS * PLANES, 128), 1) >> 3
    pieces = jnp.where(group == 0, high, jnp.where(group == 1, middle, low))
    pieces = jnp.where(group < 3, pieces, f32(0.0)).astype(bf16)
    chosen = (iota((128, DOCS), 0) & 7) == (slot & 7)
    chosen = jnp.where(chosen, f32(1.0), f32(0.0)).astype(bf16)
    values = jnp.dot(pieces, chosen, preferred_element_type=f32)
    home = slot >> 3
    home = (home & (PLANES - 1)) * REPS + home // PLANES
    line = iota((REPS * PLANES, DOCS), 0) == home
    out_ref[...] = jnp.sum(jnp.where(line, values, f32(0.0)), axis=0, keepdims=True)


VMEM = pl.BlockSpec(memory_space=pltpu.VMEM)
HBM = pl.BlockSpec(memory_space=pltpu.HBM)
PARAMS = pltpu.CompilerParams(vmem_limit_bytes=32 * 1024 * 1024)


def on_device(embeddings, cluster_of):
    labels = pltpu.with_memory_space_constraint(cluster_of.reshape(1, DOCS), pltpu.HBM)
    outgoing, slot = pl.pallas_call(
        dispatch_kernel,
        in_specs=[HBM, HBM],
        out_specs=[VMEM, VMEM],
        out_shape=[
            jax.ShapeDtypeStruct((PARTS, PAIR * PLANES * RANKS * 2, HALF), bf16),
            jax.ShapeDtypeStruct((1, DOCS), jnp.int32),
        ],
        scratch_shapes=[
            pltpu.VMEM((1, DOCS), jnp.int32),
            pltpu.VMEM((PARTS, DOCS, SHARE), bf16),
            pltpu.SemaphoreType.DMA,
            pltpu.SemaphoreType.DMA((PARTS,)),
        ],
        compiler_params=PARAMS,
        name="dispatch",
    )(labels, pltpu.with_memory_space_constraint(embeddings, pltpu.HBM))
    own_rows = lax.all_to_all(
        outgoing.reshape(SOURCES, 2 * RANKS, HALF), ("x", "z"), 0, 0, tiled=True
    ).reshape(ROWS, HALF)
    other_rows = lax.ppermute(own_rows, "core", [(0, 1), (1, 0)])
    part, slots = pl.pallas_call(
        own_kernel,
        in_specs=[VMEM],
        out_specs=[VMEM, VMEM],
        out_shape=[
            jax.ShapeDtypeStruct((LANES, BLOCK, 128), f32),
            jax.ShapeDtypeStruct((SLOTS, SHARE), bf16),
        ],
        scratch_shapes=[pltpu.VMEM((SLOTS, 128), f32)],
        compiler_params=PARAMS,
        cost_estimate=pl.CostEstimate(
            flops=2 * SLOTS * SLOTS * SHARE * 2, bytes_accessed=2**22, transcendentals=0
        ),
        name="own",
    )(own_rows)
    products = pl.pallas_call(
        cross_kernel,
        in_specs=[VMEM, VMEM, VMEM],
        out_specs=VMEM,
        out_shape=jax.ShapeDtypeStruct((LANES, BLOCK, 128), f32),
        scratch_shapes=[pltpu.VMEM((SLOTS, SHARE), bf16), pltpu.VMEM((SLOTS, 128), f32)],
        compiler_params=PARAMS,
        name="cross",
    )(part, slots, other_rows)
    products = lax.all_to_all(products, "x", 0, 0, tiled=True)
    best = pl.pallas_call(
        best_kernel,
        in_specs=[VMEM],
        out_specs=VMEM,
        out_shape=jax.ShapeDtypeStruct((PLANES, REPS, 128), f32),
        compiler_params=PARAMS,
        name="best",
    )(products)
    returned = lax.all_to_all(
        best.reshape(REPS * PLANES, 1, 128), ("z", "rep"), 0, 0, tiled=True
    ).reshape(REPS * PLANES, 128)
    out = pl.pallas_call(
        collect_kernel,
        in_specs=[VMEM, VMEM],
        out_specs=VMEM,
        out_shape=jax.ShapeDtypeStruct((1, DOCS), f32),
        compiler_params=PARAMS,
        name="collect",
    )(slot, returned)
    return out.reshape(DOCS)


def solution(mesh):
    fine = Mesh(mesh.devices.reshape(PLANES, LANES, 2, REPS), ("z", "x", "core", "rep"))
    shard = ("z", "x", "core")
    return jax.shard_map(
        on_device,
        mesh=fine,
        in_specs=(P(shard, None), P(shard)),
        out_specs=P(shard),
        check_vma=False,
    )
```

```python
import jax
import jax.numpy as jnp
from jax import lax
from jax.experimental import pallas as pl
from jax.experimental.pallas import tpu as pltpu
from jax.sharding import Mesh
from jax.sharding import PartitionSpec as P

PLANES = 16
LANES = 4
PARTS = 2
PAIR = 2
REPS = 4
RANKS = 4
DOCS = 256
WIDTH = 4096
SHARE = WIDTH // PARTS
HALF = SHARE // 2
SOURCES = PLANES * LANES
SLOTS = SOURCES * RANKS
KEPT = SLOTS // 2
ROWS = SLOTS * 2
CHUNK = 256
LOCAL = SLOTS // LANES
BLOCK = 2 * KEPT + 8

RETURNS = REPS * PAIR * PLANES

epsilon = 1e-06
f32 = jnp.float32
bf16 = jnp.bfloat16


def iota(shape, dim):
    return lax.broadcasted_iota(jnp.int32, shape, dim)


def dispatch_kernel(
    cluster_ref, docs_ref, out_ref, slot_ref, labels, docs, label_sem, sems
):
    fetch_labels = pltpu.make_async_copy(cluster_ref, labels, label_sem)
    fetch_labels.start()

    fetches = []
    for part in range(PARTS):
        columns = slice(part * SHARE, (part + 1) * SHARE)
        fetch = pltpu.make_async_copy(docs_ref.at[:, columns], docs.at[part], sems.at[part])
        fetch.start(priority=1)
        fetches.append(fetch)
    fetch_labels.wait()
    cluster = labels[...]
    row = jnp.broadcast_to(cluster.astype(f32), (DOCS, DOCS))
    first, second = iota((DOCS, DOCS), 0), iota((DOCS, DOCS), 1)
    column = jnp.max(jnp.where(first == second, row, f32(-1.0)), axis=1, keepdims=True)
    earlier = (column == row) & (first < second)
    rank = jnp.sum(jnp.where(earlier, f32(1.0), f32(0.0)), axis=0, keepdims=True)
    slot = cluster * RANKS + rank.astype(jnp.int32)
    slot_ref[...] = slot
    local = slot - lax.axis_index("rep") * (PLANES * PAIR * RANKS)
    hit = (first >> 1) == local
    odd = (first & 1) == 1
    zero, one = f32(0.0), f32(1.0)
    even = jnp.where(hit & jnp.logical_not(odd), one, zero).astype(bf16)
    uneven = jnp.where(hit & odd, one, zero).astype(bf16)
    ones = jnp.ones((DOCS, 128), bf16)
    live = jnp.dot(even + uneven, ones, preferred_element_type=f32) > 0.5
    for part in range(PARTS):
        fetches[part].wait()
        merged = jnp.dot(even, docs[part, :, :HALF], preferred_element_type=f32)
        merged = merged + jnp.dot(uneven, docs[part, :, HALF:], preferred_element_type=f32)
        marked = jnp.where(live, merged[:, :128], jnp.nan)
        merged = jnp.concatenate([marked, merged[:, 128:]], axis=1)
        out_ref[:, part, :, :] = merged.astype(bf16).reshape(PLANES, 16, HALF)


def multiply(left, right):
    return lax.dot_general(left, right, (((1,), (1,)), ((), ())), preferred_element_type=f32)


def gather_slots(rows_ref, slots_ref, vacant_ref):
    row = iota((CHUNK, CHUNK), 0)
    half, lane, rank, plane = row >> 7, (row >> 5) & 3, (row >> 3) & 3, row & 7
    source = (plane * LANES + lane) * (2 * RANKS) + rank * 2 + half
    pick = jnp.where(iota((CHUNK, CHUNK), 1) == source, f32(1.0), f32(0.0)).astype(bf16)
    for chunk in range(ROWS // CHUNK):
        span = slice(chunk * CHUNK, (chunk + 1) * CHUNK)
        marked = rows_ref[span, :128].astype(f32)
        empty = marked != marked
        clean = jnp.where(empty, f32(0.0), marked).astype(bf16)
        flags = jnp.where(empty, f32(1.0), f32(0.0)).astype(bf16)
        rows = jnp.concatenate([clean, rows_ref[span, 128:], flags], axis=1)
        picked = jnp.dot(pick, rows, preferred_element_type=f32)
        slots = picked[:, :HALF].astype(bf16)
        for lane in range(LANES):
            top = lane * LOCAL + chunk * 32
            slots_ref[top : top + 32, :HALF] = slots[lane * 32 : (lane + 1) * 32]
            slots_ref[top : top + 32, HALF:] = slots[128 + lane * 32 : 128 + (lane + 1) * 32]
            vacant_ref[top : top + 32, :] = picked[lane * 32 : (lane + 1) * 32, HALF:]


def flagged_block(block, vacant):
    eye = iota((128, 128), 0) == iota((128, 128), 1)
    flagged = jnp.where(eye & (vacant > 0.5), jnp.nan, block)
    return flagged, jnp.sum(jnp.where(eye, flagged, f32(0.0)), axis=0, keepdims=True)


def split_rows(products_ref, squares, keep_ref, send_ref):
    mine = lax.axis_index("xl")
    for target, ref in ((mine, keep_ref), (1 - mine, send_ref)):
        start = pl.multiple_of(target * KEPT, KEPT)
        for t in range(2):
            tile = products_ref[pl.ds(start, KEPT), t * 128 : (t + 1) * 128]
            ref[t * KEPT : (t + 1) * KEPT, :] = tile
        ref[2 * KEPT :, :] = jnp.concatenate(squares + [jnp.zeros((6, 128), f32)], axis=0)


def own_kernel(rows_ref, keep_ref, send_ref, slots_ref, vacant_ref, products_ref):
    gather_slots(rows_ref, slots_ref, vacant_ref)
    slots = slots_ref[...]
    products_ref[...] = multiply(slots, slots)
    squares = []
    for b in range(2):
        span = slice(b * 128, (b + 1) * 128)
        block, diagonal = flagged_block(products_ref[span, span], vacant_ref[span, :])
        products_ref[span, span] = block
        squares.append(diagonal)
    split_rows(products_ref, squares, keep_ref, send_ref)


def cross_kernel(own_ref, rows_ref, keep_ref, send_ref, other_ref, vacant_ref, products_ref):
    gather_slots(rows_ref, other_ref, vacant_ref)
    other = other_ref[...]
    products_ref[...] = multiply(jnp.concatenate([own_ref[...], other], axis=0), other)
    squares = []
    for b in range(2):
        span = slice(b * 128, (b + 1) * 128)
        below = products_ref[SLOTS + b * 128 : SLOTS + (b + 1) * 128, span]
        squares.append(flagged_block(below, vacant_ref[span, :])[1])
    split_rows(products_ref, squares, keep_ref, send_ref)


def best_kernel(own_keep, own_sent, cross_keep, cross_sent, out_ref):
    row, column = iota((KEPT, 128), 0), iota((KEPT, 128), 1)
    mine = lax.axis_index("xl")

    def scale(squares):
        return jnp.where(squares == squares, lax.rsqrt(squares + epsilon), f32(-1.0))

    tiles, mates = [], []
    for keep, sent in ((own_keep, own_sent), (cross_keep, cross_sent)):
        total = keep[...] + sent[...]
        tiles += [total[t * KEPT : (t + 1) * KEPT] for t in range(2)]
        mates += [scale(total[2 * KEPT + t : 2 * KEPT + t + 1]) for t in range(2)]
    same = [(column == row) & (mine == t) for t in range(2)]
    squares = jnp.where(same[0], tiles[0], f32(0.0)) + jnp.where(same[1], tiles[1], f32(0.0))
    own = scale(jnp.sum(squares, axis=1, keepdims=True))
    best = jnp.full((KEPT, 128), -1.0, f32)
    for t in range(4):
        cosine = tiles[t] * own * mates[t]
        allowed = (own >= 0.0) & (mates[t] >= 0.0)
        if t < 2:
            allowed = allowed & jnp.logical_not(same[t])
        best = jnp.maximum(best, jnp.where(allowed, cosine, f32(-1.0)))
    best = jnp.max(best, axis=1, keepdims=True)
    spread = jnp.where((column & 3) == ((row >> 3) & 3), best, f32(0.0))
    lines = []
    for top in range(0, KEPT, 32):
        parts = [spread[top + k * 8 : top + (k + 1) * 8] for k in range(RANKS)]
        lines.append((parts[0] + parts[1]) + (parts[2] + parts[3]))
    turned = jnp.concatenate(lines, axis=0)
    for rep in range(REPS):
        for xh in range(2):
            out_ref[rep, :, xh, :] = turned[xh * PLANES : (xh + 1) * PLANES]


def collect_kernel(slot_ref, best_ref, out_ref):
    slot = slot_ref[...]
    best = best_ref[...]
    high = best.astype(bf16).astype(f32)
    middle = (best - high).astype(bf16).astype(f32)
    low = best - high - middle
    group = iota((RETURNS, 128), 1) >> 2
    pieces = jnp.where(group == 0, high, jnp.where(group == 1, middle, low))
    pieces = jnp.where(group < 3, pieces, f32(0.0)).astype(bf16)
    chosen = (iota((128, DOCS), 0) & 3) == (slot & 3)
    chosen = jnp.where(chosen, f32(1.0), f32(0.0)).astype(bf16)
    values = jnp.dot(pieces, chosen, preferred_element_type=f32)
    hit = iota((RETURNS, DOCS), 0) == (slot >> 2)
    out_ref[...] = jnp.sum(jnp.where(hit, values, f32(0.0)), axis=0, keepdims=True)


VMEM = pl.BlockSpec(memory_space=pltpu.VMEM)
HBM = pl.BlockSpec(memory_space=pltpu.HBM)
PARAMS = pltpu.CompilerParams(vmem_limit_bytes=32 * 1024 * 1024)


def on_device(embeddings, cluster_of):
    labels = pltpu.with_memory_space_constraint(cluster_of.reshape(1, DOCS), pltpu.HBM)
    outgoing, slot = pl.pallas_call(
        dispatch_kernel,
        in_specs=[HBM, HBM],
        out_specs=[VMEM, VMEM],
        out_shape=[
            jax.ShapeDtypeStruct((PLANES, PARTS, 16, HALF), bf16),
            jax.ShapeDtypeStruct((1, DOCS), jnp.int32),
        ],
        scratch_shapes=[
            pltpu.VMEM((1, DOCS), jnp.int32),
            pltpu.VMEM((PARTS, DOCS, SHARE), bf16),
            pltpu.SemaphoreType.DMA,
            pltpu.SemaphoreType.DMA((PARTS,)),
        ],
        compiler_params=PARAMS,
        name="dispatch",
    )(labels, pltpu.with_memory_space_constraint(embeddings, pltpu.HBM))
    own_rows = lax.all_to_all(
        outgoing.reshape(SOURCES, 2 * RANKS, HALF), ("z", "xl", "xh"), 0, 0, tiled=True
    ).reshape(ROWS, HALF)
    swap = [(0, 1), (1, 0)]
    other_rows = lax.ppermute(own_rows, "core", swap)
    half_rows = jax.ShapeDtypeStruct((BLOCK, 128), f32)
    own_keep, own_send, slots = pl.pallas_call(
        own_kernel,
        in_specs=[VMEM],
        out_specs=[VMEM, VMEM, VMEM],
        out_shape=[half_rows, half_rows, jax.ShapeDtypeStruct((SLOTS, SHARE), bf16)],
        scratch_shapes=[pltpu.VMEM((SLOTS, 128), f32), pltpu.VMEM((SLOTS, SLOTS), f32)],
        compiler_params=PARAMS,
        cost_estimate=pl.CostEstimate(
            flops=2 * SLOTS * SLOTS * SHARE * 2, bytes_accessed=2**22, transcendentals=0
        ),
        name="own",
    )(own_rows)
    own_sent = lax.ppermute(own_send, "xl", swap)
    cross_keep, cross_send = pl.pallas_call(
        cross_kernel,
        in_specs=[VMEM, VMEM],
        out_specs=[VMEM, VMEM],
        out_shape=[half_rows, half_rows],
        scratch_shapes=[
            pltpu.VMEM((SLOTS, SHARE), bf16),
            pltpu.VMEM((SLOTS, 128), f32),
            pltpu.VMEM((2 * SLOTS, SLOTS), f32),
        ],
        compiler_params=PARAMS,
        cost_estimate=pl.CostEstimate(
            flops=2 * SLOTS * SLOTS * SHARE * 2, bytes_accessed=2**22, transcendentals=0
        ),
        name="cross",
    )(slots, other_rows)
    cross_sent = lax.ppermute(cross_send, "xl", swap)
    best = pl.pallas_call(
        best_kernel,
        in_specs=[VMEM, VMEM, VMEM, VMEM],
        out_specs=VMEM,
        out_shape=jax.ShapeDtypeStruct((REPS, PLANES, 2, 128), f32),
        compiler_params=PARAMS,
        name="best",
    )(own_keep, own_sent, cross_keep, cross_sent)
    returned = lax.all_to_all(
        best.reshape(RETURNS, 1, 128), ("rep", "z", "xh"), 0, 0, tiled=True
    ).reshape(RETURNS, 128)
    out = pl.pallas_call(
        collect_kernel,
        in_specs=[VMEM, VMEM],
        out_specs=VMEM,
        out_shape=jax.ShapeDtypeStruct((1, DOCS), f32),
        compiler_params=PARAMS,
        name="collect",
    )(slot, returned)
    return out.reshape(DOCS)


def solution(mesh):
    axes = ("z", "xh", "xl", "core", "rep")
    fine = Mesh(mesh.devices.reshape(PLANES, 2, 2, 2, REPS), axes)
    shard = axes[:4]
    return jax.shard_map(
        on_device,
        mesh=fine,
        in_specs=(P(shard, None), P(shard)),
        out_specs=P(shard),
        check_vma=False,
    )
```

```python
import jax
import jax.numpy as jnp
from jax import lax
from jax.experimental import pallas as pl
from jax.experimental.pallas import tpu as pltpu
from jax.sharding import Mesh
from jax.sharding import PartitionSpec as P

PLANES = 16
LANES = 4
PARTS = 2
PAIR = 2
REPS = 4
RANKS = 4
DOCS = 256
WIDTH = 4096
SHARE = WIDTH // PARTS
HALF = SHARE // 2
SOURCES = PLANES * LANES
SLOTS = SOURCES * RANKS
ROWS = SLOTS * 2
CHUNK = 256
LOCAL = SLOTS // LANES
BLOCK = 4 * LOCAL + 8

epsilon = 1e-06
f32 = jnp.float32
bf16 = jnp.bfloat16


def iota(shape, dim):
    return lax.broadcasted_iota(jnp.int32, shape, dim)


def dispatch_kernel(
    cluster_ref, docs_ref, out_ref, slot_ref, labels, docs, label_sem, sems
):
    fetch_labels = pltpu.make_async_copy(cluster_ref, labels, label_sem)
    fetch_labels.start()

    fetches = []
    for part in range(PARTS):
        columns = slice(part * SHARE, (part + 1) * SHARE)
        fetch = pltpu.make_async_copy(docs_ref.at[:, columns], docs.at[part], sems.at[part])
        fetch.start(priority=1)
        fetches.append(fetch)
    fetch_labels.wait()
    cluster = labels[...]
    row = jnp.broadcast_to(cluster.astype(f32), (DOCS, DOCS))
    first, second = iota((DOCS, DOCS), 0), iota((DOCS, DOCS), 1)
    column = jnp.max(jnp.where(first == second, row, f32(-1.0)), axis=1, keepdims=True)
    earlier = (column == row) & (first < second)
    rank = jnp.sum(jnp.where(earlier, f32(1.0), f32(0.0)), axis=0, keepdims=True)
    slot = cluster * RANKS + rank.astype(jnp.int32)
    slot_ref[...] = slot
    local = slot - lax.axis_index("rep") * (PLANES * PAIR * RANKS)
    hit = (first >> 1) == local
    odd = (first & 1) == 1
    zero, one = f32(0.0), f32(1.0)
    even = jnp.where(hit & jnp.logical_not(odd), one, zero).astype(bf16)
    uneven = jnp.where(hit & odd, one, zero).astype(bf16)
    ones = jnp.ones((DOCS, 128), bf16)
    live = jnp.dot(even + uneven, ones, preferred_element_type=f32) > 0.5
    for part in range(PARTS):
        fetches[part].wait()
        merged = jnp.dot(even, docs[part, :, :HALF], preferred_element_type=f32)
        merged = merged + jnp.dot(uneven, docs[part, :, HALF:], preferred_element_type=f32)
        marked = jnp.where(live, merged[:, :128], jnp.nan)
        merged = jnp.concatenate([marked, merged[:, 128:]], axis=1)
        out_ref[:, part, :, :] = merged.astype(bf16).reshape(PLANES, 16, HALF)


def multiply(left, right):
    return lax.dot_general(left, right, (((1,), (1,)), ((), ())), preferred_element_type=f32)


def gather_slots(rows_ref, slots_ref, vacant_ref):
    row = iota((CHUNK, CHUNK), 0)
    half, lane, rank, plane = row >> 7, (row >> 5) & 3, (row >> 3) & 3, row & 7
    source = (plane * LANES + lane) * (2 * RANKS) + rank * 2 + half
    pick = jnp.where(iota((CHUNK, CHUNK), 1) == source, f32(1.0), f32(0.0)).astype(bf16)
    for chunk in range(ROWS // CHUNK):
        span = slice(chunk * CHUNK, (chunk + 1) * CHUNK)
        marked = rows_ref[span, :128].astype(f32)
        empty = marked != marked
        clean = jnp.where(empty, f32(0.0), marked).astype(bf16)
        flags = jnp.where(empty, f32(1.0), f32(0.0)).astype(bf16)
        rows = jnp.concatenate([clean, rows_ref[span, 128:], flags], axis=1)
        picked = jnp.dot(pick, rows, preferred_element_type=f32)
        slots = picked[:, :HALF].astype(bf16)
        for lane in range(LANES):
            top = lane * LOCAL + chunk * 32
            slots_ref[top : top + 32, :HALF] = slots[lane * 32 : (lane + 1) * 32]
            slots_ref[top : top + 32, HALF:] = slots[128 + lane * 32 : 128 + (lane + 1) * 32]
            vacant_ref[top : top + 32, :] = picked[lane * 32 : (lane + 1) * 32, HALF:]


def flagged_block(block, vacant):
    eye = iota((128, 128), 0) == iota((128, 128), 1)
    flagged = jnp.where(eye & (vacant > 0.5), jnp.nan, block)
    return flagged, jnp.sum(jnp.where(eye, flagged, f32(0.0)), axis=0, keepdims=True)


def own_kernel(rows_ref, out_ref, slots_ref, vacant_ref):
    gather_slots(rows_ref, slots_ref, vacant_ref)
    slots = slots_ref[...]
    products = multiply(slots, slots)
    for b in range(2):
        span = slice(b * 128, (b + 1) * 128)
        block, squares = flagged_block(products[span, span], vacant_ref[span, :])
        for lane in range(LANES):
            rows = slice(lane * LOCAL, (lane + 1) * LOCAL)
            inside = slice((lane % 2) * LOCAL, (lane % 2 + 1) * LOCAL)
            tile = block[inside] if lane // 2 == b else products[rows, span]
            out_ref[lane, b * LOCAL : (b + 1) * LOCAL, :] = tile
            out_ref[lane, 4 * LOCAL + b : 4 * LOCAL + b + 1, :] = squares
    for lane in range(LANES):
        out_ref[lane, 4 * LOCAL + 4 :, :] = jnp.zeros((4, 128), f32)


def cross_kernel(part_ref, own_ref, rows_ref, out_ref, other_ref, vacant_ref):
    gather_slots(rows_ref, other_ref, vacant_ref)
    other = other_ref[...]
    products = multiply(jnp.concatenate([own_ref[...], other], axis=0), other)
    for lane in range(LANES):
        rows = slice(lane * LOCAL, (lane + 1) * LOCAL)
        own_rows = slice(0, 2 * LOCAL)
        out_ref[lane, own_rows, :] = part_ref[lane, own_rows, :]
        out_ref[lane, 2 * LOCAL : 3 * LOCAL, :] = products[rows, :128]
        out_ref[lane, 3 * LOCAL : 4 * LOCAL, :] = products[rows, 128:]
        out_ref[lane, 4 * LOCAL :, :] = part_ref[lane, 4 * LOCAL :, :]
    for b in range(2):
        span = slice(b * 128, (b + 1) * 128)
        below = products[SLOTS + b * 128 : SLOTS + (b + 1) * 128, span]
        squares = flagged_block(below, vacant_ref[span, :])[1]
        for lane in range(LANES):
            out_ref[lane, 4 * LOCAL + 2 + b : 4 * LOCAL + 3 + b, :] = squares


def best_kernel(parts_ref, out_ref):
    row, column = iota((LOCAL, 128), 0), iota((LOCAL, 128), 1)
    lane = lax.axis_index("xl") * 2 + lax.axis_index("xh")
    spot = column & 7
    rank = (row >> 3) & 3
    spread = jnp.zeros((LOCAL, 128), f32)

    def scale(squares):
        return jnp.where(squares == squares, lax.rsqrt(squares + epsilon), f32(-1.0))

    for cluster in range(PAIR):
        total = parts_ref[cluster] + parts_ref[PAIR + cluster]
        tiles = [total[t * LOCAL : (t + 1) * LOCAL] for t in range(4)]
        mates = [scale(total[4 * LOCAL + t : 4 * LOCAL + t + 1]) for t in range(4)]
        same = [column + t * 128 == row + lane * LOCAL for t in range(2)]
        squares = jnp.where(same[0], tiles[0], f32(0.0)) + jnp.where(same[1], tiles[1], f32(0.0))
        own = scale(jnp.sum(squares, axis=1, keepdims=True))
        best = jnp.full((LOCAL, 128), -1.0, f32)
        for t in range(4):
            cosine = tiles[t] * own * mates[t]
            allowed = (own >= 0.0) & (mates[t] >= 0.0)
            if t < 2:
                allowed = allowed & jnp.logical_not(same[t])
            best = jnp.maximum(best, jnp.where(allowed, cosine, f32(-1.0)))
        best = jnp.max(best, axis=1, keepdims=True)
        spread = jnp.where(spot == cluster * RANKS + rank, best, spread)
    planes = []
    for top in range(0, LOCAL, 32):
        tiles = [spread[top + k * 8 : top + (k + 1) * 8] for k in range(RANKS)]
        planes.append((tiles[0] + tiles[1]) + (tiles[2] + tiles[3]))
    turned = jnp.concatenate(planes, axis=0)
    for rep in range(REPS):
        out_ref[:, rep, :] = turned


def collect_kernel(slot_ref, best_ref, out_ref):
    slot = slot_ref[...]
    best = best_ref[...]
    high = best.astype(bf16).astype(f32)
    middle = (best - high).astype(bf16).astype(f32)
    low = best - high - middle
    group = iota((REPS * PLANES, 128), 1) >> 3
    pieces = jnp.where(group == 0, high, jnp.where(group == 1, middle, low))
    pieces = jnp.where(group < 3, pieces, f32(0.0)).astype(bf16)
    chosen = (iota((128, DOCS), 0) & 7) == (slot & 7)
    chosen = jnp.where(chosen, f32(1.0), f32(0.0)).astype(bf16)
    values = jnp.dot(pieces, chosen, preferred_element_type=f32)
    home = slot >> 3
    home = (home & (PLANES - 1)) * REPS + home // PLANES
    line = iota((REPS * PLANES, DOCS), 0) == home
    out_ref[...] = jnp.sum(jnp.where(line, values, f32(0.0)), axis=0, keepdims=True)


VMEM = pl.BlockSpec(memory_space=pltpu.VMEM)
HBM = pl.BlockSpec(memory_space=pltpu.HBM)
PARAMS = pltpu.CompilerParams(vmem_limit_bytes=32 * 1024 * 1024)


def on_device(embeddings, cluster_of):
    labels = pltpu.with_memory_space_constraint(cluster_of.reshape(1, DOCS), pltpu.HBM)
    outgoing, slot = pl.pallas_call(
        dispatch_kernel,
        in_specs=[HBM, HBM],
        out_specs=[VMEM, VMEM],
        out_shape=[
            jax.ShapeDtypeStruct((PLANES, PARTS, 16, HALF), bf16),
            jax.ShapeDtypeStruct((1, DOCS), jnp.int32),
        ],
        scratch_shapes=[
            pltpu.VMEM((1, DOCS), jnp.int32),
            pltpu.VMEM((PARTS, DOCS, SHARE), bf16),
            pltpu.SemaphoreType.DMA,
            pltpu.SemaphoreType.DMA((PARTS,)),
        ],
        compiler_params=PARAMS,
        name="dispatch",
    )(labels, pltpu.with_memory_space_constraint(embeddings, pltpu.HBM))
    own_rows = lax.all_to_all(
        outgoing.reshape(SOURCES, 2 * RANKS, HALF), ("z", "xl", "xh"), 0, 0, tiled=True
    ).reshape(ROWS, HALF)
    other_rows = lax.ppermute(own_rows, "core", [(0, 1), (1, 0)])
    part, slots = pl.pallas_call(
        own_kernel,
        in_specs=[VMEM],
        out_specs=[VMEM, VMEM],
        out_shape=[
            jax.ShapeDtypeStruct((LANES, BLOCK, 128), f32),
            jax.ShapeDtypeStruct((SLOTS, SHARE), bf16),
        ],
        scratch_shapes=[pltpu.VMEM((SLOTS, 128), f32)],
        compiler_params=PARAMS,
        cost_estimate=pl.CostEstimate(
            flops=2 * SLOTS * SLOTS * SHARE * 2, bytes_accessed=2**22, transcendentals=0
        ),
        name="own",
    )(own_rows)
    products = pl.pallas_call(
        cross_kernel,
        in_specs=[VMEM, VMEM, VMEM],
        out_specs=VMEM,
        out_shape=jax.ShapeDtypeStruct((LANES, BLOCK, 128), f32),
        scratch_shapes=[pltpu.VMEM((SLOTS, SHARE), bf16), pltpu.VMEM((SLOTS, 128), f32)],
        compiler_params=PARAMS,
        name="cross",
    )(part, slots, other_rows)
    products = lax.all_to_all(products, ("xl", "xh"), 0, 0, tiled=True)
    best = pl.pallas_call(
        best_kernel,
        in_specs=[VMEM],
        out_specs=VMEM,
        out_shape=jax.ShapeDtypeStruct((PLANES, REPS, 128), f32),
        compiler_params=PARAMS,
        name="best",
    )(products)
    returned = lax.all_to_all(
        best.reshape(REPS * PLANES, 1, 128), ("z", "rep"), 0, 0, tiled=True
    ).reshape(REPS * PLANES, 128)
    out = pl.pallas_call(
        collect_kernel,
        in_specs=[VMEM, VMEM],
        out_specs=VMEM,
        out_shape=jax.ShapeDtypeStruct((1, DOCS), f32),
        compiler_params=PARAMS,
        name="collect",
    )(slot, returned)
    return out.reshape(DOCS)


def solution(mesh):
    axes = ("z", "xh", "xl", "core", "rep")
    fine = Mesh(mesh.devices.reshape(PLANES, 2, 2, 2, REPS), axes)
    shard = axes[:4]
    return jax.shard_map(
        on_device,
        mesh=fine,
        in_specs=(P(shard, None), P(shard)),
        out_specs=P(shard),
        check_vma=False,
    )
```
